32 devices in a mesh: rep: 2 (over x), shard: 16 (over z, y, core).
Axes of the slice: x: 2, y: 2, z: 4, core: 2. Of those that a mesh axis runs over, the one named last changes fastest.
Arguments:
- images: bfloat16 [64, 1024, 512], P(('rep', 'shard')), may hold values from -6 to 6
- embeds: bfloat16 [64, 1024], P(('rep', 'shard')), may hold values from -6 to 6
- cotangent: bfloat16 [64, 1024, 512], P(('rep', 'shard')), may hold values from -6 to 6
- counts: int32 [32, 2], P(('rep', 'shard')), may hold values from 0 to 2, as said below
- bucket_weight: float32 [2], replicated, may hold values from 0.5 to 2
- owner: int32 [32], replicated, may hold values from 0 to 31, as said below
- master: float32 [32, 512, 512], P('shard')
- first_moment: float32 [32, 512, 512], P('shard')
- second_moment: float32 [32, 512, 512], P('shard')
- left_basis: float32 [32, 512, 512], P('shard'), as said below
- right_basis: float32 [32, 512, 512], P('shard'), as said below
- vec_master: float32 [13, 512], P(None, 'shard')
- vec_first: float32 [13, 512], P(None, 'shard')
- vec_second: float32 [13, 512], P(None, 'shard')
Outputs:
- block_out: bfloat16 [64, 1024, 512], P(('rep', 'shard'))
- grad_images: float32 [64, 1024, 512], P(('rep', 'shard'))
- grad_embeds: float32 [64, 1024], P(('rep', 'shard'))
- new_first: float32 [32, 512, 512], P('shard')
- new_second: float32 [32, 512, 512], P('shard')
- new_master: float32 [32, 512, 512], P('shard')
- master_low: bfloat16 [32, 512, 512], P('shard')
- vec_first_new: float32 [13, 512], P(None, 'shard')
- vec_second_new: float32 [13, 512], P(None, 'shard')
- vec_master_new: float32 [13, 512], P(None, 'shard')
- vec_low: bfloat16 [13, 512], P(None, 'shard')
The draws below stay inside these ranges and needn't reach their ends.
Inputs may be any that keep to these rules, and one draw needn't show every extreme that they name: `counts`: row d gives device d's images of bucket 0 and of bucket 1; they fill its first slots in that order, the rest of its 2 slots are unused; every row sums to 1 or more and some row sums to 2. A permutation of the 32 slots; block b, for b < 26, lives in slot owner[b]; the other slots hold no block. `left_basis`: each slot's matrix is orthogonal. `right_basis`: each slot's matrix is orthogonal.
All inputs are finite; a program needn't handle non-finite values.
Results may differ from the reference program's by a relative error of at most 0.025.
Values may be sent and summed in bfloat16 or wider, within the bound.
No kernel may reach another device: no remote copies, remote signals or barrier semaphores. Data moves between devices by JAX's collectives and lax.ppermute only.
A program may use at most 320 MiB of HBM per device.

```python
import math
import jax
import jax.numpy as jnp
from jax import lax

C = 512
EMB = 1024
HEADS = 8
HEAD = 64
GROUPS = 32
SIDE = 32
HW = 1024
IMG_DEV = 2
IMAGES = 64
BLOCKS = 26
MATS = 32
VECS = 13
STEP = 2
N_REP = 2
N_SHARD = 16


VECTOR_SCALES = [1.0, 1.0, 2.0, 1.0, 1.0, 1.3, 1.3, 2.5, 2.3, 2.3, 1.0, 1.0, 1.0]


def slot_blocks(base_key):
    placed = jax.random.permutation(jax.random.fold_in(base_key, 11), MATS).astype(jnp.int32)
    return jnp.zeros((MATS,), jnp.int32).at[placed].set(jnp.arange(MATS, dtype=jnp.int32))


def block_spread_drawn(block_index):
    return jnp.where(block_index < 18, (9.0 * C) ** (-0.5), jnp.where(block_index < 22, EMB ** (-0.5), jnp.where(block_index < 24, 1.25 * C ** (-0.5), jnp.where(block_index < 25, C ** (-0.5), jnp.where(block_index < 26, 0.295 * (HW / C) ** 0.5, C ** (-0.5))))))


def gradient_size(block_index):
    factor = jnp.where(block_index < 9, 1.2, jnp.where(block_index < 18, 1.5, jnp.where(block_index < 22, 0.6, jnp.where(block_index < 25, 1.0, jnp.where(block_index < 26, 0.1, 1.0)))))
    return factor * math.sqrt(IMAGES * HW)


def draw_owner(key, part):
    return jax.random.permutation(jax.random.fold_in(key, 11), MATS).astype(jnp.int32)


def draw_counts(key, part):
    devices_all = N_REP * N_SHARD
    heavy_load = jax.random.randint(jax.random.fold_in(key, 31), (devices_all,), 0, 4) == 0
    heavy_load = heavy_load.at[0].set(True)
    image_total = jnp.where(heavy_load, IMG_DEV, max(IMG_DEV // 2, 1)).astype(jnp.int32)
    bucket_zero = jax.random.randint(jax.random.fold_in(key, 32), (devices_all,), 0, image_total + 1).astype(jnp.int32)
    return jnp.stack([bucket_zero, image_total - bucket_zero], axis=1)


def draw_master(key, part):
    noise = jax.random.normal(jax.random.fold_in(key, 21), (MATS, C, C), jnp.float32)
    return noise * block_spread_drawn(slot_blocks(key))[:, None, None]


def draw_first_moment(key, part):
    noise = jax.random.normal(jax.random.fold_in(key, 22), (MATS, C, C), jnp.float32)
    return noise * gradient_size(slot_blocks(key))[:, None, None]


def draw_second_moment(key, part):
    factor = jnp.exp(jax.random.uniform(jax.random.fold_in(key, 23), (MATS, C, C), jnp.float32, 0.0, math.log(4.0)))
    sizes_now = gradient_size(slot_blocks(key))
    return factor * (sizes_now * sizes_now)[:, None, None]


def slot_orders(layer_key):
    keys_all = jax.random.split(layer_key, MATS)
    return jax.vmap(lambda part_key: jax.random.permutation(part_key, C))(keys_all).astype(jnp.int32)


def turn_columns(basis_now, layer_key):
    orders = slot_orders(layer_key)
    picked = jnp.take_along_axis(basis_now, jnp.broadcast_to(orders[:, None, :], basis_now.shape), axis=2)
    angles = jax.random.uniform(jax.random.fold_in(layer_key, 1), (MATS, 1, C // 2), jnp.float32, 0.0, 2.0 * math.pi)
    paired = picked.reshape(MATS, C, C // 2, 2)
    first_half = paired[..., 0]
    second_half = paired[..., 1]
    cosine = jnp.cos(angles)
    sine = jnp.sin(angles)
    turned = jnp.stack([cosine * first_half - sine * second_half, sine * first_half + cosine * second_half], axis=3)
    return turned.reshape(MATS, C, C)


def turn_rows(basis_now, layer_key):
    orders = slot_orders(layer_key)
    picked = jnp.take_along_axis(basis_now, jnp.broadcast_to(orders[:, :, None], basis_now.shape), axis=1)
    angles = jax.random.uniform(jax.random.fold_in(layer_key, 1), (MATS, C // 2, 1), jnp.float32, 0.0, 2.0 * math.pi)
    paired = picked.reshape(MATS, C // 2, 2, C)
    first_half = paired[:, :, 0, :]
    second_half = paired[:, :, 1, :]
    cosine = jnp.cos(angles)
    sine = jnp.sin(angles)
    turned = jnp.stack([cosine * first_half - sine * second_half, sine * first_half + cosine * second_half], axis=2)
    return turned.reshape(MATS, C, C)


def rotation(base_key):
    keys_all = jax.random.split(base_key, MATS)
    orders = jax.vmap(lambda part_key: jax.random.permutation(part_key, C))(keys_all).astype(jnp.float32)
    sign_flips = (2 * jax.random.randint(jax.random.fold_in(base_key, 5), (MATS, C), 0, 2) - 1).astype(jnp.float32)
    columns = jnp.arange(C, dtype=jnp.float32)
    cosines = jnp.cos(math.pi * (2.0 * orders[:, :, None] + 1.0) * columns[None, None, :] / (2.0 * C))
    column_norm = jnp.where(columns == 0, math.sqrt(1.0 / C), math.sqrt(2.0 / C))
    basis_now = cosines * column_norm[None, None, :] * sign_flips[:, None, :]
    for layer_index in range(10):
        basis_now = turn_columns(basis_now, jax.random.fold_in(base_key, 100 + layer_index))
        basis_now = turn_rows(basis_now, jax.random.fold_in(base_key, 200 + layer_index))
    return basis_now


def draw_left_basis(key, part):
    return rotation(jax.random.fold_in(key, 24))


def draw_right_basis(key, part):
    return rotation(jax.random.fold_in(key, 25))


def draw_vec_master(key, part):
    noise = jax.random.normal(jax.random.fold_in(key, 26), (VECS, C), jnp.float32)
    row_ids = jnp.arange(VECS)[:, None]
    gain_rows = (row_ids == 0) | (row_ids == 5) | (row_ids == 8)
    return jnp.where(gain_rows, 1.0 + 0.15 * noise, 0.2 * noise)


def draw_vec_first(key, part):
    noise = jax.random.normal(jax.random.fold_in(key, 27), (VECS, C), jnp.float32)
    return noise * (jnp.array(VECTOR_SCALES, jnp.float32) * math.sqrt(IMAGES * HW))[:, None]


def draw_vec_second(key, part):
    factor = jnp.exp(jax.random.uniform(jax.random.fold_in(key, 28), (VECS, C), jnp.float32, 0.0, math.log(4.0)))
    sizes_now = jnp.array(VECTOR_SCALES, jnp.float32) * math.sqrt(IMAGES * HW)
    return factor * (sizes_now * sizes_now)[:, None]


def levels(rng, shape, cuts, smallest, top_value):
    factor_of = 1.0
    for position, shards_of in cuts:
        draws = jax.random.uniform(jax.random.fold_in(jax.random.fold_in(rng, 6), position), (shards_of,), jnp.float32, smallest / len(cuts), top_value / len(cuts))
        factor_of = factor_of * jnp.repeat(jnp.exp(draws), shape[position] // shards_of).reshape((-1,) + (1,) * (len(shape) - 1 - position))
    return factor_of


def gaussian(own_key, extent, deviation, reach, cuts=(), kind=jnp.bfloat16):
    values = deviation * jax.random.normal(own_key, extent, jnp.float32)
    if cuts:
        values = values * levels(own_key, extent, cuts, -0.22, 0.18)
    return jnp.clip(values, -reach, reach).astype(kind)


def setup_inputs(seed: int = 0) -> dict:
    keys = jax.random.split(jax.random.key(seed), 15)
    return {
        "images": gaussian(keys[0], (IMAGES, HW, C), 1.0, 6.0, ((0, 32),)),
        "embeds": gaussian(keys[1], (IMAGES, EMB), 1.0, 6.0, ((0, 32),)),
        "cotangent": gaussian(keys[2], (IMAGES, HW, C), 1.0, 6.0, ((0, 32),)),
        "counts": draw_counts(jax.random.fold_in(keys[14], 71), 0),
        "bucket_weight": jnp.clip(jnp.exp(jax.random.uniform(keys[4], (2,), jnp.float32, math.log(0.5), math.log(2.0))), 0.5, 2.0),
        "owner": draw_owner(jax.random.fold_in(keys[14], 71), 0),
        "master": draw_master(jax.random.fold_in(keys[14], 71), 0),
        "first_moment": draw_first_moment(jax.random.fold_in(keys[14], 71), 0),
        "second_moment": draw_second_moment(jax.random.fold_in(keys[14], 71), 0),
        "left_basis": draw_left_basis(jax.random.fold_in(keys[14], 71), 0),
        "right_basis": draw_right_basis(jax.random.fold_in(keys[14], 71), 0),
        "vec_master": draw_vec_master(jax.random.fold_in(keys[14], 71), 0),
        "vec_first": draw_vec_first(jax.random.fold_in(keys[14], 71), 0),
        "vec_second": draw_vec_second(jax.random.fold_in(keys[14], 71), 0),
    }


@jax.custom_vjp
def low(v):
    return lax.optimization_barrier(v.astype(jnp.bfloat16)).astype(jnp.float32)

@jax.custom_vjp
def low_back(v):
    return v

def low_keep(v):
    return (low(v), None)

def low_pass(kept, grad):
    return (grad,)

def back_keep(v):
    return (v, None)

def back_low(kept, grad):
    return (low(grad),)
low.defvjp(low_keep, low_pass)
low_back.defvjp(back_keep, back_low)
EPS_NORM = 1e-05
ADAM_EPS = 1e-08
MOMENT_DECAY = 0.5
WEIGHT_DECAY = 0.01
VECTOR_RATE = 0.2
PRECISE = lax.Precision.HIGHEST

def block_spread(block_index):
    return jnp.where(block_index < 18, (9.0 * C) ** (-0.5), jnp.where(block_index < 22, EMB ** (-0.5), jnp.where(block_index < 24, 1.25 * C ** (-0.5), jnp.where(block_index < 25, C ** (-0.5), jnp.where(block_index < 26, 0.295 * (HW / C) ** 0.5, C ** (-0.5))))))

def group_norm(values_in):
    row_count = values_in.shape[0]
    grouped = values_in.reshape(row_count, GROUPS, C // GROUPS)
    group_mean = lax.optimization_barrier(jnp.mean(grouped, axis=(0, 2), keepdims=True))
    centered = grouped - group_mean
    group_var = lax.optimization_barrier(jnp.mean(centered * centered, axis=(0, 2), keepdims=True))
    return (centered * lax.rsqrt(group_var + EPS_NORM)).reshape(row_count, C)

def unfold(activation):
    padded_grid = jnp.pad(activation.reshape(SIDE, SIDE, C), ((1, 1), (1, 1), (0, 0)))
    pieces = []
    for tap_index in range(9):
        row_off = tap_index // 3
        col_off = tap_index % 3
        pieces.append(padded_grid[row_off:row_off + SIDE, col_off:col_off + SIDE].reshape(HW, C))
    return jnp.concatenate(pieces, axis=1)

def convolve(activation, tap_blocks):
    return jnp.dot(unfold(activation), tap_blocks.reshape(9 * C, C), precision=PRECISE)

def attention(queries, keys_in, values):
    query_heads = queries.reshape(HW, HEADS, HEAD)
    key_heads = keys_in.reshape(HW, HEADS, HEAD)
    value_heads = values.reshape(HW, HEADS, HEAD)
    scores = jnp.einsum('qhd,khd->hqk', query_heads, key_heads, precision=PRECISE) * (1.0 / math.sqrt(HEAD))
    scores = low_back(scores)
    row_max = lax.optimization_barrier(jnp.max(scores, axis=-1, keepdims=True))
    exponent = jnp.exp(scores - row_max)
    probabilities = low(exponent / lax.optimization_barrier(jnp.sum(exponent, axis=-1, keepdims=True)))
    return jnp.einsum('hqk,khd->qhd', probabilities, value_heads, precision=PRECISE).reshape(HW, C)

def forward(blocks, vectors, image_rows, embed_row):
    act_one = low(jax.nn.silu(group_norm(image_rows) * vectors[0] + vectors[1]))
    hidden_one = low_back(convolve(act_one, blocks[0:9]) + vectors[2])
    emb_act = low(jax.nn.silu(embed_row))
    ada_scale = jnp.dot(emb_act[:C], blocks[18], precision=PRECISE) + jnp.dot(emb_act[C:], blocks[19], precision=PRECISE) + vectors[3]
    ada_shift = jnp.dot(emb_act[:C], blocks[20], precision=PRECISE) + jnp.dot(emb_act[C:], blocks[21], precision=PRECISE) + vectors[4]
    normed_two = group_norm(hidden_one) * vectors[5] + vectors[6]
    act_two = low(jax.nn.silu(normed_two * (1.0 + ada_scale) + ada_shift))
    hidden_two = low_back(convolve(act_two, blocks[9:18]) + vectors[7])
    resid = image_rows + hidden_two
    normed_three = low(group_norm(resid) * vectors[8] + vectors[9])
    queries = low(low_back(jnp.dot(normed_three, blocks[22], precision=PRECISE) + vectors[10]))
    keys_in = low(low_back(jnp.dot(normed_three, blocks[23], precision=PRECISE)))
    values = low(low_back(jnp.dot(normed_three, blocks[24], precision=PRECISE) + vectors[11]))
    attended = low(low_back(attention(queries, keys_in, values)))
    branch = low_back(jnp.dot(attended, blocks[25], precision=PRECISE) + vectors[12])
    return resid + branch

def reference(images, embeds, cotangent, counts, bucket_weight, owner, master, first_moment, second_moment, left_basis, right_basis, vec_master, vec_first, vec_second):
    blocks = master.astype(jnp.bfloat16).astype(jnp.float32)[owner[:BLOCKS]]
    vectors = vec_master.astype(jnp.bfloat16).astype(jnp.float32)
    image_index = jnp.arange(IMAGES, dtype=jnp.int32)
    device_row = image_index // IMG_DEV
    slot_place = image_index % IMG_DEV
    bucket_zero = counts[device_row, 0]
    image_total = bucket_zero + counts[device_row, 1]
    alive_flag = slot_place < image_total
    weights = jnp.where(slot_place < bucket_zero, bucket_weight[0], bucket_weight[1]) * alive_flag.astype(jnp.float32)

    def one_image(loop_state, inputs):
        grad_blocks, grad_vectors = loop_state
        image_rows, embed_row, cot_rows, weight, live_flag = inputs

        def compute(ignored):
            result_rows, pullback = jax.vjp(forward, blocks, vectors, image_rows.astype(jnp.float32), embed_row.astype(jnp.float32))
            grads = pullback(cot_rows.astype(jnp.float32) * weight)
            return (result_rows.astype(jnp.bfloat16),) + tuple(grads)

        def skip(ignored):
            return (jnp.zeros((HW, C), jnp.bfloat16), jnp.zeros((BLOCKS, C, C), jnp.float32), jnp.zeros((VECS, C), jnp.float32), jnp.zeros((HW, C), jnp.float32), jnp.zeros((EMB,), jnp.float32))
        result_rows, block_grad, vector_grad, image_grad, embed_grad = lax.cond(live_flag, compute, skip, 0)
        return ((grad_blocks + block_grad, grad_vectors + vector_grad), (result_rows, image_grad, embed_grad))
    start_state = (jnp.zeros((BLOCKS, C, C), jnp.float32), jnp.zeros((VECS, C), jnp.float32))
    (grad_blocks, grad_vectors), (block_out, grad_images, grad_embeds) = lax.scan(one_image, start_state, (images, embeds, cotangent, weights, alive_flag))
    grad_slot = jnp.zeros((MATS, C, C), jnp.float32).at[owner[:BLOCKS]].set(grad_blocks)
    rotated = jnp.matmul(jnp.matmul(jnp.swapaxes(left_basis, 1, 2), grad_slot, precision=PRECISE), right_basis, precision=PRECISE)
    new_first = MOMENT_DECAY * first_moment + (1.0 - MOMENT_DECAY) * rotated
    new_second = MOMENT_DECAY * second_moment + (1.0 - MOMENT_DECAY) * rotated * rotated
    correction = 1.0 - MOMENT_DECAY ** STEP
    direction = new_first / correction / (jnp.sqrt(new_second / correction) + ADAM_EPS)
    update = jnp.matmul(jnp.matmul(left_basis, direction, precision=PRECISE), jnp.swapaxes(right_basis, 1, 2), precision=PRECISE)
    slot_block = jnp.zeros((MATS,), jnp.int32).at[owner].set(jnp.arange(MATS, dtype=jnp.int32))
    step_rate = jnp.where(slot_block < BLOCKS, 2.0 * block_spread(slot_block), 0.0)
    new_master = master - step_rate[:, None, None] * (update + WEIGHT_DECAY * master)
    vec_first_new = MOMENT_DECAY * vec_first + (1.0 - MOMENT_DECAY) * grad_vectors
    vec_second_new = MOMENT_DECAY * vec_second + (1.0 - MOMENT_DECAY) * grad_vectors * grad_vectors
    vec_master_new = vec_master - VECTOR_RATE * (vec_first_new / correction) / (jnp.sqrt(vec_second_new / correction) + ADAM_EPS)
    return (block_out, grad_images, grad_embeds, new_first, new_second, new_master, new_master.astype(jnp.bfloat16), vec_first_new, vec_second_new, vec_master_new, vec_master_new.astype(jnp.bfloat16))
```

```python
import functools
import math

import jax
import jax.numpy as jnp
from jax import lax
from jax.experimental import pallas as pl
from jax.experimental.pallas import tpu as pltpu
from jax.sharding import PartitionSpec as P

C = 512
EMB = 1024
HEADS = 8
HEAD = 64
GROUPS = 32
SIDE = 32
HW = 1024
BLOCKS = 26
VECS = 13
STEP = 2
PAD = SIDE
SLAB = HW + 2 * PAD
ROWS = 128
QROWS = 256

EPS_NORM = 1e-05
ADAM_EPS = 1e-08
MOMENT_DECAY = 0.5
WEIGHT_DECAY = 0.01
VECTOR_RATE = 0.2
PRECISE = lax.Precision.HIGHEST
F32 = jnp.float32
BF16 = jnp.bfloat16
ANY = pl.BlockSpec(memory_space=pl.ANY)
SMEM = pl.BlockSpec(memory_space=pltpu.SMEM)
VMEM = pl.BlockSpec(memory_space=pltpu.VMEM)
VMEM_LIMIT = 56 * 2**20


def block_spread(block_index):
    return jnp.where(
        block_index < 18,
        (9.0 * C) ** (-0.5),
        jnp.where(
            block_index < 22,
            EMB ** (-0.5),
            jnp.where(
                block_index < 24,
                1.25 * C ** (-0.5),
                jnp.where(
                    block_index < 25,
                    C ** (-0.5),
                    jnp.where(block_index < 26, 0.295 * (HW / C) ** 0.5, C ** (-0.5)),
                ),
            ),
        ),
    )


def mm(a, b):
    return jnp.dot(a, b, preferred_element_type=F32)


def mm_t(a, b):
    return lax.dot_general(a, b, (((1,), (1,)), ((), ())), preferred_element_type=F32)


def sigmoid(u):
    return 1.0 / (1.0 + jnp.exp(-u))


def silu_slope(u):
    s = sigmoid(u)
    return s * (1.0 + u * (1.0 - s))


def chunks(count, body, init=0):
    return lax.fori_loop(0, count, body, init)


def rows_of(index, size):
    return pl.ds(pl.multiple_of(index * size, size), size)


def group_mean(column_sum):
    total = jnp.broadcast_to(column_sum, (8, C))
    lane = lax.broadcasted_iota(jnp.int32, (8, C), 1)
    for step in (1, 2, 4, 8):
        other = jnp.where(
            (lane & step) != 0, pltpu.roll(total, step, 1), pltpu.roll(total, C - step, 1)
        )
        total = total + other
    return total[0:1] * (1.0 / (HW * (C // GROUPS)))


def norm_stats(read):
    zero = jnp.zeros((1, C), F32)
    total = chunks(
        HW // ROWS,
        lambda c, t: t + jnp.sum(read(rows_of(c, ROWS)), axis=0, keepdims=True),
        zero,
    )
    mean = group_mean(total)

    def squares(c, t):
        centered = read(rows_of(c, ROWS)) - mean
        return t + jnp.sum(centered * centered, axis=0, keepdims=True)

    var = group_mean(chunks(HW // ROWS, squares, zero))
    return mean, lax.rsqrt(var + EPS_NORM)


def clear_pads(slab):
    zeros = jnp.zeros((PAD, C), BF16)
    for lead in slab_leads(slab):
        slab[lead + (pl.ds(0, PAD), slice(None))] = zeros
        slab[lead + (pl.ds(PAD + HW, PAD), slice(None))] = zeros


def slab_leads(slab):
    if len(slab.shape) == 3:
        return [(j,) for j in range(3)]
    return [(i, j) for i in range(slab.shape[0]) for j in range(3)]


def store_slab(slab, lead, c, chunk):
    column = lax.broadcasted_iota(jnp.int32, (ROWS, C), 0) & (SIDE - 1)
    before = jnp.where(column == 0, 0.0, pltpu.roll(chunk, 1, 0))
    after = jnp.where(column == SIDE - 1, 0.0, pltpu.roll(chunk, ROWS - 1, 0))
    rows = pl.ds(pl.multiple_of(c * ROWS + PAD, PAD), ROWS)
    slab[lead + (0, rows, slice(None))] = before.astype(BF16)
    slab[lead + (1, rows, slice(None))] = chunk.astype(BF16)
    slab[lead + (2, rows, slice(None))] = after.astype(BF16)


def conv_rows(slab, lead, weights, base, size, back):
    total = None
    for tap in range(9):
        di, dj = tap // 3, tap % 3
        if back:
            di, dj = 2 - di, 2 - dj
        rows = pl.ds(pl.multiple_of(base + di * SIDE, SIDE), size)
        piece = slab[lead + (dj, rows, slice(None))]
        term = (mm_t if back else mm)(piece, weights[tap])
        total = term if total is None else total + term
    return total


CONV_ROWS = 512


def block_copies(owner, slots, dest, sem, first, count, offset=0):
    return [
        pltpu.make_async_copy(slots.at[owner[first + n]], dest.at[offset + n], sem.at[offset + n])
        for n in range(count)
    ]


def fwd_one(owner, slots, x, vec, h1, a1, weights, slab, sem):
    step = pl.program_id(0)

    @pl.when(step == 0)
    def _():
        for copy in block_copies(owner, slots, weights, sem, 0, 9):
            copy.start()
        clear_pads(slab)

    def read(rows):
        return x[0, rows, :].astype(F32)

    mean, inv = norm_stats(read)
    gain = inv * vec[0:1]
    bias = vec[1:2]

    def activate(c, _):
        rows = rows_of(c, ROWS)
        pre = (read(rows) - mean) * gain + bias
        act = pre * sigmoid(pre)
        a1[0, rows, :] = act.astype(BF16)
        store_slab(slab, (), c, act)
        return 0

    chunks(HW // ROWS, activate)

    @pl.when(step == 0)
    def _():
        for copy in block_copies(owner, slots, weights, sem, 0, 9):
            copy.wait()

    def conv(c, _):
        h1[0, rows_of(c, CONV_ROWS), :] = (
            conv_rows(slab, (), weights, c * CONV_ROWS, CONV_ROWS, False) + vec[2:3]
        )
        return 0

    chunks(HW // CONV_ROWS, conv)


def fwd_two(owner, slots, h1, x, act, vec, a2, r1, nhat, stats, weights, maps, slab, sem):
    step = pl.program_id(0)

    def copies():
        return block_copies(owner, slots, maps, sem, 18, 4) + block_copies_at(
            owner, slots, weights, sem, 9, 9, 4
        )

    @pl.when(step == 0)
    def _():
        for copy in copies():
            copy.start()
        clear_pads(slab)

    mean, inv = norm_stats(lambda rows: h1[0, rows, :])

    @pl.when(step == 0)
    def _():
        for copy in block_copies(owner, slots, maps, sem, 18, 4):
            copy.wait()

    row = act[0]
    scale = (mm(row[:, :C], maps[0]) + mm(row[:, C:], maps[1]))[0:1] + vec[3:4]
    shift = (mm(row[:, :C], maps[2]) + mm(row[:, C:], maps[3]))[0:1] + vec[4:5]
    stats[0] = jnp.concatenate([scale, shift, inv, jnp.zeros((5, C), F32)], axis=0)
    gain = vec[5:6]
    bias = vec[6:7]

    def activate(c, _):
        rows = rows_of(c, ROWS)
        normed = (h1[0, rows, :] - mean) * inv
        nhat[0, rows, :] = normed
        pre = (normed * gain + bias) * (1.0 + scale) + shift
        act_two = pre * sigmoid(pre)
        a2[0, rows, :] = act_two.astype(BF16)
        store_slab(slab, (), c, act_two)
        return 0

    chunks(HW // ROWS, activate)

    @pl.when(step == 0)
    def _():
        for copy in block_copies_at(owner, slots, weights, sem, 9, 9, 4):
            copy.wait()

    def conv(c, _):
        rows = rows_of(c, CONV_ROWS)
        hidden = conv_rows(slab, (), weights, c * CONV_ROWS, CONV_ROWS, False) + vec[7:8]
        r1[0, rows, :] = x[0, rows, :].astype(F32) + hidden
        return 0

    chunks(HW // CONV_ROWS, conv)


def block_copies_at(owner, slots, dest, sem, first, count, sem_from):
    return [
        pltpu.make_async_copy(slots.at[owner[first + n]], dest.at[n], sem.at[sem_from + n])
        for n in range(count)
    ]


MM_ROWS = 512


def attention(
    owner, slots, weight, live, r1, cot, vec, out, dr1, grads, sums,
    weights, nhat, n3, n3t, q, k, v, da, dat, qt, att, dyb, dq, dk, dv, dkt, dvt, dn3, acc, sem,
):
    step = pl.program_id(0)

    @pl.when(step == 0)
    def _():
        for copy in block_copies(owner, slots, weights, sem, 22, 4):
            copy.start()
        sums[...] = jnp.zeros((8, C), F32)

    mean, inv = norm_stats(lambda rows: r1[0, rows, :])
    gain = vec[8:9]
    bias = vec[9:10]
    image_weight = weight[step]

    def normalize(c, total):
        rows = rows_of(c, ROWS)
        normed = (r1[0, rows, :] - mean) * inv
        nhat[rows, :] = normed
        n3[rows, :] = (normed * gain + bias).astype(BF16)
        low = (cot[0, rows, :].astype(F32) * image_weight).astype(BF16)
        dyb[rows, :] = low
        return total + jnp.sum(low.astype(F32), axis=0, keepdims=True)

    zero = jnp.zeros((1, C), F32)
    sum_dy = chunks(HW // ROWS, normalize, zero)

    @pl.when(step == 0)
    def _():
        for copy in block_copies(owner, slots, weights, sem, 22, 4):
            copy.wait()

    def project(c, _):
        rows = rows_of(c, MM_ROWS)
        normed = n3[rows, :]
        q[rows, :] = (mm(normed, weights[0]) + vec[10:11]).astype(BF16) * 0.125
        k[rows, :] = mm(normed, weights[1]).astype(BF16)
        v[rows, :] = (mm(normed, weights[2]) + vec[11:12]).astype(BF16)
        da[rows, :] = mm_t(dyb[rows, :], weights[3]).astype(BF16)
        return 0

    chunks(HW // MM_ROWS, project)
    n3t[...] = n3[...].T
    qt[...] = q[...].T
    dat[...] = da[...].T

    def head_pair(pair, _):
        cols = pl.ds(pl.multiple_of(pair * 128, 128), 128)
        dkt[...] = jnp.zeros((128, HW), F32)
        dvt[...] = jnp.zeros((128, HW), F32)

        def query_rows(c, _):
            rows = rows_of(c, QROWS)
            keys = k[:, cols]
            values = v[:, cols]
            q_pair = q[rows, cols]
            da_pair = da[rows, cols]
            lane = lax.broadcasted_iota(jnp.int32, (QROWS, 128), 1)
            parts = []
            for side in range(2):
                mine = (lane < HEAD) if side == 0 else (lane >= HEAD)
                q_one = jnp.where(mine, q_pair, jnp.zeros_like(q_pair))
                da_one = jnp.where(mine, da_pair, jnp.zeros_like(da_pair))
                head_rows = pl.ds(pl.multiple_of(pair * 128 + side * HEAD, HEAD), HEAD)
                scores = mm_t(q_one, keys)
                top = jnp.max(scores, axis=1, keepdims=True)
                expo = jnp.exp(scores - top)
                probs = expo * (1.0 / jnp.sum(expo, axis=1, keepdims=True))
                low = probs.astype(BF16)
                dprobs = mm_t(da_one, values)
                dot = jnp.sum(probs * dprobs, axis=1, keepdims=True)
                dscores = (probs * (dprobs - dot)).astype(BF16)
                acc_rows = slice(side * HEAD, (side + 1) * HEAD)
                dvt[acc_rows, :] += mm(dat[head_rows, rows], low)
                dkt[acc_rows, :] += mm(qt[head_rows, rows], dscores)
                parts.append((mm(low, values), mm(dscores, keys)))
            first = lane < HEAD
            att[rows, cols] = jnp.where(first, parts[0][0], parts[1][0]).astype(BF16)
            dq[rows, cols] = (jnp.where(first, parts[0][1], parts[1][1]) * 0.125).astype(BF16)
            return 0

        chunks(HW // QROWS, query_rows)
        dk[:, cols] = dkt[...].astype(BF16).T
        dv[:, cols] = dvt[...].astype(BF16).T
        return 0

    chunks(HEADS // 2, head_pair)

    is_live = live[step] > 0

    def result(c, _):
        rows = rows_of(c, MM_ROWS)
        y = r1[0, rows, :] + mm(att[rows, :], weights[3]) + vec[12:13]
        out[0, rows, :] = jnp.where(is_live, y, 0.0).astype(BF16)
        dn3[rows, :] = (
            mm_t(dq[rows, :], weights[0])
            + mm_t(dk[rows, :], weights[1])
            + mm_t(dv[rows, :], weights[2])
        )
        return 0

    chunks(HW // MM_ROWS, result)

    qt[...] = att[...].T
    terms = (
        lambda: mm(n3t[...], dq[...]),
        lambda: mm(n3t[...], dk[...]),
        lambda: mm(n3t[...], dv[...]),
        lambda: mm(qt[...], dyb[...]),
    )
    for n, term in enumerate(terms):
        @pl.when(step == 0)
        def _(n=n, term=term):
            acc[n] = term()

        @pl.when(step != 0)
        def _(n=n, term=term):
            grads[n] = (acc[n] + term()).astype(BF16)

    def column_sums(c, totals):
        rows = rows_of(c, ROWS)
        grad = dn3[rows, :]
        new = (
            grad * nhat[rows, :],
            grad,
            dq[rows, :].astype(F32),
            dv[rows, :].astype(F32),
        )
        return tuple(t + jnp.sum(n, axis=0, keepdims=True) for t, n in zip(totals, new))

    sum_cross, sum_grad, sum_q, sum_v = chunks(HW // ROWS, column_sums, (zero,) * 4)
    sums[...] += jnp.concatenate(
        [sum_cross, sum_grad, sum_q, sum_v, sum_dy, jnp.zeros((3, C), F32)], axis=0
    )
    mean_grad = group_mean(gain * sum_grad)
    mean_cross = group_mean(gain * sum_cross)

    def back(c, _):
        rows = rows_of(c, ROWS)
        inner = gain * dn3[rows, :] - mean_grad - nhat[rows, :] * mean_cross
        dr1[0, rows, :] = cot[0, rows, :].astype(F32) * image_weight + inv * inner
        return 0

    chunks(HW // ROWS, back)


def split_three(value):
    high = value.astype(BF16)
    rest = value - high.astype(F32)
    middle = rest.astype(BF16)
    return high, middle, (rest - middle.astype(F32)).astype(BF16)


def bwd_two(
    owner, slots, dr1, a2, nhat, stats, vec, emb, actt, dh1, grads, map_grads, demb, sums,
    weights, maps, slab, at, dz, keep, sem,
):
    step = pl.program_id(0)
    last = pl.num_programs(0) - 1

    def copies():
        return block_copies(owner, slots, weights, sem, 9, 9) + block_copies_at(
            owner, slots, maps, sem, 18, 4, 9
        )

    @pl.when(step == 0)
    def _():
        for copy in copies():
            copy.start()
        clear_pads(slab)
        sums[...] = jnp.zeros((8, C), F32)

    zero = jnp.zeros((1, C), F32)

    def fill(c, total):
        chunk = dr1[0, rows_of(c, ROWS), :]
        store_slab(slab, (step,), c, chunk)
        return total + jnp.sum(chunk.astype(BF16).astype(F32), axis=0, keepdims=True)

    sum_h2 = chunks(HW // ROWS, fill, zero)
    at[step] = a2[0].T

    @pl.when(step == 0)
    def _():
        for copy in copies():
            copy.wait()

    scale = 1.0 + stats[0, 0:1]
    shift = stats[0, 1:2]
    inv = stats[0, 2:3]
    gain = vec[5:6]
    bias = vec[6:7]

    def conv(c, _):
        dz[rows_of(c, CONV_ROWS), :] = conv_rows(
            slab, (step,), weights, c * CONV_ROWS, CONV_ROWS, True
        )
        return 0

    chunks(HW // CONV_ROWS, conv)

    def slope(c, totals):
        rows = rows_of(c, ROWS)
        normed = nhat[0, rows, :]
        pre = (normed * gain + bias) * scale + shift
        grad = dz[rows, :] * silu_slope(pre)
        dz[rows, :] = grad
        return (
            totals[0] + jnp.sum(grad, axis=0, keepdims=True),
            totals[1] + jnp.sum(grad * normed, axis=0, keepdims=True),
        )

    sum_dz, sum_cross = chunks(HW // ROWS, slope, (zero, zero))
    factor = scale * gain
    mean_grad = group_mean(factor * sum_dz)
    mean_cross = group_mean(factor * sum_cross)

    def back(c, total):
        rows = rows_of(c, ROWS)
        low = (inv * (factor * dz[rows, :] - mean_grad - nhat[0, rows, :] * mean_cross)).astype(BF16)
        dh1[0, rows, :] = low
        return total + jnp.sum(low.astype(F32), axis=0, keepdims=True)

    sum_h1 = chunks(HW // ROWS, back, zero)
    dscale = gain * sum_cross + bias * sum_dz
    sums[...] += jnp.concatenate(
        [sum_h1, dscale, sum_dz, scale * sum_cross, scale * sum_dz, sum_h2, jnp.zeros((2, C), F32)],
        axis=0,
    )
    pieces_scale = split_three(dscale)
    pieces_shift = split_three(sum_dz)
    blank = jnp.zeros((5, C), F32)

    def stack(pieces):
        return jnp.concatenate([p.astype(F32) for p in pieces] + [blank], axis=0).astype(BF16)

    d_scale = stack(pieces_scale)
    d_shift = stack(pieces_shift)

    def reach(upper):
        parts = mm_t(d_scale, maps[upper]) + mm_t(d_shift, maps[2 + upper])
        return jnp.sum(parts, axis=0, keepdims=True)

    row = jnp.concatenate([reach(0), reach(1)], axis=1)
    demb[0] = jnp.broadcast_to(row * silu_slope(emb[0, 0:1].astype(F32)), (8, EMB))
    keep[step, 0] = d_scale
    keep[step, 1] = d_shift

    @pl.when(step == last)
    def _():
        def tap_grad(tap, _):
            di = 2 - tap // 3
            dj = tap // 3 * 3 + 2 - tap
            rows = pl.ds(pl.multiple_of(di * SIDE, SIDE), HW)
            grads[tap] = (mm(at[0], slab[0, dj, rows, :]) + mm(at[1], slab[1, dj, rows, :])).astype(
                BF16
            )
            return 0

        chunks(9, tap_grad)
        for n in range(4):
            half = n % 2
            seg = slice(half * C, (half + 1) * C)
            map_grads[n] = (
                mm(actt[0, seg, :], keep[0, n // 2]) + mm(actt[1, seg, :], keep[1, n // 2])
            ).astype(BF16)


def bwd_one_taps(dh1, a1, grads, slab, at):
    step = pl.program_id(0)

    @pl.when(step == 0)
    def _():
        clear_pads(slab)

    def fill(c, _):
        store_slab(slab, (step,), c, dh1[0, rows_of(c, ROWS), :].astype(F32))
        return 0

    chunks(HW // ROWS, fill)
    at[step] = a1[0].T

    @pl.when(step == pl.num_programs(0) - 1)
    def _():
        def tap_grad(tap, _):
            di = 2 - tap // 3
            dj = tap // 3 * 3 + 2 - tap
            rows = pl.ds(pl.multiple_of(di * SIDE, SIDE), HW)
            grads[tap] = (mm(at[0], slab[0, dj, rows, :]) + mm(at[1], slab[1, dj, rows, :])).astype(
                BF16
            )
            return 0

        chunks(9, tap_grad)


def bwd_one_data(owner, slots, dh1, x, dr1, vec, dx, sums, weights, slab, dp, sem):
    step = pl.program_id(0)

    @pl.when(step == 0)
    def _():
        for copy in block_copies(owner, slots, weights, sem, 0, 9):
            copy.start()
        clear_pads(slab)
        sums[...] = jnp.zeros((8, C), F32)

    def fill(c, _):
        store_slab(slab, (), c, dh1[0, rows_of(c, ROWS), :].astype(F32))
        return 0

    chunks(HW // ROWS, fill)

    def read(rows):
        return x[0, rows, :].astype(F32)

    mean, inv = norm_stats(read)
    gain = vec[0:1]
    bias = vec[1:2]

    @pl.when(step == 0)
    def _():
        for copy in block_copies(owner, slots, weights, sem, 0, 9):
            copy.wait()

    def conv(c, _):
        dp[rows_of(c, CONV_ROWS), :] = conv_rows(
            slab, (), weights, c * CONV_ROWS, CONV_ROWS, True
        )
        return 0

    chunks(HW // CONV_ROWS, conv)
    zero = jnp.zeros((1, C), F32)

    def slope(c, totals):
        rows = rows_of(c, ROWS)
        normed = (read(rows) - mean) * inv
        grad = dp[rows, :] * silu_slope(normed * gain + bias)
        dp[rows, :] = grad
        return (
            totals[0] + jnp.sum(grad * normed, axis=0, keepdims=True),
            totals[1] + jnp.sum(grad, axis=0, keepdims=True),
        )

    sum_cross, sum_grad = chunks(HW // ROWS, slope, (zero, zero))
    sums[...] += jnp.concatenate([sum_cross, sum_grad, jnp.zeros((6, C), F32)], axis=0)
    mean_grad = group_mean(gain * sum_grad)
    mean_cross = group_mean(gain * sum_cross)

    def back(c, _):
        rows = rows_of(c, ROWS)
        normed = (read(rows) - mean) * inv
        dx[0, rows, :] = dr1[0, rows, :] + inv * (
            gain * dp[rows, :] - mean_grad - normed * mean_cross
        )
        return 0

    chunks(HW // ROWS, back)


def per_image(*shape):
    return pl.BlockSpec((1,) + shape, lambda i: (i,) + (0,) * len(shape))


def whole(*shape):
    return pl.BlockSpec(shape, lambda i: (0,) * len(shape))


def struct(shape, kind):
    return jax.ShapeDtypeStruct(shape, kind)


def call(body, images, in_specs, out_specs, out_shape, scratch, args, name):
    return pl.pallas_call(
        body,
        grid=(images,),
        in_specs=in_specs,
        out_specs=out_specs,
        out_shape=out_shape,
        scratch_shapes=scratch,
        name=name,
        compiler_params=pltpu.CompilerParams(
            vmem_limit_bytes=VMEM_LIMIT, dimension_semantics=("arbitrary",)
        ),
    )(*args)


IMAGE = per_image(HW, C)
VEC = whole(VECS, C)
TAPS = whole(9, C, C)


def layer(images, embeds, cotangent, weight, live, owner, slots, vectors):
    count = images.shape[0]
    big = lambda kind: struct((count, HW, C), kind)
    taps = pltpu.VMEM((9, C, C), BF16)
    slab = pltpu.VMEM((3, SLAB, C), BF16)
    slabs = pltpu.VMEM((count, 3, SLAB, C), BF16)
    h1, a1 = call(
        fwd_one, count, [SMEM, ANY, IMAGE, VEC], [IMAGE, IMAGE], [big(F32), big(BF16)],
        [taps, slab, pltpu.SemaphoreType.DMA((9,))],
        (owner, slots, images, vectors), "first_conv",
    )
    emb = embeds.astype(F32)
    act = jax.nn.silu(emb).astype(BF16)
    act_rows = jnp.broadcast_to(act[:, None, :], (count, 16, EMB))
    a2, r1, nhat, stats = call(
        fwd_two, count, [SMEM, ANY, IMAGE, IMAGE, per_image(16, EMB), VEC],
        [IMAGE, IMAGE, IMAGE, per_image(8, C)],
        [big(BF16), big(F32), big(F32), struct((count, 8, C), F32)],
        [taps, pltpu.VMEM((4, C, C), BF16), slab, pltpu.SemaphoreType.DMA((13,))],
        (owner, slots, h1, images, act_rows, vectors), "second_conv",
    )
    low = pltpu.VMEM((HW, C), BF16)
    lowt = pltpu.VMEM((C, HW), BF16)
    full = pltpu.VMEM((HW, C), F32)
    pair = pltpu.VMEM((128, HW), F32)
    out, dr1, grads_attn, sums_attn = call(
        attention, count, [SMEM, ANY, SMEM, SMEM, IMAGE, IMAGE, VEC],
        [IMAGE, IMAGE, whole(4, C, C), whole(8, C)],
        [big(BF16), big(F32), struct((4, C, C), BF16), struct((8, C), F32)],
        [pltpu.VMEM((4, C, C), BF16), full, low, lowt, low, low, low, low, lowt, lowt, low, low,
         low, low, low, pair, pair, full, pltpu.VMEM((4, C, C), F32), pltpu.SemaphoreType.DMA((4,))],
        (owner, slots, weight, live, r1, cotangent, vectors), "attention",
    )
    actt = jnp.pad(jnp.broadcast_to(act[:, :, None], (count, EMB, 3)), ((0, 0), (0, 0), (0, 5)))
    emb_rows = jnp.broadcast_to(emb[:, None, :], (count, 8, EMB))
    dh1, grads_two, grads_maps, demb, sums_two = call(
        bwd_two, count,
        [SMEM, ANY, IMAGE, IMAGE, IMAGE, per_image(8, C), VEC, per_image(8, EMB), whole(count, EMB, 8)],
        [IMAGE, TAPS, whole(4, C, C), per_image(8, EMB), whole(8, C)],
        [big(BF16), struct((9, C, C), BF16), struct((4, C, C), BF16), struct((count, 8, EMB), F32),
         struct((8, C), F32)],
        [taps, pltpu.VMEM((4, C, C), BF16), slabs, pltpu.VMEM((count, C, HW), BF16), full,
         pltpu.VMEM((count, 2, 8, C), BF16), pltpu.SemaphoreType.DMA((13,))],
        (owner, slots, dr1, a2, nhat, stats, vectors, emb_rows, actt), "second_conv_back",
    )
    (grads_one,) = call(
        bwd_one_taps, count, [IMAGE, IMAGE], [TAPS], [struct((9, C, C), BF16)],
        [slabs, pltpu.VMEM((count, C, HW), BF16)], (dh1, a1), "first_conv_taps",
    )
    dx, sums_one = call(
        bwd_one_data, count, [SMEM, ANY, IMAGE, IMAGE, IMAGE, VEC], [IMAGE, whole(8, C)],
        [big(F32), struct((8, C), F32)],
        [taps, slab, full, pltpu.SemaphoreType.DMA((9,))],
        (owner, slots, dh1, images, dr1, vectors), "first_conv_back",
    )
    grads = (grads_one, grads_two, grads_maps, grads_attn)
    grad_vectors = jnp.concatenate([sums_one[:2], sums_two[:6], sums_attn[:5]], axis=0)
    return out, dx, demb[:, 0], grads, grad_vectors


def shards(
    images,
    embeds,
    cotangent,
    counts,
    bucket_weight,
    owner,
    master,
    first_moment,
    second_moment,
    left_basis,
    right_basis,
    vec_master,
    vec_first,
    vec_second,
):
    mat_dev = master.shape[0]
    mats_all = mat_dev * lax.axis_size("shard")
    slot_weights, vec_full = (
        lax.all_gather(master.astype(jnp.bfloat16), "shard", axis=0, tiled=True),
        lax.all_gather(vec_master.astype(jnp.bfloat16), "shard", axis=1, tiled=True),
    )
    vectors = vec_full.astype(jnp.float32)
    slot_ids = jnp.arange(images.shape[0], dtype=jnp.int32)
    live = (slot_ids < counts[0, 0] + counts[0, 1]).astype(jnp.int32)
    weight = jnp.where(slot_ids < counts[0, 0], bucket_weight[0], bucket_weight[1])
    weight = jnp.where(live > 0, weight, 0.0)
    outputs, grad_images, grad_embeds, grads, grad_vectors = layer(
        images, embeds, cotangent, weight, live, owner, slot_weights, vectors
    )
    one, two, maps, attn = grads
    grad_blocks = jnp.concatenate([one, two, maps, attn], axis=0)
    block_ids = jnp.arange(mats_all, dtype=jnp.int32)
    all_slots = jnp.sum(
        jnp.where(owner[None, :] == block_ids[:, None], block_ids[None, :], 0), axis=1
    )
    slot_block = lax.dynamic_slice_in_dim(all_slots, lax.axis_index("shard") * mat_dev, mat_dev, 0)
    picked = jnp.take(grad_blocks, jnp.minimum(all_slots, BLOCKS - 1), axis=0)
    grad_slot = jnp.where((all_slots < BLOCKS)[:, None, None], picked, jnp.zeros((), BF16))
    own_grads, own_vec = (
        lax.psum_scatter(grad_slot, "shard", scatter_dimension=0, tiled=True),
        lax.psum_scatter(
            grad_vectors.astype(jnp.bfloat16), "shard", scatter_dimension=1, tiled=True
        ),
    )
    own_grads, own_vec = (
        lax.psum(own_grads, "rep").astype(jnp.float32),
        lax.psum(own_vec, "rep").astype(jnp.float32),
    )
    rotated = jnp.matmul(
        jnp.matmul(jnp.swapaxes(left_basis, 1, 2), own_grads, precision=PRECISE),
        right_basis,
        precision=PRECISE,
    )
    new_first = MOMENT_DECAY * first_moment + (1.0 - MOMENT_DECAY) * rotated
    new_second = MOMENT_DECAY * second_moment + (1.0 - MOMENT_DECAY) * rotated * rotated
    correction = 1.0 - MOMENT_DECAY**STEP
    direction = new_first / correction / (jnp.sqrt(new_second / correction) + ADAM_EPS)
    update = jnp.matmul(
        jnp.matmul(left_basis, direction, precision=PRECISE),
        jnp.swapaxes(right_basis, 1, 2),
        precision=PRECISE,
    )
    step_rate = jnp.where(slot_block < BLOCKS, 2.0 * block_spread(slot_block), 0.0)
    new_master = master - step_rate[:, None, None] * (update + WEIGHT_DECAY * master)
    vec_first_new = MOMENT_DECAY * vec_first + (1.0 - MOMENT_DECAY) * own_vec
    vec_second_new = MOMENT_DECAY * vec_second + (1.0 - MOMENT_DECAY) * own_vec * own_vec
    vec_master_new = vec_master - VECTOR_RATE * (vec_first_new / correction) / (
        jnp.sqrt(vec_second_new / correction) + ADAM_EPS
    )
    return (
        outputs,
        grad_images,
        grad_embeds,
        new_first,
        new_second,
        new_master,
        new_master.astype(jnp.bfloat16),
        vec_first_new,
        vec_second_new,
        vec_master_new,
        vec_master_new.astype(jnp.bfloat16),
    )


def solution(mesh):
    return jax.shard_map(
        shards,
        mesh=mesh,
        in_specs=(
            P(("rep", "shard"), None, None),
            P(("rep", "shard"), None),
            P(("rep", "shard"), None, None),
            P(("rep", "shard"), None),
            P(),
            P(),
            P("shard", None, None),
            P("shard", None, None),
            P("shard", None, None),
            P("shard", None, None),
            P("shard", None, None),
            P(None, "shard"),
            P(None, "shard"),
            P(None, "shard"),
        ),
        out_specs=(
            P(("rep", "shard"), None, None),
            P(("rep", "shard"), None, None),
            P(("rep", "shard"), None),
            P("shard", None, None),
            P("shard", None, None),
            P("shard", None, None),
            P("shard", None, None),
            P(None, "shard"),
            P(None, "shard"),
            P(None, "shard"),
            P(None, "shard"),
        ),
        check_vma=False,
    )
```

```python
import functools
import math

import jax
import jax.numpy as jnp
from jax import lax
from jax.experimental import pallas as pl
from jax.experimental.pallas import tpu as pltpu
from jax.sharding import PartitionSpec as P

C = 512
EMB = 1024
HEADS = 8
HEAD = 64
GROUPS = 32
SIDE = 32
HW = 1024
BLOCKS = 26
VECS = 13
STEP = 2
PAD = SIDE
SLAB = HW + 2 * PAD
ROWS = 128
QROWS = 256

EPS_NORM = 1e-05
ADAM_EPS = 1e-08
MOMENT_DECAY = 0.5
WEIGHT_DECAY = 0.01
VECTOR_RATE = 0.2
PRECISE = lax.Precision.HIGHEST
F32 = jnp.float32
BF16 = jnp.bfloat16
ANY = pl.BlockSpec(memory_space=pl.ANY)
SMEM = pl.BlockSpec(memory_space=pltpu.SMEM)
VMEM = pl.BlockSpec(memory_space=pltpu.VMEM)
VMEM_LIMIT = 56 * 2**20


def block_spread(block_index):
    return jnp.where(
        block_index < 18,
        (9.0 * C) ** (-0.5),
        jnp.where(
            block_index < 22,
            EMB ** (-0.5),
            jnp.where(
                block_index < 24,
                1.25 * C ** (-0.5),
                jnp.where(
                    block_index < 25,
                    C ** (-0.5),
                    jnp.where(block_index < 26, 0.295 * (HW / C) ** 0.5, C ** (-0.5)),
                ),
            ),
        ),
    )


def mm(a, b):
    return jnp.dot(a, b, preferred_element_type=F32)


def mm_t(a, b):
    return lax.dot_general(a, b, (((1,), (1,)), ((), ())), preferred_element_type=F32)


def sigmoid(u):
    return 1.0 / (1.0 + jnp.exp(-u))


def silu_slope(u):
    s = sigmoid(u)
    return s * (1.0 + u * (1.0 - s))


def chunks(count, body, init=0):
    return lax.fori_loop(0, count, body, init)


def rows_of(index, size):
    return pl.ds(pl.multiple_of(index * size, size), size)


def group_mean(column_sum):
    total = jnp.broadcast_to(column_sum, (8, C))
    lane = lax.broadcasted_iota(jnp.int32, (8, C), 1)
    for step in (1, 2, 4, 8):
        other = jnp.where(
            (lane & step) != 0, pltpu.roll(total, step, 1), pltpu.roll(total, C - step, 1)
        )
        total = total + other
    return total[0:1] * (1.0 / (HW * (C // GROUPS)))


def norm_stats(read):
    zero = jnp.zeros((1, C), F32)
    total = chunks(
        HW // ROWS,
        lambda c, t: t + jnp.sum(read(rows_of(c, ROWS)), axis=0, keepdims=True),
        zero,
    )
    mean = group_mean(total)

    def squares(c, t):
        centered = read(rows_of(c, ROWS)) - mean
        return t + jnp.sum(centered * centered, axis=0, keepdims=True)

    var = group_mean(chunks(HW // ROWS, squares, zero))
    return mean, lax.rsqrt(var + EPS_NORM)


def clear_pads(slab):
    zeros = jnp.zeros((PAD, C), BF16)
    for lead in slab_leads(slab):
        slab[lead + (pl.ds(0, PAD), slice(None))] = zeros
        slab[lead + (pl.ds(PAD + HW, PAD), slice(None))] = zeros


def slab_leads(slab):
    if len(slab.shape) == 3:
        return [(j,) for j in range(3)]
    return [(i, j) for i in range(slab.shape[0]) for j in range(3)]


def store_slab(slab, lead, c, chunk):
    column = lax.broadcasted_iota(jnp.int32, (ROWS, C), 0) & (SIDE - 1)
    before = jnp.where(column == 0, 0.0, pltpu.roll(chunk, 1, 0))
    after = jnp.where(column == SIDE - 1, 0.0, pltpu.roll(chunk, ROWS - 1, 0))
    rows = pl.ds(pl.multiple_of(c * ROWS + PAD, PAD), ROWS)
    slab[lead + (0, rows, slice(None))] = before.astype(BF16)
    slab[lead + (1, rows, slice(None))] = chunk.astype(BF16)
    slab[lead + (2, rows, slice(None))] = after.astype(BF16)


def conv_rows(slab, lead, weights, base, size, back):
    total = None
    for tap in range(9):
        di, dj = tap // 3, tap % 3
        if back:
            di, dj = 2 - di, 2 - dj
        rows = pl.ds(pl.multiple_of(base + di * SIDE, SIDE), size)
        piece = slab[lead + (dj, rows, slice(None))]
        term = (mm_t if back else mm)(piece, weights[tap])
        total = term if total is None else total + term
    return total


CONV_ROWS = 512


PIECES = 32
PIECE = C // PIECES


def piece_rows(ids, core, plane, line):
    index = ((ids[0] ^ core) * 4 + (ids[1] ^ plane)) * 4 + (ids[2] ^ line)
    return pl.ds(pl.multiple_of(index * PIECE, PIECE), PIECE)


def flat_place(n):
    return (n % 2 * 4 + n // 16 * 2 + n // 2 % 2) * 4 + n // 4 % 4


def block_copies(ids, parts, dest, sem, first, count):
    if len(parts) == 1:
        return [
            pltpu.make_async_copy(
                parts[0].at[n, pl.ds(first, count)],
                dest.at[:, pl.ds(flat_place(n) * PIECE, PIECE), :],
                sem.at[n],
            )
            for n in range(PIECES)
        ]
    copies = []
    for core in range(2):
        for plane in range(4):
            for line in range(4):
                copies.append(
                    pltpu.make_async_copy(
                        parts[core * 4 + plane].at[line, pl.ds(first, count)],
                        dest.at[:, piece_rows(ids, core, plane, line), :],
                        sem.at[len(copies)],
                    )
                )
    return copies


def start_all(*args):
    for copy in block_copies(*args):
        copy.start()


def wait_all(*args):
    for copy in block_copies(*args):
        copy.wait()


def store_flat(out, block, grad):
    for n in range(PIECES):
        place = flat_place(n) * PIECE
        out[n % 16, block, n // 16] = grad[place : place + PIECE]


def store_pieces(ids, keep, send, block, grad):
    half = C // 2
    mine = ids[0] == 0
    kept = jnp.where(mine, grad[:half], grad[half:])
    sent = jnp.where(mine, grad[half:], grad[:half])
    for plane in range(4):
        for line in range(4):
            rows = slice((plane * 4 + line) * PIECE, (plane * 4 + line + 1) * PIECE)
            keep[plane ^ ids[1], line ^ ids[2], block] = kept[rows]
            send[plane ^ ids[1], line ^ ids[2], block] = sent[rows]


def fwd_one(ids, *refs):
    parts, (x, vec, h1, a1, weights, slab, sem) = refs[:8], refs[8:]
    step = pl.program_id(0)

    @pl.when(step == 0)
    def _():
        start_all(ids, parts, weights, sem, 0, 9)
        clear_pads(slab)

    def read(rows):
        return x[0, rows, :].astype(F32)

    mean, inv = norm_stats(read)
    gain = inv * vec[0:1]
    bias = vec[1:2]

    def activate(c, _):
        rows = rows_of(c, ROWS)
        pre = (read(rows) - mean) * gain + bias
        act = pre * sigmoid(pre)
        a1[0, rows, :] = act.astype(BF16)
        store_slab(slab, (), c, act)
        return 0

    chunks(HW // ROWS, activate)

    @pl.when(step == 0)
    def _():
        wait_all(ids, parts, weights, sem, 0, 9)

    def conv(c, _):
        h1[0, rows_of(c, CONV_ROWS), :] = (
            conv_rows(slab, (), weights, c * CONV_ROWS, CONV_ROWS, False) + vec[2:3]
        )
        return 0

    chunks(HW // CONV_ROWS, conv)


def fwd_two(ids, *refs):
    parts = refs[:8]
    h1, x, act, vec, a2, r1, nhat, stats, weights, maps, slab, sem, map_sem = refs[8:]
    step = pl.program_id(0)

    @pl.when(step == 0)
    def _():
        start_all(ids, parts, maps, map_sem, 9, 4)
        start_all(ids, parts, weights, sem, 0, 9)
        clear_pads(slab)

    mean, inv = norm_stats(lambda rows: h1[0, rows, :])

    @pl.when(step == 0)
    def _():
        wait_all(ids, parts, maps, map_sem, 9, 4)

    row = act[0]
    scale = (mm(row[:, :C], maps[0]) + mm(row[:, C:], maps[1]))[0:1] + vec[3:4]
    shift = (mm(row[:, :C], maps[2]) + mm(row[:, C:], maps[3]))[0:1] + vec[4:5]
    stats[0] = jnp.concatenate([scale, shift, inv, jnp.zeros((5, C), F32)], axis=0)
    gain = vec[5:6]
    bias = vec[6:7]

    def activate(c, _):
        rows = rows_of(c, ROWS)
        normed = (h1[0, rows, :] - mean) * inv
        nhat[0, rows, :] = normed
        pre = (normed * gain + bias) * (1.0 + scale) + shift
        act_two = pre * sigmoid(pre)
        a2[0, rows, :] = act_two.astype(BF16)
        store_slab(slab, (), c, act_two)
        return 0

    chunks(HW // ROWS, activate)

    @pl.when(step == 0)
    def _():
        wait_all(ids, parts, weights, sem, 0, 9)

    def conv(c, _):
        rows = rows_of(c, CONV_ROWS)
        hidden = conv_rows(slab, (), weights, c * CONV_ROWS, CONV_ROWS, False) + vec[7:8]
        r1[0, rows, :] = x[0, rows, :].astype(F32) + hidden
        return 0

    chunks(HW // CONV_ROWS, conv)


MM_ROWS = 512


def attention(ids, weight, live, *refs):
    parts = refs[:1]
    (
    r1, cot, vec, out, dr1, grads, sums, weights, nhat, n3, n3t, q, k, v, da, dat, qt, att, dyb, dq, dk, dv, dkt, dvt, dn3, acc, sem,
    ) = refs[1:]
    step = pl.program_id(0)

    @pl.when(step == 0)
    def _():
        start_all(ids, parts, weights, sem, 0, 4)
        sums[...] = jnp.zeros((8, C), F32)

    mean, inv = norm_stats(lambda rows: r1[0, rows, :])
    gain = vec[8:9]
    bias = vec[9:10]
    image_weight = weight[step]

    def normalize(c, total):
        rows = rows_of(c, ROWS)
        normed = (r1[0, rows, :] - mean) * inv
        nhat[rows, :] = normed
        n3[rows, :] = (normed * gain + bias).astype(BF16)
        low = (cot[0, rows, :].astype(F32) * image_weight).astype(BF16)
        dyb[rows, :] = low
        return total + jnp.sum(low.astype(F32), axis=0, keepdims=True)

    zero = jnp.zeros((1, C), F32)
    sum_dy = chunks(HW // ROWS, normalize, zero)

    @pl.when(step == 0)
    def _():
        wait_all(ids, parts, weights, sem, 0, 4)

    def project(c, _):
        rows = rows_of(c, MM_ROWS)
        normed = n3[rows, :]
        q[rows, :] = (mm(normed, weights[0]) + vec[10:11]).astype(BF16) * 0.125
        k[rows, :] = mm(normed, weights[1]).astype(BF16)
        v[rows, :] = (mm(normed, weights[2]) + vec[11:12]).astype(BF16)
        da[rows, :] = mm_t(dyb[rows, :], weights[3]).astype(BF16)
        return 0

    chunks(HW // MM_ROWS, project)
    n3t[...] = n3[...].T
    qt[...] = q[...].T
    dat[...] = da[...].T

    def head_pair(pair, _):
        cols = pl.ds(pl.multiple_of(pair * 128, 128), 128)
        dkt[...] = jnp.zeros((128, HW), F32)
        dvt[...] = jnp.zeros((128, HW), F32)

        def query_rows(c, _):
            rows = rows_of(c, QROWS)
            keys = k[:, cols]
            values = v[:, cols]
            q_pair = q[rows, cols]
            da_pair = da[rows, cols]
            lane = lax.broadcasted_iota(jnp.int32, (QROWS, 128), 1)
            parts = []
            for side in range(2):
                mine = (lane < HEAD) if side == 0 else (lane >= HEAD)
                q_one = jnp.where(mine, q_pair, jnp.zeros_like(q_pair))
                da_one = jnp.where(mine, da_pair, jnp.zeros_like(da_pair))
                head_rows = pl.ds(pl.multiple_of(pair * 128 + side * HEAD, HEAD), HEAD)
                scores = mm_t(q_one, keys)
                top = jnp.max(scores, axis=1, keepdims=True)
                expo = jnp.exp(scores - top)
                probs = expo * (1.0 / jnp.sum(expo, axis=1, keepdims=True))
                low = probs.astype(BF16)
                dprobs = mm_t(da_one, values)
                dot = jnp.sum(probs * dprobs, axis=1, keepdims=True)
                dscores = (probs * (dprobs - dot)).astype(BF16)
                acc_rows = slice(side * HEAD, (side + 1) * HEAD)
                dvt[acc_rows, :] += mm(dat[head_rows, rows], low)
                dkt[acc_rows, :] += mm(qt[head_rows, rows], dscores)
                parts.append((mm(low, values), mm(dscores, keys)))
            first = lane < HEAD
            att[rows, cols] = jnp.where(first, parts[0][0], parts[1][0]).astype(BF16)
            dq[rows, cols] = (jnp.where(first, parts[0][1], parts[1][1]) * 0.125).astype(BF16)
            return 0

        chunks(HW // QROWS, query_rows)
        dk[:, cols] = dkt[...].astype(BF16).T
        dv[:, cols] = dvt[...].astype(BF16).T
        return 0

    chunks(HEADS // 2, head_pair)

    is_live = live[step] > 0

    def result(c, _):
        rows = rows_of(c, MM_ROWS)
        y = r1[0, rows, :] + mm(att[rows, :], weights[3]) + vec[12:13]
        out[0, rows, :] = jnp.where(is_live, y, 0.0).astype(BF16)
        dn3[rows, :] = (
            mm_t(dq[rows, :], weights[0])
            + mm_t(dk[rows, :], weights[1])
            + mm_t(dv[rows, :], weights[2])
        )
        return 0

    chunks(HW // MM_ROWS, result)

    qt[...] = att[...].T
    terms = (
        lambda: mm(n3t[...], dq[...]),
        lambda: mm(n3t[...], dk[...]),
        lambda: mm(n3t[...], dv[...]),
        lambda: mm(qt[...], dyb[...]),
    )
    for n, term in enumerate(terms):
        @pl.when(step == 0)
        def _(n=n, term=term):
            acc[n] = term()

        @pl.when(step != 0)
        def _(n=n, term=term):
            store_flat(grads, n, (acc[n] + term()).astype(BF16))

    def column_sums(c, totals):
        rows = rows_of(c, ROWS)
        grad = dn3[rows, :]
        new = (
            grad * nhat[rows, :],
            grad,
            dq[rows, :].astype(F32),
            dv[rows, :].astype(F32),
        )
        return tuple(t + jnp.sum(n, axis=0, keepdims=True) for t, n in zip(totals, new))

    sum_cross, sum_grad, sum_q, sum_v = chunks(HW // ROWS, column_sums, (zero,) * 4)
    sums[...] += jnp.concatenate(
        [sum_cross, sum_grad, sum_q, sum_v, sum_dy, jnp.zeros((3, C), F32)], axis=0
    )
    mean_grad = group_mean(gain * sum_grad)
    mean_cross = group_mean(gain * sum_cross)

    def back(c, _):
        rows = rows_of(c, ROWS)
        inner = gain * dn3[rows, :] - mean_grad - nhat[rows, :] * mean_cross
        dr1[0, rows, :] = cot[0, rows, :].astype(F32) * image_weight + inv * inner
        return 0

    chunks(HW // ROWS, back)


def split_three(value):
    high = value.astype(BF16)
    rest = value - high.astype(F32)
    middle = rest.astype(BF16)
    return high, middle, (rest - middle.astype(F32)).astype(BF16)


def bwd_two_data(ids, *refs):
    parts = refs[:8]
    dr1, nhat, stats, vec, emb, dh1, dvec, demb, sums = refs[8:17]
    weights, maps, slab, dz, sem, map_sem = refs[17:]
    step = pl.program_id(0)

    @pl.when(step == 0)
    def _():
        start_all(ids, parts, weights, sem, 0, 9)
        start_all(ids, parts, maps, map_sem, 9, 4)
        clear_pads(slab)
        sums[...] = jnp.zeros((8, C), F32)

    zero = jnp.zeros((1, C), F32)

    def fill(c, total):
        chunk = dr1[0, rows_of(c, ROWS), :]
        store_slab(slab, (), c, chunk)
        return total + jnp.sum(chunk.astype(BF16).astype(F32), axis=0, keepdims=True)

    sum_h2 = chunks(HW // ROWS, fill, zero)

    @pl.when(step == 0)
    def _():
        wait_all(ids, parts, weights, sem, 0, 9)
        wait_all(ids, parts, maps, map_sem, 9, 4)

    scale = 1.0 + stats[0, 0:1]
    shift = stats[0, 1:2]
    inv = stats[0, 2:3]
    gain = vec[5:6]
    bias = vec[6:7]

    def conv(c, _):
        dz[rows_of(c, CONV_ROWS), :] = conv_rows(
            slab, (), weights, c * CONV_ROWS, CONV_ROWS, True
        )
        return 0

    chunks(HW // CONV_ROWS, conv)

    def slope(c, totals):
        rows = rows_of(c, ROWS)
        normed = nhat[0, rows, :]
        pre = (normed * gain + bias) * scale + shift
        grad = dz[rows, :] * silu_slope(pre)
        dz[rows, :] = grad
        return (
            totals[0] + jnp.sum(grad, axis=0, keepdims=True),
            totals[1] + jnp.sum(grad * normed, axis=0, keepdims=True),
        )

    sum_dz, sum_cross = chunks(HW // ROWS, slope, (zero, zero))
    factor = scale * gain
    mean_grad = group_mean(factor * sum_dz)
    mean_cross = group_mean(factor * sum_cross)

    def back(c, total):
        rows = rows_of(c, ROWS)
        low = (inv * (factor * dz[rows, :] - mean_grad - nhat[0, rows, :] * mean_cross)).astype(BF16)
        dh1[0, rows, :] = low
        return total + jnp.sum(low.astype(F32), axis=0, keepdims=True)

    sum_h1 = chunks(HW // ROWS, back, zero)
    dscale = gain * sum_cross + bias * sum_dz
    sums[...] += jnp.concatenate(
        [sum_h1, dscale, sum_dz, scale * sum_cross, scale * sum_dz, sum_h2, jnp.zeros((2, C), F32)],
        axis=0,
    )
    pieces_scale = split_three(dscale)
    pieces_shift = split_three(sum_dz)
    blank = jnp.zeros((5, C), F32)

    def stack(pieces):
        return jnp.concatenate([p.astype(F32) for p in pieces] + [blank], axis=0).astype(BF16)

    d_scale = stack(pieces_scale)
    d_shift = stack(pieces_shift)

    def reach(upper):
        parts = mm_t(d_scale, maps[upper]) + mm_t(d_shift, maps[2 + upper])
        return jnp.sum(parts, axis=0, keepdims=True)

    row = jnp.concatenate([reach(0), reach(1)], axis=1)
    demb[0] = jnp.broadcast_to(row * silu_slope(emb[0, 0:1].astype(F32)), (8, EMB))
    dvec[0] = jnp.concatenate([dscale, sum_dz, jnp.zeros((6, C), F32)], axis=0)


def fill_taps(grad, act, slab, at):
    step = pl.program_id(0)

    @pl.when(step == 0)
    def _():
        clear_pads(slab)

    def fill(c, _):
        store_slab(slab, (step,), c, grad[0, rows_of(c, ROWS), :].astype(F32))
        return 0

    chunks(HW // ROWS, fill)
    at[step] = act[0].T


def tap_grad(slab, at, tap):
    di = 2 - tap // 3
    dj = tap // 3 * 3 + 2 - tap
    rows = pl.ds(pl.multiple_of(di * SIDE, SIDE), HW)
    total = mm(at[0], slab[0, dj, rows, :])
    for image in range(1, slab.shape[0]):
        total = total + mm(at[image], slab[image, dj, rows, :])
    return total.astype(BF16)


def one_taps(ids, grad, act, keep, send, slab, at):
    fill_taps(grad, act, slab, at)

    @pl.when(pl.program_id(0) == pl.num_programs(0) - 1)
    def _():
        def one(tap, _):
            store_pieces(ids, keep, send, tap, tap_grad(slab, at, tap))
            return 0

        chunks(9, one)


def two_taps(grad, act, others, out, slab, at):
    fill_taps(grad, act, slab, at)

    @pl.when(pl.program_id(0) == pl.num_programs(0) - 1)
    def _():
        out[:, pl.ds(9, 4)] = others[...]

        def one(tap, _):
            store_flat(out, tap, tap_grad(slab, at, tap))
            return 0

        chunks(9, one)


def bwd_one_data(ids, *refs):
    parts, (dh1, x, dr1, vec, dx, sums, weights, slab, dp, sem) = refs[:8], refs[8:]
    step = pl.program_id(0)

    @pl.when(step == 0)
    def _():
        start_all(ids, parts, weights, sem, 0, 9)
        clear_pads(slab)
        sums[...] = jnp.zeros((8, C), F32)

    def fill(c, _):
        store_slab(slab, (), c, dh1[0, rows_of(c, ROWS), :].astype(F32))
        return 0

    chunks(HW // ROWS, fill)

    def read(rows):
        return x[0, rows, :].astype(F32)

    mean, inv = norm_stats(read)
    gain = vec[0:1]
    bias = vec[1:2]

    @pl.when(step == 0)
    def _():
        wait_all(ids, parts, weights, sem, 0, 9)

    def conv(c, _):
        dp[rows_of(c, CONV_ROWS), :] = conv_rows(
            slab, (), weights, c * CONV_ROWS, CONV_ROWS, True
        )
        return 0

    chunks(HW // CONV_ROWS, conv)
    zero = jnp.zeros((1, C), F32)

    def slope(c, totals):
        rows = rows_of(c, ROWS)
        normed = (read(rows) - mean) * inv
        grad = dp[rows, :] * silu_slope(normed * gain + bias)
        dp[rows, :] = grad
        return (
            totals[0] + jnp.sum(grad * normed, axis=0, keepdims=True),
            totals[1] + jnp.sum(grad, axis=0, keepdims=True),
        )

    sum_cross, sum_grad = chunks(HW // ROWS, slope, (zero, zero))
    sums[...] += jnp.concatenate([sum_cross, sum_grad, jnp.zeros((6, C), F32)], axis=0)
    mean_grad = group_mean(gain * sum_grad)
    mean_cross = group_mean(gain * sum_cross)

    def back(c, _):
        rows = rows_of(c, ROWS)
        normed = (read(rows) - mean) * inv
        dx[0, rows, :] = dr1[0, rows, :] + inv * (
            gain * dp[rows, :] - mean_grad - normed * mean_cross
        )
        return 0

    chunks(HW // ROWS, back)


def per_image(*shape):
    return pl.BlockSpec((1,) + shape, lambda i: (i,) + (0,) * len(shape))


def whole(*shape):
    return pl.BlockSpec(shape, lambda i: (0,) * len(shape))


def struct(shape, kind):
    return jax.ShapeDtypeStruct(shape, kind)


def call(body, images, in_specs, out_specs, out_shape, scratch, args, name, flops=20 * 10**9):
    return pl.pallas_call(
        body,
        grid=(images,),
        in_specs=in_specs,
        out_specs=out_specs,
        out_shape=out_shape,
        scratch_shapes=scratch,
        name=name,
        compiler_params=pltpu.CompilerParams(
            vmem_limit_bytes=VMEM_LIMIT, dimension_semantics=("arbitrary",)
        ),
        cost_estimate=pl.CostEstimate(flops=flops, bytes_accessed=30 * 2**20, transcendentals=0),
    )(*args)


IMAGE = per_image(HW, C)
VEC = whole(16, C)
PARTS = [ANY] * 8
SEMS = pltpu.SemaphoreType.DMA((PIECES,))


def layer(images, embeds, cotangent, weight, live, plan, gathered):
    chunk_one, vectors, planes_two, chunk_attn = gathered
    ids = plan.ids
    count = images.shape[0]
    big = lambda kind: struct((count, HW, C), kind)
    taps = pltpu.VMEM((9, C, C), BF16)
    maps = pltpu.VMEM((4, C, C), BF16)
    slab = pltpu.VMEM((3, SLAB, C), BF16)
    slabs = pltpu.VMEM((count, 3, SLAB, C), BF16)
    turned = pltpu.VMEM((count, C, HW), BF16)
    low = pltpu.VMEM((HW, C), BF16)
    lowt = pltpu.VMEM((C, HW), BF16)
    full = pltpu.VMEM((HW, C), F32)
    pair = pltpu.VMEM((128, HW), F32)
    h1, a1 = call(
        fwd_one, count, [SMEM] + PARTS + [IMAGE, VEC], [IMAGE, IMAGE], [big(F32), big(BF16)],
        [taps, slab, SEMS], (ids, *chunk_one, images, vectors), "first_conv",
    )
    planes_two, h1 = lax.optimization_barrier((planes_two, h1))
    chunk_two = plan.gather_core(planes_two)
    emb = embeds.astype(F32)
    act = jax.nn.silu(emb).astype(BF16)
    act_rows = jnp.broadcast_to(act[:, None, :], (count, 16, EMB))
    a2, r1, nhat, stats = call(
        fwd_two, count, [SMEM] + PARTS + [IMAGE, IMAGE, per_image(16, EMB), VEC],
        [IMAGE, IMAGE, IMAGE, per_image(8, C)],
        [big(BF16), big(F32), big(F32), struct((count, 8, C), F32)],
        [taps, maps, slab, SEMS, SEMS],
        (ids, *chunk_two, h1, images, act_rows, vectors), "second_conv",
    )
    out, dr1, grads_attn, sums_attn = call(
        attention, count, [SMEM, SMEM, SMEM, ANY] + [IMAGE, IMAGE, VEC],
        [IMAGE, IMAGE, whole(16, 4, 2, PIECE, C), whole(8, C)],
        [big(BF16), big(F32), struct((16, 4, 2, PIECE, C), BF16), struct((8, C), F32)],
        [maps, full, low, lowt, low, low, low, low, lowt, lowt, low, low,
         low, low, low, pair, pair, full, pltpu.VMEM((4, C, C), F32), SEMS],
        (ids, weight, live, chunk_attn, r1, cotangent, vectors), "attention", 80 * 10**9,
    )
    (early,) = call(
        two_taps, count, [IMAGE, IMAGE, whole(16, 4, 2, PIECE, C)],
        [whole(16, 13, 2, PIECE, C)], [struct((16, 13, 2, PIECE, C), BF16)],
        [slabs, turned], (dr1, a2, grads_attn), "second_conv_taps",
    )
    grads_early = plan.reduce_early(early)
    dr1, _ = lax.optimization_barrier((dr1, early))
    emb_rows = jnp.broadcast_to(emb[:, None, :], (count, 8, EMB))
    dh1, dvec, demb, sums_two = call(
        bwd_two_data, count,
        [SMEM] + PARTS + [IMAGE, IMAGE, per_image(8, C), VEC, per_image(8, EMB)],
        [IMAGE, per_image(8, C), per_image(8, EMB), whole(8, C)],
        [big(BF16), struct((count, 8, C), F32), struct((count, 8, EMB), F32), struct((8, C), F32)],
        [taps, maps, slab, full, SEMS, SEMS],
        (ids, *chunk_two, dr1, nhat, stats, vectors, emb_rows), "second_conv_back",
    )
    late = call(
        one_taps, count, [SMEM, IMAGE, IMAGE], [whole(4, 4, 9, PIECE, C)] * 2,
        [struct((4, 4, 9, PIECE, C), BF16)] * 2,
        [slabs, turned], (ids, dh1, a1), "first_conv_taps",
    )
    planes = plan.reduce_core(*late)
    dh1, _ = lax.optimization_barrier((dh1, planes))
    dx, sums_one = call(
        bwd_one_data, count, [SMEM] + PARTS + [IMAGE, IMAGE, IMAGE, VEC], [IMAGE, whole(8, C)],
        [big(F32), struct((8, C), F32)],
        [taps, slab, full, SEMS],
        (ids, *chunk_one, dh1, images, dr1, vectors), "first_conv_back",
    )
    grads_late = plan.reduce_late(planes, dx)
    grads = plan.finish_early(grads_late, grads_early)
    map_terms = jnp.concatenate([act.astype(F32), dvec[:, 0], dvec[:, 1]], axis=1).astype(BF16)
    grad_vectors = jnp.concatenate([sums_one[:2], sums_two[:6], sums_attn[:5]], axis=0)
    return out, dx, demb[:, 0], grads, map_terms, grad_vectors


AXES = ("rep", "shard")


def swap(value, mask):
    return lax.ppermute(value, AXES, [(i, i ^ mask) for i in range(PIECES)])


def plane_mask(step):
    return (step // 2) * 16 + (step % 2) * 2


def gather_line(piece):
    return jnp.stack([piece] + [swap(piece, 4 * k) for k in (1, 2, 3)])


def gather_plane(line):
    return [line] + [swap(line, plane_mask(k)) for k in (1, 2, 3)]


def gather_core(plane):
    return plane + [swap(part, 1) for part in plane]


def add_up(*terms):
    total = terms[0].astype(F32)
    for term in terms[1:]:
        total = total + term.astype(F32)
    return total.astype(BF16)


def block_slots(owner, mats_all):
    block_ids = jnp.arange(mats_all, dtype=jnp.int32)
    return jnp.sum(
        jnp.where(owner[None, :] == block_ids[:, None], block_ids[None, :], 0), axis=1
    )


def pick_slots(grads, slots):
    index = jnp.where(slots < 18, slots, jnp.clip(slots - 4, 0, 21))
    held = (slots < 18) | ((slots >= 22) & (slots < BLOCKS))
    picked = jnp.take(grads, index, axis=0)
    return jnp.where(held.reshape((-1,) + (1,) * (grads.ndim - 1)), picked, jnp.zeros((), BF16))


class Split:
    def __init__(self):
        self.rep = lax.axis_index("rep")
        shard = lax.axis_index("shard")
        self.ids = jnp.stack([shard % 2, self.rep * 2 + shard // 2 % 2, shard // 4])

    def gather(self, master, vec_master, owner):
        mat_dev = master.shape[0]
        rows = master.astype(BF16).reshape(mat_dev, 2, 2, 2, 4, PIECE, C)
        rows = lax.dynamic_index_in_dim(rows, self.rep, 2, keepdims=False)
        rows = rows.transpose(3, 2, 1, 0, 4, 5).reshape(16, mat_dev, PIECE, C)
        slots = lax.all_to_all(rows, "shard", 0, 0).reshape(16 * mat_dev, PIECE, C)
        blocks = jnp.take(slots, owner[:BLOCKS], axis=0)
        width = vec_master.shape[1]
        vec = jnp.pad(vec_master.astype(BF16), ((0, 16 - VECS), (0, C - width)))
        place = lax.axis_index("shard") * width
        vec = jnp.where(self.rep == 0, jnp.roll(vec, place, axis=1), jnp.zeros((), BF16))
        attn = lax.all_gather(blocks[22:26], AXES)
        line_one = gather_line(jnp.concatenate([blocks[:9], vec[None]], axis=0))
        second, line_one = lax.optimization_barrier((blocks[9:22], line_one))
        plane_one = gather_plane(line_one)
        line_two = gather_line(second)
        line_two, plane_one = lax.optimization_barrier((line_two, plane_one))
        one = gather_core(plane_one)
        two = gather_plane(line_two)
        vectors = sum(jnp.sum(part[:, 9].astype(F32), axis=0) for part in one)
        return one, vectors, two, attn

    def gather_core(self, planes):
        return gather_core(planes)

    def reduce_early(self, grads):
        return lax.psum_scatter(grads, "shard", scatter_dimension=0, tiled=True)[0]

    def finish_early(self, late, *early):
        own = jnp.concatenate(early, axis=0)
        mine = lax.dynamic_index_in_dim(own, self.rep, 1, keepdims=False)
        other = lax.dynamic_index_in_dim(own, 1 - self.rep, 1, keepdims=False)
        return jnp.concatenate([late, add_up(mine, swap(other, 16))], axis=0)

    def reduce_core(self, keep, send):
        other = swap(send, 1)
        return [add_up(keep[k], other[k]) for k in range(4)]

    def reduce_late(self, planes, after):
        line = [swap(planes[k], plane_mask(k)) for k in (1, 2, 3)]
        lines = [add_up(planes[0][j], *[part[j] for part in line]) for j in range(4)]
        lines, _ = lax.optimization_barrier((lines, after))
        return add_up(lines[0], *[swap(lines[k], 4 * k) for k in (1, 2, 3)])

    def own(self, grads, slots, mat_dev, map_terms, grad_vectors):
        picked = pick_slots(grads, slots).reshape(16, mat_dev * PIECE, C)
        terms = jnp.broadcast_to(map_terms.reshape(1, -1, C), (16, map_terms.size // C, C))
        width = C // 16
        vec = grad_vectors.astype(BF16).reshape(VECS, 16, width).transpose(1, 0, 2)
        vec = jnp.pad(vec.reshape(16, 1, VECS * width), ((0, 0), (0, 0), (0, C - VECS * width)))
        sent = jnp.concatenate([picked, terms, vec], axis=1)
        mine = lax.all_to_all(sent, "shard", 0, 0)
        other = swap(mine, 16)
        first = jnp.where(self.rep == 0, mine, other)
        second = jnp.where(self.rep == 0, other, mine)
        both = jnp.stack([first, second])
        split = mat_dev * PIECE
        rows = both[:, :, :split].reshape(2, 4, 2, 2, mat_dev, PIECE, C)
        rows = rows.transpose(4, 3, 0, 2, 1, 5, 6).reshape(mat_dev, C, C)
        terms = both[:, :, split:-1].reshape(-1, map_terms.shape[1])
        vec = jnp.sum(both[:, :, -1, : VECS * width].astype(F32), axis=(0, 1))
        return rows.astype(F32), terms, vec.reshape(VECS, width)


class Plain:
    def __init__(self):
        self.ids = jnp.zeros((3,), jnp.int32)

    def gather(self, master, vec_master, owner):
        slots = lax.all_gather(master.astype(BF16), "shard", axis=0, tiled=True)
        vec = lax.all_gather(vec_master.astype(BF16), "shard", axis=1, tiled=True)
        blocks = jnp.take(slots, owner[:BLOCKS], axis=0)

        def parts(some):
            split = some.reshape(-1, 2, 4, 4, PIECE, C).transpose(1, 2, 3, 0, 4, 5)
            return [split[core, plane] for core in range(2) for plane in range(4)]

        vectors = jnp.pad(vec.astype(F32), ((0, 16 - VECS), (0, 0)))
        flat = blocks[22:26].reshape(4, 2, 2, 2, 4, PIECE, C).transpose(2, 4, 3, 1, 0, 5, 6)
        attn = flat.reshape(PIECES, 4, PIECE, C)
        return parts(blocks[:9]), vectors, parts(blocks[9:22]), attn

    def gather_core(self, planes):
        return planes

    def reduce_early(self, grads):
        split = grads.reshape(4, 2, 2, -1, 2, PIECE, C).transpose(3, 2, 4, 1, 0, 5, 6)
        return split.reshape(-1, C, C)

    def finish_early(self, late, *early):
        return jnp.concatenate([late, *early], axis=0)

    def reduce_core(self, keep, send):
        return [jnp.stack([keep, send]).transpose(3, 0, 1, 2, 4, 5).reshape(-1, C, C)]

    def reduce_late(self, planes, after):
        return planes[0]

    def own(self, grads, slots, mat_dev, map_terms, grad_vectors):
        picked = pick_slots(grads, slots)
        mine = lax.psum_scatter(picked, "shard", scatter_dimension=0, tiled=True)
        rows = lax.psum(mine, "rep").astype(F32)
        terms = lax.all_gather(map_terms, AXES, axis=0, tiled=True)
        vec = lax.psum_scatter(grad_vectors, "shard", scatter_dimension=1, tiled=True)
        return rows, terms, lax.psum(vec, "rep")


def shards(
    images,
    embeds,
    cotangent,
    counts,
    bucket_weight,
    owner,
    master,
    first_moment,
    second_moment,
    left_basis,
    right_basis,
    vec_master,
    vec_first,
    vec_second,
):
    mat_dev = master.shape[0]
    mats_all = mat_dev * lax.axis_size("shard")
    sizes = (lax.axis_size("rep"), lax.axis_size("shard"))
    plan = Split() if sizes == (2, 16) else Plain()
    gathered = plan.gather(master, vec_master, owner)
    slot_ids = jnp.arange(images.shape[0], dtype=jnp.int32)
    live = (slot_ids < counts[0, 0] + counts[0, 1]).astype(jnp.int32)
    weight = jnp.where(slot_ids < counts[0, 0], bucket_weight[0], bucket_weight[1])
    weight = jnp.where(live > 0, weight, 0.0)
    outputs, grad_images, grad_embeds, grads, map_terms, grad_vectors = layer(
        images, embeds, cotangent, weight, live, plan, gathered
    )
    all_slots = block_slots(owner, mats_all)
    shard = lax.axis_index("shard")
    slot_block = lax.dynamic_slice_in_dim(all_slots, shard * mat_dev, mat_dev, 0)
    own_grads, all_terms, own_vec = plan.own(
        grads, all_slots, mat_dev, map_terms, grad_vectors
    )
    maps = slot_block - 18
    lower = (maps % 2 == 0)[:, None, None]
    acts = jnp.where(lower, all_terms[None, :, :C], all_terms[None, :, C:EMB])
    is_scale = (maps < 2)[:, None, None]
    sides = jnp.where(is_scale, all_terms[None, :, EMB : EMB + C], all_terms[None, :, EMB + C :])
    map_grads = jnp.einsum("sic,sio->sco", acts, sides, preferred_element_type=F32)
    is_map = ((maps >= 0) & (maps < 4))[:, None, None]
    own_grads = jnp.where(is_map, map_grads, own_grads)
    rotated = jnp.matmul(
        jnp.matmul(jnp.swapaxes(left_basis, 1, 2), own_grads, precision=PRECISE),
        right_basis,
        precision=PRECISE,
    )
    new_first = MOMENT_DECAY * first_moment + (1.0 - MOMENT_DECAY) * rotated
    new_second = MOMENT_DECAY * second_moment + (1.0 - MOMENT_DECAY) * rotated * rotated
    correction = 1.0 - MOMENT_DECAY**STEP
    direction = new_first / correction / (jnp.sqrt(new_second / correction) + ADAM_EPS)
    update = jnp.matmul(
        jnp.matmul(left_basis, direction, precision=PRECISE),
        jnp.swapaxes(right_basis, 1, 2),
        precision=PRECISE,
    )
    step_rate = jnp.where(slot_block < BLOCKS, 2.0 * block_spread(slot_block), 0.0)
    new_master = master - step_rate[:, None, None] * (update + WEIGHT_DECAY * master)
    vec_first_new = MOMENT_DECAY * vec_first + (1.0 - MOMENT_DECAY) * own_vec
    vec_second_new = MOMENT_DECAY * vec_second + (1.0 - MOMENT_DECAY) * own_vec * own_vec
    vec_master_new = vec_master - VECTOR_RATE * (vec_first_new / correction) / (
        jnp.sqrt(vec_second_new / correction) + ADAM_EPS
    )
    return (
        outputs,
        grad_images,
        grad_embeds,
        new_first,
        new_second,
        new_master,
        new_master.astype(jnp.bfloat16),
        vec_first_new,
        vec_second_new,
        vec_master_new,
        vec_master_new.astype(jnp.bfloat16),
    )


def solution(mesh):
    return jax.shard_map(
        shards,
        mesh=mesh,
        in_specs=(
            P(("rep", "shard"), None, None),
            P(("rep", "shard"), None),
            P(("rep", "shard"), None, None),
            P(("rep", "shard"), None),
            P(),
            P(),
            P("shard", None, None),
            P("shard", None, None),
            P("shard", None, None),
            P("shard", None, None),
            P("shard", None, None),
            P(None, "shard"),
            P(None, "shard"),
            P(None, "shard"),
        ),
        out_specs=(
            P(("rep", "shard"), None, None),
            P(("rep", "shard"), None, None),
            P(("rep", "shard"), None),
            P("shard", None, None),
            P("shard", None, None),
            P("shard", None, None),
            P("shard", None, None),
            P(None, "shard"),
            P(None, "shard"),
            P(None, "shard"),
            P(None, "shard"),
        ),
        check_vma=False,
    )
```

```python
import functools
import math

import jax
import jax.numpy as jnp
from jax import lax
from jax.experimental import pallas as pl
from jax.experimental.pallas import tpu as pltpu
from jax.sharding import PartitionSpec as P

C = 512
EMB = 1024
HEADS = 8
HEAD = 64
GROUPS = 32
SIDE = 32
HW = 1024
BLOCKS = 26
VECS = 13
STEP = 2
PAD = SIDE
SLAB = HW + 2 * PAD
ROWS = 128
QROWS = 256

EPS_NORM = 1e-05
ADAM_EPS = 1e-08
MOMENT_DECAY = 0.5
WEIGHT_DECAY = 0.01
VECTOR_RATE = 0.2
PRECISE = lax.Precision.HIGHEST
F32 = jnp.float32
BF16 = jnp.bfloat16
ANY = pl.BlockSpec(memory_space=pl.ANY)
SMEM = pl.BlockSpec(memory_space=pltpu.SMEM)
VMEM = pl.BlockSpec(memory_space=pltpu.VMEM)
VMEM_LIMIT = 56 * 2**20


def block_spread(block_index):
    return jnp.where(
        block_index < 18,
        (9.0 * C) ** (-0.5),
        jnp.where(
            block_index < 22,
            EMB ** (-0.5),
            jnp.where(
                block_index < 24,
                1.25 * C ** (-0.5),
                jnp.where(
                    block_index < 25,
                    C ** (-0.5),
                    jnp.where(block_index < 26, 0.295 * (HW / C) ** 0.5, C ** (-0.5)),
                ),
            ),
        ),
    )


def mm(a, b):
    return jnp.dot(a, b, preferred_element_type=F32)


def mm_t(a, b):
    return lax.dot_general(a, b, (((1,), (1,)), ((), ())), preferred_element_type=F32)


def sigmoid(u):
    return 1.0 / (1.0 + jnp.exp(-u))


def silu_slope(u):
    s = sigmoid(u)
    return s * (1.0 + u * (1.0 - s))


def chunks(count, body, init=0):
    return lax.fori_loop(0, count, body, init)


def rows_of(index, size):
    return pl.ds(pl.multiple_of(index * size, size), size)


def group_mean(column_sum):
    total = jnp.broadcast_to(column_sum, (8, C))
    lane = lax.broadcasted_iota(jnp.int32, (8, C), 1)
    for step in (1, 2, 4, 8):
        other = jnp.where(
            (lane & step) != 0, pltpu.roll(total, step, 1), pltpu.roll(total, C - step, 1)
        )
        total = total + other
    return total[0:1] * (1.0 / (HW * (C // GROUPS)))


def norm_stats(read):
    zero = jnp.zeros((1, C), F32)
    total = chunks(
        HW // ROWS,
        lambda c, t: t + jnp.sum(read(rows_of(c, ROWS)), axis=0, keepdims=True),
        zero,
    )
    mean = group_mean(total)

    def squares(c, t):
        centered = read(rows_of(c, ROWS)) - mean
        return t + jnp.sum(centered * centered, axis=0, keepdims=True)

    var = group_mean(chunks(HW // ROWS, squares, zero))
    return mean, lax.rsqrt(var + EPS_NORM)


def clear_pads(slab):
    zeros = jnp.zeros((PAD, C), BF16)
    for lead in slab_leads(slab):
        slab[lead + (pl.ds(0, PAD), slice(None))] = zeros
        slab[lead + (pl.ds(PAD + HW, PAD), slice(None))] = zeros


def slab_leads(slab):
    if len(slab.shape) == 3:
        return [(j,) for j in range(3)]
    return [(i, j) for i in range(slab.shape[0]) for j in range(3)]


def store_slab(slab, lead, c, chunk):
    column = lax.broadcasted_iota(jnp.int32, (ROWS, C), 0) & (SIDE - 1)
    before = jnp.where(column == 0, 0.0, pltpu.roll(chunk, 1, 0))
    after = jnp.where(column == SIDE - 1, 0.0, pltpu.roll(chunk, ROWS - 1, 0))
    rows = pl.ds(pl.multiple_of(c * ROWS + PAD, PAD), ROWS)
    slab[lead + (0, rows, slice(None))] = before.astype(BF16)
    slab[lead + (1, rows, slice(None))] = chunk.astype(BF16)
    slab[lead + (2, rows, slice(None))] = after.astype(BF16)


def conv_rows(slab, lead, weights, base, size, back):
    total = None
    for tap in range(9):
        di, dj = tap // 3, tap % 3
        if back:
            di, dj = 2 - di, 2 - dj
        rows = pl.ds(pl.multiple_of(base + di * SIDE, SIDE), size)
        piece = slab[lead + (dj, rows, slice(None))]
        term = (mm_t if back else mm)(piece, weights[tap])
        total = term if total is None else total + term
    return total


CONV_ROWS = 1024


PIECES = 32
PIECE = C // PIECES


def piece_rows(ids, core, plane, line):
    index = ((ids[0] ^ core) * 4 + (ids[1] ^ plane)) * 4 + (ids[2] ^ line)
    return pl.ds(pl.multiple_of(index * PIECE, PIECE), PIECE)


DIRECT = (((0,), 0), ((1,), 0), ((2,), 0), ((3,), 0))
HALVED = (((0, 2), 0), ((1, 3), 0), ((0, 1), 1), ((2, 3), 1))
COPIES = 64


def flat_place(n):
    return (n % 2 * 4 + n // 16 * 2 + n // 2 % 2) * 4 + n // 4 % 4


def block_copies(ids, parts, dest, sem, first, count):
    if len(parts) == 1:
        return [
            pltpu.make_async_copy(
                parts[0].at[n, pl.ds(first, count)],
                dest.at[:, pl.ds(flat_place(n) * PIECE, PIECE), :],
                sem.at[n],
            )
            for n in range(PIECES)
        ]
    copies = []
    layout = HALVED if parts[0].shape[0] == 2 else DIRECT
    for n, part in enumerate(parts):
        planes, half = layout[n % 4]
        start = half * parts[0].shape[2]
        low, high = max(first, start), min(first + count, start + part.shape[2])
        if low >= high:
            continue
        for side, plane in enumerate(planes):
            for line in range(4):
                rows = piece_rows(ids, n // 4, plane, line)
                copies.append(
                    pltpu.make_async_copy(
                        part.at[side, line, pl.ds(low - start, high - low)],
                        dest.at[pl.ds(low - first, high - low), rows, :],
                        sem.at[len(copies)],
                    )
                )
    return copies


def start_all(*args):
    for copy in block_copies(*args):
        copy.start()


def wait_all(*args):
    for copy in block_copies(*args):
        copy.wait()


def store_flat(out, block, grad):
    for n in range(PIECES):
        place = flat_place(n) * PIECE
        out[n % 16, block, n // 16] = grad[place : place + PIECE]


def store_pieces(ids, keep, send, block, grad):
    half = C // 2
    mine = ids[0] == 0
    kept = jnp.where(mine, grad[:half], grad[half:])
    sent = jnp.where(mine, grad[half:], grad[:half])
    for plane in range(4):
        for line in range(4):
            rows = slice((plane * 4 + line) * PIECE, (plane * 4 + line + 1) * PIECE)
            keep[plane ^ ids[1], line ^ ids[2], block] = kept[rows]
            send[plane ^ ids[1], line ^ ids[2], block] = sent[rows]


def fwd_one(ids, *refs):
    parts, (x, h1, a1, vec, weights, slab, held, sem, vec_sem) = refs[:8], refs[8:]
    step = pl.program_id(0)

    def vec_copies():
        last = [part for n, part in enumerate(parts) if n % 4 > 1]
        return [
            pltpu.make_async_copy(part.at[:, :, part.shape[2] - 1], held.at[n], vec_sem.at[n])
            for n, part in enumerate(last)
        ]

    @pl.when(step == 0)
    def _():
        for copy in vec_copies():
            copy.start()
        start_all(ids, parts, weights, sem, 0, 9)
        clear_pads(slab)

    def read(rows):
        return x[0, rows, :].astype(F32)

    mean, inv = norm_stats(read)

    @pl.when(step == 0)
    def _():
        for copy in vec_copies():
            copy.wait()
        total = jnp.zeros((16, C), F32)
        for n in range(PIECES):
            total = total + held[n // 8, n // 4 % 2, n % 4].astype(F32)
        vec[...] = total

    gain = inv * vec[0:1]
    bias = vec[1:2]

    def activate(c, _):
        rows = rows_of(c, ROWS)
        pre = (read(rows) - mean) * gain + bias
        act = pre * sigmoid(pre)
        a1[0, rows, :] = act.astype(BF16)
        store_slab(slab, (), c, act)
        return 0

    chunks(HW // ROWS, activate)

    @pl.when(step == 0)
    def _():
        wait_all(ids, parts, weights, sem, 0, 9)

    def conv(c, _):
        h1[0, rows_of(c, CONV_ROWS), :] = (
            conv_rows(slab, (), weights, c * CONV_ROWS, CONV_ROWS, False) + vec[2:3]
        )
        return 0

    chunks(HW // CONV_ROWS, conv)


def fwd_two(ids, *refs):
    parts = refs[:8]
    h1, x, act, vec, a2, r1, nhat, stats, weights, maps, slab, sem, map_sem = refs[8:]
    step = pl.program_id(0)

    @pl.when(step == 0)
    def _():
        start_all(ids, parts, maps, map_sem, 9, 4)
        start_all(ids, parts, weights, sem, 0, 9)
        clear_pads(slab)

    mean, inv = norm_stats(lambda rows: h1[0, rows, :])

    @pl.when(step == 0)
    def _():
        wait_all(ids, parts, maps, map_sem, 9, 4)

    row = act[0]
    scale = (mm(row[:, :C], maps[0]) + mm(row[:, C:], maps[1]))[0:1] + vec[3:4]
    shift = (mm(row[:, :C], maps[2]) + mm(row[:, C:], maps[3]))[0:1] + vec[4:5]
    stats[0] = jnp.concatenate([scale, shift, inv, jnp.zeros((5, C), F32)], axis=0)
    gain = vec[5:6]
    bias = vec[6:7]

    def activate(c, _):
        rows = rows_of(c, ROWS)
        normed = (h1[0, rows, :] - mean) * inv
        nhat[0, rows, :] = normed
        pre = (normed * gain + bias) * (1.0 + scale) + shift
        act_two = pre * sigmoid(pre)
        a2[0, rows, :] = act_two.astype(BF16)
        store_slab(slab, (), c, act_two)
        return 0

    chunks(HW // ROWS, activate)

    @pl.when(step == 0)
    def _():
        wait_all(ids, parts, weights, sem, 0, 9)

    def conv(c, _):
        rows = rows_of(c, CONV_ROWS)
        hidden = conv_rows(slab, (), weights, c * CONV_ROWS, CONV_ROWS, False) + vec[7:8]
        r1[0, rows, :] = x[0, rows, :].astype(F32) + hidden
        return 0

    chunks(HW // CONV_ROWS, conv)


MM_ROWS = 512


def attention(ids, weight, live, *refs):
    parts = refs[:1]
    (
    r1, cot, vec, out, dr1, grads, sums, weights,
    nhat, n3, n3t, q, k, v, da, dat, qt, kt, vt, att, dyb, dq, dk, dv, dn3, acc, sem,
    ) = refs[1:]
    step = pl.program_id(0)

    @pl.when(step == 0)
    def _():
        start_all(ids, parts, weights, sem, 0, 4)
        sums[...] = jnp.zeros((8, C), F32)

    mean, inv = norm_stats(lambda rows: r1[0, rows, :])
    gain = vec[8:9]
    bias = vec[9:10]
    image_weight = weight[step]

    def normalize(c, total):
        rows = rows_of(c, ROWS)
        normed = (r1[0, rows, :] - mean) * inv
        nhat[rows, :] = normed
        n3[rows, :] = (normed * gain + bias).astype(BF16)
        low = (cot[0, rows, :].astype(F32) * image_weight).astype(BF16)
        dyb[rows, :] = low
        return total + jnp.sum(low.astype(F32), axis=0, keepdims=True)

    zero = jnp.zeros((1, C), F32)
    sum_dy = chunks(HW // ROWS, normalize, zero)

    @pl.when(step == 0)
    def _():
        wait_all(ids, parts, weights, sem, 0, 4)

    def project(c, _):
        rows = rows_of(c, MM_ROWS)
        normed = n3[rows, :]
        q[rows, :] = (mm(normed, weights[0]) + vec[10:11]).astype(BF16) * 0.125
        k[rows, :] = mm(normed, weights[1]).astype(BF16)
        v[rows, :] = (mm(normed, weights[2]) + vec[11:12]).astype(BF16)
        da[rows, :] = mm_t(dyb[rows, :], weights[3]).astype(BF16)
        return 0

    chunks(HW // MM_ROWS, project)
    n3t[...] = n3[...].T
    qt[...] = q[...].T
    kt[...] = k[...].T
    vt[...] = v[...].T
    dat[...] = da[...].T

    def head_pair(pair, _):
        cols = pl.ds(pl.multiple_of(pair * 128, 128), 128)
        first = lax.broadcasted_iota(jnp.int32, (HW, 128), 1) < HEAD

        def one_head(value, side):
            blank = jnp.zeros_like(value)
            return jnp.where(first, value, blank) if side == 0 else jnp.where(first, blank, value)

        keys, values = k[:, cols], v[:, cols]
        expos, scaled, dots = [], [], []
        for side in range(2):
            head_rows = pl.ds(pl.multiple_of(pair * 128 + side * HEAD, HEAD), HEAD)
            scores = mm(one_head(keys, side), qt[cols, :])
            expo = jnp.exp(scores - jnp.max(scores, axis=0, keepdims=True))
            inverse = 1.0 / jnp.sum(expo, axis=0, keepdims=True)
            expos.append(expo.astype(BF16))
            attended = mm(vt[head_rows, :], expos[side]) * inverse
            att[head_rows, :] = attended.astype(BF16)
            scaled.append((dat[head_rows, :].astype(F32) * inverse).astype(BF16))
            dots.append(jnp.sum(attended * scaled[side].astype(F32), axis=0, keepdims=True))
        both = jnp.concatenate(scaled, axis=0)
        turned = both.T
        dks, dvs = [], []
        for side in range(2):
            head_rows = pl.ds(pl.multiple_of(pair * 128 + side * HEAD, HEAD), HEAD)
            dprobs = mm(one_head(values, side), both)
            dscores = (expos[side].astype(F32) * (dprobs - dots[side])).astype(BF16)
            dvs.append(mm(expos[side], turned))
            dks.append(mm(dscores, q[:, cols]))
            dat[head_rows, :] = (mm(kt[head_rows, :], dscores) * 0.125).astype(BF16)
        dk[:, cols] = jnp.where(first, dks[0], dks[1]).astype(BF16)
        dv[:, cols] = jnp.where(first, dvs[0], dvs[1]).astype(BF16)
        return 0

    chunks(HEADS // 2, head_pair)
    dq[...] = dat[...].T
    q[...] = att[...].T

    is_live = live[step] > 0

    def result(c, _):
        rows = rows_of(c, MM_ROWS)
        y = r1[0, rows, :] + mm(q[rows, :], weights[3]) + vec[12:13]
        out[0, rows, :] = jnp.where(is_live, y, 0.0).astype(BF16)
        dn3[rows, :] = (
            mm_t(dq[rows, :], weights[0])
            + mm_t(dk[rows, :], weights[1])
            + mm_t(dv[rows, :], weights[2])
        )
        return 0

    chunks(HW // MM_ROWS, result)

    terms = (
        lambda: mm(n3t[...], dq[...]),
        lambda: mm(n3t[...], dk[...]),
        lambda: mm(n3t[...], dv[...]),
        lambda: mm(att[...], dyb[...]),
    )
    for n, term in enumerate(terms):
        @pl.when(step == 0)
        def _(n=n, term=term):
            acc[n] = term()

        @pl.when(step != 0)
        def _(n=n, term=term):
            store_flat(grads, n, (acc[n] + term()).astype(BF16))

    def column_sums(c, totals):
        rows = rows_of(c, ROWS)
        grad = dn3[rows, :]
        new = (
            grad * nhat[rows, :],
            grad,
            dq[rows, :].astype(F32),
            dv[rows, :].astype(F32),
        )
        return tuple(t + jnp.sum(n, axis=0, keepdims=True) for t, n in zip(totals, new))

    sum_cross, sum_grad, sum_q, sum_v = chunks(HW // ROWS, column_sums, (zero,) * 4)
    sums[...] += jnp.concatenate(
        [sum_cross, sum_grad, sum_q, sum_v, sum_dy, jnp.zeros((3, C), F32)], axis=0
    )
    mean_grad = group_mean(gain * sum_grad)
    mean_cross = group_mean(gain * sum_cross)

    def back(c, _):
        rows = rows_of(c, ROWS)
        inner = gain * dn3[rows, :] - mean_grad - nhat[rows, :] * mean_cross
        dr1[0, rows, :] = cot[0, rows, :].astype(F32) * image_weight + inv * inner
        return 0

    chunks(HW // ROWS, back)


def split_three(value):
    high = value.astype(BF16)
    rest = value - high.astype(F32)
    middle = rest.astype(BF16)
    return high, middle, (rest - middle.astype(F32)).astype(BF16)


def bwd_two_data(ids, *refs):
    parts = refs[:8]
    dr1, nhat, stats, vec, emb, dh1, dvec, demb, sums = refs[8:17]
    weights, maps, slab, dz, sem, map_sem = refs[17:]
    step = pl.program_id(0)

    @pl.when(step == 0)
    def _():
        start_all(ids, parts, weights, sem, 0, 9)
        start_all(ids, parts, maps, map_sem, 9, 4)
        clear_pads(slab)
        sums[...] = jnp.zeros((8, C), F32)

    zero = jnp.zeros((1, C), F32)

    def fill(c, total):
        chunk = dr1[0, rows_of(c, ROWS), :]
        store_slab(slab, (), c, chunk)
        return total + jnp.sum(chunk.astype(BF16).astype(F32), axis=0, keepdims=True)

    sum_h2 = chunks(HW // ROWS, fill, zero)

    @pl.when(step == 0)
    def _():
        wait_all(ids, parts, weights, sem, 0, 9)
        wait_all(ids, parts, maps, map_sem, 9, 4)

    scale = 1.0 + stats[0, 0:1]
    shift = stats[0, 1:2]
    inv = stats[0, 2:3]
    gain = vec[5:6]
    bias = vec[6:7]

    def conv(c, _):
        dz[rows_of(c, CONV_ROWS), :] = conv_rows(
            slab, (), weights, c * CONV_ROWS, CONV_ROWS, True
        )
        return 0

    chunks(HW // CONV_ROWS, conv)

    def slope(c, totals):
        rows = rows_of(c, ROWS)
        normed = nhat[0, rows, :]
        pre = (normed * gain + bias) * scale + shift
        grad = dz[rows, :] * silu_slope(pre)
        dz[rows, :] = grad
        return (
            totals[0] + jnp.sum(grad, axis=0, keepdims=True),
            totals[1] + jnp.sum(grad * normed, axis=0, keepdims=True),
        )

    sum_dz, sum_cross = chunks(HW // ROWS, slope, (zero, zero))
    factor = scale * gain
    mean_grad = group_mean(factor * sum_dz)
    mean_cross = group_mean(factor * sum_cross)

    def back(c, total):
        rows = rows_of(c, ROWS)
        low = (inv * (factor * dz[rows, :] - mean_grad - nhat[0, rows, :] * mean_cross)).astype(BF16)
        dh1[0, rows, :] = low
        return total + jnp.sum(low.astype(F32), axis=0, keepdims=True)

    sum_h1 = chunks(HW // ROWS, back, zero)
    dscale = gain * sum_cross + bias * sum_dz
    sums[...] += jnp.concatenate(
        [sum_h1, dscale, sum_dz, scale * sum_cross, scale * sum_dz, sum_h2, jnp.zeros((2, C), F32)],
        axis=0,
    )
    pieces_scale = split_three(dscale)
    pieces_shift = split_three(sum_dz)
    blank = jnp.zeros((5, C), F32)

    def stack(pieces):
        return jnp.concatenate([p.astype(F32) for p in pieces] + [blank], axis=0).astype(BF16)

    d_scale = stack(pieces_scale)
    d_shift = stack(pieces_shift)

    def reach(upper):
        parts = mm_t(d_scale, maps[upper]) + mm_t(d_shift, maps[2 + upper])
        return jnp.sum(parts, axis=0, keepdims=True)

    row = jnp.concatenate([reach(0), reach(1)], axis=1)
    demb[0] = jnp.broadcast_to(row * silu_slope(emb[0, 0:1].astype(F32)), (8, EMB))
    dvec[0] = jnp.concatenate([dscale, sum_dz, jnp.zeros((6, C), F32)], axis=0)


def fill_taps(grad, act, slab, at):
    step = pl.program_id(0)

    @pl.when(step == 0)
    def _():
        clear_pads(slab)

    def fill(c, _):
        store_slab(slab, (step,), c, grad[0, rows_of(c, ROWS), :].astype(F32))
        return 0

    chunks(HW // ROWS, fill)
    at[step] = act[0].T


def tap_grad(slab, at, tap):
    di = 2 - tap // 3
    dj = tap // 3 * 3 + 2 - tap
    rows = pl.ds(pl.multiple_of(di * SIDE, SIDE), HW)
    total = mm(at[0], slab[0, dj, rows, :])
    for image in range(1, slab.shape[0]):
        total = total + mm(at[image], slab[image, dj, rows, :])
    return total.astype(BF16)


def one_taps(ids, grad, act, keep, send, slab, at):
    fill_taps(grad, act, slab, at)

    @pl.when(pl.program_id(0) == pl.num_programs(0) - 1)
    def _():
        def one(tap, _):
            store_pieces(ids, keep, send, tap, tap_grad(slab, at, tap))
            return 0

        for tap in range(9):
            one(tap, 0)


def two_taps(grad, act, others, out, slab, at):
    fill_taps(grad, act, slab, at)

    @pl.when(pl.program_id(0) == pl.num_programs(0) - 1)
    def _():
        out[:, pl.ds(9, 4)] = others[...]

        def one(tap, _):
            store_flat(out, tap, tap_grad(slab, at, tap))
            return 0

        for tap in range(9):
            one(tap, 0)


def bwd_one_data(ids, *refs):
    parts, (dh1, x, dr1, vec, dx, sums, weights, slab, dp, sem) = refs[:8], refs[8:]
    step = pl.program_id(0)

    @pl.when(step == 0)
    def _():
        start_all(ids, parts, weights, sem, 0, 9)
        clear_pads(slab)
        sums[...] = jnp.zeros((8, C), F32)

    def fill(c, _):
        store_slab(slab, (), c, dh1[0, rows_of(c, ROWS), :].astype(F32))
        return 0

    chunks(HW // ROWS, fill)

    def read(rows):
        return x[0, rows, :].astype(F32)

    mean, inv = norm_stats(read)
    gain = vec[0:1]
    bias = vec[1:2]

    @pl.when(step == 0)
    def _():
        wait_all(ids, parts, weights, sem, 0, 9)

    def conv(c, _):
        dp[rows_of(c, CONV_ROWS), :] = conv_rows(
            slab, (), weights, c * CONV_ROWS, CONV_ROWS, True
        )
        return 0

    chunks(HW // CONV_ROWS, conv)
    zero = jnp.zeros((1, C), F32)

    def slope(c, totals):
        rows = rows_of(c, ROWS)
        normed = (read(rows) - mean) * inv
        grad = dp[rows, :] * silu_slope(normed * gain + bias)
        dp[rows, :] = grad
        return (
            totals[0] + jnp.sum(grad * normed, axis=0, keepdims=True),
            totals[1] + jnp.sum(grad, axis=0, keepdims=True),
        )

    sum_cross, sum_grad = chunks(HW // ROWS, slope, (zero, zero))
    sums[...] += jnp.concatenate([sum_cross, sum_grad, jnp.zeros((6, C), F32)], axis=0)
    mean_grad = group_mean(gain * sum_grad)
    mean_cross = group_mean(gain * sum_cross)

    def back(c, _):
        rows = rows_of(c, ROWS)
        normed = (read(rows) - mean) * inv
        dx[0, rows, :] = dr1[0, rows, :] + inv * (
            gain * dp[rows, :] - mean_grad - normed * mean_cross
        )
        return 0

    chunks(HW // ROWS, back)


def per_image(*shape):
    return pl.BlockSpec((1,) + shape, lambda i: (i,) + (0,) * len(shape))


def whole(*shape):
    return pl.BlockSpec(shape, lambda i: (0,) * len(shape))


def struct(shape, kind):
    return jax.ShapeDtypeStruct(shape, kind)


def call(body, images, in_specs, out_specs, out_shape, scratch, args, name, flops=20 * 10**9):
    return pl.pallas_call(
        body,
        grid=(images,),
        in_specs=in_specs,
        out_specs=out_specs,
        out_shape=out_shape,
        scratch_shapes=scratch,
        name=name,
        compiler_params=pltpu.CompilerParams(
            vmem_limit_bytes=VMEM_LIMIT, dimension_semantics=("arbitrary",)
        ),
        cost_estimate=pl.CostEstimate(flops=flops, bytes_accessed=30 * 2**20, transcendentals=0),
    )(*args)


IMAGE = per_image(HW, C)
VEC = whole(16, C)
PARTS = [ANY] * 8
SEMS = pltpu.SemaphoreType.DMA((COPIES,))


def layer(images, embeds, cotangent, weight, live, plan, gathered):
    chunk_one, planes_two, chunk_attn = gathered
    ids = plan.ids
    count = images.shape[0]
    big = lambda kind: struct((count, HW, C), kind)
    taps = pltpu.VMEM((9, C, C), BF16)
    maps = pltpu.VMEM((4, C, C), BF16)
    slab = pltpu.VMEM((3, SLAB, C), BF16)
    slabs = pltpu.VMEM((count, 3, SLAB, C), BF16)
    turned = pltpu.VMEM((count, C, HW), BF16)
    low = pltpu.VMEM((HW, C), BF16)
    lowt = pltpu.VMEM((C, HW), BF16)
    full = pltpu.VMEM((HW, C), F32)
    h1, a1, vectors = call(
        fwd_one, count, [SMEM] + PARTS + [IMAGE], [IMAGE, IMAGE, VEC],
        [big(F32), big(BF16), struct((16, C), F32)],
        [taps, slab, pltpu.VMEM((4, 2, 4, PIECE, C), BF16), SEMS, pltpu.SemaphoreType.DMA((4,))],
        (ids, *chunk_one, images), "first_conv",
    )
    planes_two, h1 = lax.optimization_barrier((planes_two, h1))
    chunk_two = plan.gather_core(planes_two)
    emb = embeds.astype(F32)
    act = jax.nn.silu(emb).astype(BF16)
    act_rows = jnp.broadcast_to(act[:, None, :], (count, 16, EMB))
    a2, r1, nhat, stats = call(
        fwd_two, count, [SMEM] + PARTS + [IMAGE, IMAGE, per_image(16, EMB), VEC],
        [IMAGE, IMAGE, IMAGE, per_image(8, C)],
        [big(BF16), big(F32), big(F32), struct((count, 8, C), F32)],
        [taps, maps, slab, SEMS, SEMS],
        (ids, *chunk_two, h1, images, act_rows, vectors), "second_conv",
    )
    out, dr1, grads_attn, sums_attn = call(
        attention, count, [SMEM, SMEM, SMEM, ANY] + [IMAGE, IMAGE, VEC],
        [IMAGE, IMAGE, whole(16, 4, 2, PIECE, C), whole(8, C)],
        [big(BF16), big(F32), struct((16, 4, 2, PIECE, C), BF16), struct((8, C), F32)],
        [maps, full, low, lowt, low, low, low, low, lowt, lowt, lowt, lowt, lowt,
         low, low, low, low, full, pltpu.VMEM((4, C, C), F32), SEMS],
        (ids, weight, live, chunk_attn, r1, cotangent, vectors), "attention", 80 * 10**9,
    )
    (early,) = call(
        two_taps, count, [IMAGE, IMAGE, whole(16, 4, 2, PIECE, C)],
        [whole(16, 13, 2, PIECE, C)], [struct((16, 13, 2, PIECE, C), BF16)],
        [slabs, turned], (dr1, a2, grads_attn), "second_conv_taps",
    )
    grads_early = plan.reduce_early(early)
    dr1, _ = lax.optimization_barrier((dr1, early))
    emb_rows = jnp.broadcast_to(emb[:, None, :], (count, 8, EMB))
    dh1, dvec, demb, sums_two = call(
        bwd_two_data, count,
        [SMEM] + PARTS + [IMAGE, IMAGE, per_image(8, C), VEC, per_image(8, EMB)],
        [IMAGE, per_image(8, C), per_image(8, EMB), whole(8, C)],
        [big(BF16), struct((count, 8, C), F32), struct((count, 8, EMB), F32), struct((8, C), F32)],
        [taps, maps, slab, full, SEMS, SEMS],
        (ids, *chunk_two, dr1, nhat, stats, vectors, emb_rows), "second_conv_back",
    )
    late = call(
        one_taps, count, [SMEM, IMAGE, IMAGE], [whole(4, 4, 9, PIECE, C)] * 2,
        [struct((4, 4, 9, PIECE, C), BF16)] * 2,
        [slabs, turned], (ids, dh1, a1), "first_conv_taps",
    )
    planes = plan.reduce_core(*late)
    dh1, _ = lax.optimization_barrier((dh1, planes))
    dx, sums_one = call(
        bwd_one_data, count, [SMEM] + PARTS + [IMAGE, IMAGE, IMAGE, VEC], [IMAGE, whole(8, C)],
        [big(F32), struct((8, C), F32)],
        [taps, slab, full, SEMS],
        (ids, *chunk_one, dh1, images, dr1, vectors), "first_conv_back",
    )
    grads_late = plan.reduce_late(planes, dx)
    grads = plan.finish_early(grads_late, grads_early)
    map_terms = jnp.concatenate([act.astype(F32), dvec[:, 0], dvec[:, 1]], axis=1).astype(BF16)
    grad_vectors = jnp.concatenate([sums_one[:2], sums_two[:6], sums_attn[:5]], axis=0)
    return out, dx, demb[:, 0], grads, map_terms, grad_vectors


def split_two(value):
    high = value.astype(BF16)
    return high, (value - high.astype(F32)).astype(BF16)


def mm_two(dot, a, b):
    return dot(a[0], b[0]) + (dot(a[0], b[1]) + dot(a[1], b[0]))


def rotated_adam(block, rate, got, terms, left, right, first, second, master, *refs):
    new_first, new_second, new_master, low, grad = refs
    slot = pl.program_id(0)
    held = block[slot]
    for n in range(PIECES):
        place = flat_place(n) * PIECE
        grad[place : place + PIECE] = got[n, rows_of(slot, PIECE), :]

    @pl.when((held >= 18) & (held < 22))
    def _():
        acts = terms[(held - 18) % 2]
        sides = terms[2 + (held - 18) // 2]
        grad[...] = mm(acts.astype(F32).T.astype(BF16), sides).astype(BF16)

    lefts = split_two(left[0])
    rights = split_two(right[0])
    g = grad[...]
    turned = split_two(mm(g, rights[0]) + mm(g, rights[1]))
    rotated = mm_two(mm, (lefts[0].T, lefts[1].T), turned)
    moment = MOMENT_DECAY * first[0] + (1.0 - MOMENT_DECAY) * rotated
    square = MOMENT_DECAY * second[0] + (1.0 - MOMENT_DECAY) * rotated * rotated
    new_first[0] = moment
    new_second[0] = square
    correction = 1.0 - MOMENT_DECAY**STEP
    direction = split_two(
        moment * (1.0 / correction) / (jnp.sqrt(square * (1.0 / correction)) + ADAM_EPS)
    )
    update = mm_two(mm, lefts, split_two(mm_two(mm_t, direction, rights)))
    fresh = master[0] - rate[slot] * (update + WEIGHT_DECAY * master[0])
    new_master[0] = fresh
    low[0] = fresh.astype(BF16)


def optimize(slot_block, rate, got, terms, state):
    count = state[0].shape[0]
    matrix = per_image(C, C)
    full = struct((count, C, C), F32)
    return call(
        rotated_adam, count,
        [SMEM, SMEM, whole(*got.shape), whole(*terms.shape)] + [matrix] * 5,
        [matrix] * 4, [full, full, full, struct((count, C, C), BF16)],
        [pltpu.VMEM((C, C), BF16)], (slot_block, rate, got, terms, *state), "rotated_adam",
    )


AXES = ("rep", "shard")


def swap(value, mask):
    return lax.ppermute(value, AXES, [(i, i ^ mask) for i in range(PIECES)])


def plane_mask(step):
    return (step // 2) * 16 + (step % 2) * 2


def gather_line(piece):
    return jnp.stack([piece] + [swap(piece, 4 * k) for k in (1, 2, 3)])


def gather_first(line):
    split = (line.shape[1] + 1) // 2
    halves = line[:, :split], line[:, split:]
    return [jnp.stack([half, swap(half, mask)]) for half, mask in zip(halves, (16, 2))]


def gather_second(firsts):
    seconds = [swap(first, mask) for first, mask in zip(firsts, (2, 16))]
    return [firsts[0], seconds[0], firsts[1], seconds[1]]


def gather_plane(line):
    line = line[None]
    return [line] + [swap(line, mask) for mask in (2, 16, 18)]


def gather_core(plane):
    return plane + [swap(part, 1) for part in plane]


def add_up(*terms):
    total = terms[0].astype(F32)
    for term in terms[1:]:
        total = total + term.astype(F32)
    return total.astype(BF16)


def block_slots(owner, mats_all):
    block_ids = jnp.arange(mats_all, dtype=jnp.int32)
    return jnp.sum(
        jnp.where(owner[None, :] == block_ids[:, None], block_ids[None, :], 0), axis=1
    )


def pick_slots(grads, slots):
    index = jnp.where(slots < 18, slots, jnp.clip(slots - 4, 0, 21))
    held = (slots < 18) | ((slots >= 22) & (slots < BLOCKS))
    picked = jnp.take(grads, index, axis=0)
    return jnp.where(held.reshape((-1,) + (1,) * (grads.ndim - 1)), picked, jnp.zeros((), BF16))


class Split:
    def __init__(self):
        self.rep = lax.axis_index("rep")
        shard = lax.axis_index("shard")
        self.ids = jnp.stack([shard % 2, self.rep * 2 + shard // 2 % 2, shard // 4])

    def gather(self, master, vec_master, owner):
        mat_dev = master.shape[0]
        rows = master.astype(BF16).reshape(mat_dev, 2, 2, 2, 4, PIECE, C)
        rows = lax.dynamic_index_in_dim(rows, self.rep, 2, keepdims=False)
        rows = rows.transpose(3, 2, 1, 0, 4, 5).reshape(16, mat_dev, PIECE, C)
        slots = lax.all_to_all(rows, "shard", 0, 0).reshape(16 * mat_dev, PIECE, C)
        blocks = jnp.take(slots, owner[:BLOCKS], axis=0)
        width = vec_master.shape[1]
        vec = jnp.pad(vec_master.astype(BF16), ((0, 16 - VECS), (0, C - width)))
        place = lax.axis_index("shard") * width
        vec = jnp.where(self.rep == 0, jnp.roll(vec, place, axis=1), jnp.zeros((), BF16))
        line_one = gather_line(jnp.concatenate([blocks[:9], vec[None]], axis=0))
        second, line_one = lax.optimization_barrier((blocks[9:22], line_one))
        first_one = gather_first(line_one)
        line_two = gather_line(second)
        planes_one = gather_second(first_one)
        line_two, attn, planes_one = lax.optimization_barrier((line_two, blocks[22:26], planes_one))
        one = gather_core(planes_one)
        return one, gather_plane(line_two), lax.all_gather(attn, AXES)

    def gather_core(self, planes):
        return gather_core(planes)

    def reduce_early(self, grads):
        return lax.psum_scatter(grads, "shard", scatter_dimension=0, tiled=True)[0]

    def finish_early(self, late, *early):
        own = jnp.concatenate(early, axis=0)
        mine = lax.dynamic_index_in_dim(own, self.rep, 1, keepdims=False)
        other = lax.dynamic_index_in_dim(own, 1 - self.rep, 1, keepdims=False)
        return jnp.concatenate([late, add_up(mine, swap(other, 16))], axis=0)

    def reduce_core(self, keep, send):
        other = swap(send, 1)
        return [add_up(keep[k], other[k]) for k in range(4)]

    def reduce_late(self, planes, after):
        line = [swap(planes[k], plane_mask(k)) for k in (1, 2, 3)]
        lines = [add_up(planes[0][j], *[part[j] for part in line]) for j in range(4)]
        lines, _ = lax.optimization_barrier((lines, after))
        return add_up(lines[0], *[swap(lines[k], 4 * k) for k in (1, 2, 3)])

    def own(self, grads, slots, mat_dev, map_terms, grad_vectors):
        picked = pick_slots(grads, slots).reshape(16, mat_dev * PIECE, C)
        terms = jnp.broadcast_to(map_terms.reshape(1, -1, C), (16, map_terms.size // C, C))
        width = C // 16
        vec = grad_vectors.astype(BF16).reshape(VECS, 16, width).transpose(1, 0, 2)
        vec = jnp.pad(vec.reshape(16, 1, VECS * width), ((0, 0), (0, 0), (0, C - VECS * width)))
        sent = jnp.concatenate([picked, terms, vec], axis=1)
        got = lax.all_to_all(jnp.concatenate([sent, sent]), AXES, 0, 0)
        split = mat_dev * PIECE
        terms = got[:, split:-1].reshape(-1, 4, C).transpose(1, 0, 2)
        vec = jnp.sum(got[:, -1, : VECS * width].astype(F32), axis=0)
        return got, terms, vec.reshape(VECS, width)


class Plain:
    def __init__(self):
        self.ids = jnp.zeros((3,), jnp.int32)

    def gather(self, master, vec_master, owner):
        slots = lax.all_gather(master.astype(BF16), "shard", axis=0, tiled=True)
        vec = lax.all_gather(vec_master.astype(BF16), "shard", axis=1, tiled=True)
        blocks = jnp.take(slots, owner[:BLOCKS], axis=0)

        def parts(some):
            split = (some.shape[0] + 1) // 2
            pieces = some.reshape(-1, 2, 4, 4, PIECE, C).transpose(1, 2, 3, 0, 4, 5)
            halves = (slice(0, split), slice(split, None))
            return [
                jnp.stack([pieces[core, plane][:, halves[n // 2]] for plane in planes])
                for core in range(2)
                for n, (planes, _) in enumerate(HALVED)
            ]

        rows = jnp.zeros((C, C), BF16).at[:VECS].set(vec)
        one = parts(jnp.concatenate([blocks[:9], rows[None]], axis=0))
        flat = blocks[22:26].reshape(4, 2, 2, 2, 4, PIECE, C).transpose(2, 4, 3, 1, 0, 5, 6)
        return one, parts(blocks[9:22]), flat.reshape(PIECES, 4, PIECE, C)

    def gather_core(self, planes):
        return planes

    def reduce_early(self, grads):
        split = grads.reshape(4, 2, 2, -1, 2, PIECE, C).transpose(3, 2, 4, 1, 0, 5, 6)
        return split.reshape(-1, C, C)

    def finish_early(self, late, *early):
        return jnp.concatenate([late, *early], axis=0)

    def reduce_core(self, keep, send):
        return [jnp.stack([keep, send]).transpose(3, 0, 1, 2, 4, 5).reshape(-1, C, C)]

    def reduce_late(self, planes, after):
        return planes[0]

    def own(self, grads, slots, mat_dev, map_terms, grad_vectors):
        picked = pick_slots(grads, slots)
        mine = lax.psum_scatter(picked, "shard", scatter_dimension=0, tiled=True)
        rows = lax.psum(mine, "rep").reshape(mat_dev, 2, 2, 2, 4, PIECE, C)
        got = rows.transpose(2, 4, 3, 1, 0, 5, 6).reshape(PIECES, mat_dev * PIECE, C)
        terms = lax.all_gather(map_terms, AXES, axis=0, tiled=True)
        terms = terms.reshape(-1, 4, C).transpose(1, 0, 2)
        vec = lax.psum_scatter(grad_vectors, "shard", scatter_dimension=1, tiled=True)
        return got, terms, lax.psum(vec, "rep")


def shards(
    images,
    embeds,
    cotangent,
    counts,
    bucket_weight,
    owner,
    master,
    first_moment,
    second_moment,
    left_basis,
    right_basis,
    vec_master,
    vec_first,
    vec_second,
):
    mat_dev = master.shape[0]
    mats_all = mat_dev * lax.axis_size("shard")
    sizes = (lax.axis_size("rep"), lax.axis_size("shard"))
    plan = Split() if sizes == (2, 16) else Plain()
    gathered = plan.gather(master, vec_master, owner)
    slot_ids = jnp.arange(images.shape[0], dtype=jnp.int32)
    live = (slot_ids < counts[0, 0] + counts[0, 1]).astype(jnp.int32)
    weight = jnp.where(slot_ids < counts[0, 0], bucket_weight[0], bucket_weight[1])
    weight = jnp.where(live > 0, weight, 0.0)
    outputs, grad_images, grad_embeds, grads, map_terms, grad_vectors = layer(
        images, embeds, cotangent, weight, live, plan, gathered
    )
    all_slots = block_slots(owner, mats_all)
    shard = lax.axis_index("shard")
    slot_block = lax.dynamic_slice_in_dim(all_slots, shard * mat_dev, mat_dev, 0)
    got, terms, own_vec = plan.own(grads, all_slots, mat_dev, map_terms, grad_vectors)
    step_rate = jnp.where(slot_block < BLOCKS, 2.0 * block_spread(slot_block), 0.0)
    new_first, new_second, new_master, master_low = optimize(
        slot_block,
        step_rate,
        got,
        terms,
        (left_basis, right_basis, first_moment, second_moment, master),
    )
    correction = 1.0 - MOMENT_DECAY**STEP
    vec_first_new = MOMENT_DECAY * vec_first + (1.0 - MOMENT_DECAY) * own_vec
    vec_second_new = MOMENT_DECAY * vec_second + (1.0 - MOMENT_DECAY) * own_vec * own_vec
    vec_master_new = vec_master - VECTOR_RATE * (vec_first_new / correction) / (
        jnp.sqrt(vec_second_new / correction) + ADAM_EPS
    )
    return (
        outputs,
        grad_images,
        grad_embeds,
        new_first,
        new_second,
        new_master,
        master_low,
        vec_first_new,
        vec_second_new,
        vec_master_new,
        vec_master_new.astype(jnp.bfloat16),
    )


def solution(mesh):
    return jax.shard_map(
        shards,
        mesh=mesh,
        in_specs=(
            P(("rep", "shard"), None, None),
            P(("rep", "shard"), None),
            P(("rep", "shard"), None, None),
            P(("rep", "shard"), None),
            P(),
            P(),
            P("shard", None, None),
            P("shard", None, None),
            P("shard", None, None),
            P("shard", None, None),
            P("shard", None, None),
            P(None, "shard"),
            P(None, "shard"),
            P(None, "shard"),
        ),
        out_specs=(
            P(("rep", "shard"), None, None),
            P(("rep", "shard"), None, None),
            P(("rep", "shard"), None),
            P("shard", None, None),
            P("shard", None, None),
            P("shard", None, None),
            P("shard", None, None),
            P(None, "shard"),
            P(None, "shard"),
            P(None, "shard"),
            P(None, "shard"),
        ),
        check_vma=False,
    )
```

```python
import functools
import math

import jax
import jax.numpy as jnp
from jax import lax
from jax.experimental import pallas as pl
from jax.experimental.pallas import tpu as pltpu
from jax.sharding import PartitionSpec as P

C = 512
EMB = 1024
HEADS = 8
HEAD = 64
GROUPS = 32
SIDE = 32
HW = 1024
BLOCKS = 26
VECS = 13
STEP = 2
PAD = SIDE
SLAB = HW + 2 * PAD
ROWS = 128
QROWS = 256

EPS_NORM = 1e-05
ADAM_EPS = 1e-08
MOMENT_DECAY = 0.5
WEIGHT_DECAY = 0.01
VECTOR_RATE = 0.2
PRECISE = lax.Precision.HIGHEST
F32 = jnp.float32
BF16 = jnp.bfloat16
ANY = pl.BlockSpec(memory_space=pl.ANY)
SMEM = pl.BlockSpec(memory_space=pltpu.SMEM)
VMEM = pl.BlockSpec(memory_space=pltpu.VMEM)
VMEM_LIMIT = 56 * 2**20


def block_spread(block_index):
    return jnp.where(
        block_index < 18,
        (9.0 * C) ** (-0.5),
        jnp.where(
            block_index < 22,
            EMB ** (-0.5),
            jnp.where(
                block_index < 24,
                1.25 * C ** (-0.5),
                jnp.where(
                    block_index < 25,
                    C ** (-0.5),
                    jnp.where(block_index < 26, 0.295 * (HW / C) ** 0.5, C ** (-0.5)),
                ),
            ),
        ),
    )


def mm(a, b):
    return jnp.dot(a, b, preferred_element_type=F32)


def mm_t(a, b):
    return lax.dot_general(a, b, (((1,), (1,)), ((), ())), preferred_element_type=F32)


def sigmoid(u):
    return 1.0 / (1.0 + jnp.exp(-u))


def silu_slope(u):
    s = sigmoid(u)
    return s * (1.0 + u * (1.0 - s))


def chunks(count, body, init=0):
    return lax.fori_loop(0, count, body, init)


def rows_of(index, size):
    return pl.ds(pl.multiple_of(index * size, size), size)


def group_mean(column_sum):
    total = jnp.broadcast_to(column_sum, (8, C))
    lane = lax.broadcasted_iota(jnp.int32, (8, C), 1)
    for step in (1, 2, 4, 8):
        other = jnp.where(
            (lane & step) != 0, pltpu.roll(total, step, 1), pltpu.roll(total, C - step, 1)
        )
        total = total + other
    return total[0:1] * (1.0 / (HW * (C // GROUPS)))


def norm_stats(read):
    zero = jnp.zeros((1, C), F32)
    total = chunks(
        HW // ROWS,
        lambda c, t: t + jnp.sum(read(rows_of(c, ROWS)), axis=0, keepdims=True),
        zero,
    )
    mean = group_mean(total)

    def squares(c, t):
        centered = read(rows_of(c, ROWS)) - mean
        return t + jnp.sum(centered * centered, axis=0, keepdims=True)

    var = group_mean(chunks(HW // ROWS, squares, zero))
    return mean, lax.rsqrt(var + EPS_NORM)


def clear_pads(slab):
    zeros = jnp.zeros((PAD, C), BF16)
    for lead in slab_leads(slab):
        slab[lead + (pl.ds(0, PAD), slice(None))] = zeros
        slab[lead + (pl.ds(PAD + HW, PAD), slice(None))] = zeros


def slab_leads(slab):
    if len(slab.shape) == 3:
        return [(j,) for j in range(3)]
    return [(i, j) for i in range(slab.shape[0]) for j in range(3)]


def store_slab(slab, lead, c, chunk):
    column = lax.broadcasted_iota(jnp.int32, (ROWS, C), 0) & (SIDE - 1)
    before = jnp.where(column == 0, 0.0, pltpu.roll(chunk, 1, 0))
    after = jnp.where(column == SIDE - 1, 0.0, pltpu.roll(chunk, ROWS - 1, 0))
    rows = pl.ds(pl.multiple_of(c * ROWS + PAD, PAD), ROWS)
    slab[lead + (0, rows, slice(None))] = before.astype(BF16)
    slab[lead + (1, rows, slice(None))] = chunk.astype(BF16)
    slab[lead + (2, rows, slice(None))] = after.astype(BF16)


def conv_rows(slab, lead, weights, base, size, back):
    total = None
    for tap in range(9):
        di, dj = tap // 3, tap % 3
        if back:
            di, dj = 2 - di, 2 - dj
        rows = pl.ds(pl.multiple_of(base + di * SIDE, SIDE), size)
        piece = slab[lead + (dj, rows, slice(None))]
        term = (mm_t if back else mm)(piece, weights[tap])
        total = term if total is None else total + term
    return total


CONV_ROWS = 1024


PIECES = 32
PIECE = C // PIECES


def piece_rows(ids, core, plane, line):
    index = ((ids[0] ^ core) * 4 + (ids[1] ^ plane)) * 4 + (ids[2] ^ line)
    return pl.ds(pl.multiple_of(index * PIECE, PIECE), PIECE)


DIRECT = (((0,), 0), ((1,), 0), ((2,), 0), ((3,), 0))
HALVED = (((0, 2), 0), ((1, 3), 0), ((0, 1), 1), ((2, 3), 1))
COPIES = 64


def flat_place(n):
    return (n % 2 * 4 + n // 16 * 2 + n // 2 % 2) * 4 + n // 4 % 4


def block_copies(ids, parts, dest, sem, first, count):
    if len(parts) == 1:
        return [
            pltpu.make_async_copy(
                parts[0].at[n, pl.ds(first, count)],
                dest.at[:, pl.ds(flat_place(n) * PIECE, PIECE), :],
                sem.at[n],
            )
            for n in range(PIECES)
        ]
    copies = []
    layout = HALVED if parts[0].shape[0] == 2 else DIRECT
    for n, part in enumerate(parts):
        planes, half = layout[n % 4]
        start = half * parts[0].shape[2]
        low, high = max(first, start), min(first + count, start + part.shape[2])
        if low >= high:
            continue
        for side, plane in enumerate(planes):
            for line in range(4):
                rows = piece_rows(ids, n // 4, plane, line)
                copies.append(
                    pltpu.make_async_copy(
                        part.at[side, line, pl.ds(low - start, high - low)],
                        dest.at[pl.ds(low - first, high - low), rows, :],
                        sem.at[len(copies)],
                    )
                )
    return copies


def start_all(*args):
    for copy in block_copies(*args):
        copy.start()


def wait_all(*args):
    for copy in block_copies(*args):
        copy.wait()


def store_flat(out, slot, grad):
    for n in range(PIECES):
        place = flat_place(n) * PIECE
        out[slot, n % 16, n // 16] = grad[place : place + PIECE]


def store_pieces(ids, keep, send, block, grad):
    half = C // 2
    mine = ids[0] == 0
    kept = jnp.where(mine, grad[:half], grad[half:])
    sent = jnp.where(mine, grad[half:], grad[:half])
    for plane in range(4):
        for line in range(4):
            rows = slice((plane * 4 + line) * PIECE, (plane * 4 + line + 1) * PIECE)
            keep[plane ^ ids[1], line ^ ids[2], block] = kept[rows]
            send[plane ^ ids[1], line ^ ids[2], block] = sent[rows]


def fwd_one(ids, *refs):
    parts, (x, h1, a1, vec, weights, slab, held, sem, vec_sem) = refs[:8], refs[8:]
    step = pl.program_id(0)

    def vec_copies():
        last = [part for n, part in enumerate(parts) if n % 4 > 1]
        return [
            pltpu.make_async_copy(part.at[:, :, part.shape[2] - 1], held.at[n], vec_sem.at[n])
            for n, part in enumerate(last)
        ]

    @pl.when(step == 0)
    def _():
        for copy in vec_copies():
            copy.start()
        start_all(ids, parts, weights, sem, 0, 9)
        clear_pads(slab)

    def read(rows):
        return x[0, rows, :].astype(F32)

    mean, inv = norm_stats(read)

    @pl.when(step == 0)
    def _():
        for copy in vec_copies():
            copy.wait()
        total = jnp.zeros((16, C), F32)
        for n in range(PIECES):
            total = total + held[n // 8, n // 4 % 2, n % 4].astype(F32)
        vec[...] = total

    gain = inv * vec[0:1]
    bias = vec[1:2]

    def activate(c, _):
        rows = rows_of(c, ROWS)
        pre = (read(rows) - mean) * gain + bias
        act = pre * sigmoid(pre)
        a1[0, rows, :] = act.astype(BF16)
        store_slab(slab, (), c, act)
        return 0

    chunks(HW // ROWS, activate)

    @pl.when(step == 0)
    def _():
        wait_all(ids, parts, weights, sem, 0, 9)

    def conv(c, _):
        h1[0, rows_of(c, CONV_ROWS), :] = (
            conv_rows(slab, (), weights, c * CONV_ROWS, CONV_ROWS, False) + vec[2:3]
        )
        return 0

    chunks(HW // CONV_ROWS, conv)


def fwd_two(ids, *refs):
    parts = refs[:8]
    h1, x, act, vec, a2, r1, nhat, stats, weights, maps, slab, sem, map_sem = refs[8:]
    step = pl.program_id(0)

    @pl.when(step == 0)
    def _():
        start_all(ids, parts, maps, map_sem, 9, 4)
        start_all(ids, parts, weights, sem, 0, 9)
        clear_pads(slab)

    mean, inv = norm_stats(lambda rows: h1[0, rows, :])

    @pl.when(step == 0)
    def _():
        wait_all(ids, parts, maps, map_sem, 9, 4)

    row = act[0]
    scale = (mm(row[:, :C], maps[0]) + mm(row[:, C:], maps[1]))[0:1] + vec[3:4]
    shift = (mm(row[:, :C], maps[2]) + mm(row[:, C:], maps[3]))[0:1] + vec[4:5]
    stats[0] = jnp.concatenate([scale, shift, inv, jnp.zeros((5, C), F32)], axis=0)
    gain = vec[5:6]
    bias = vec[6:7]

    def activate(c, _):
        rows = rows_of(c, ROWS)
        normed = (h1[0, rows, :] - mean) * inv
        nhat[0, rows, :] = normed
        pre = (normed * gain + bias) * (1.0 + scale) + shift
        act_two = pre * sigmoid(pre)
        a2[0, rows, :] = act_two.astype(BF16)
        store_slab(slab, (), c, act_two)
        return 0

    chunks(HW // ROWS, activate)

    @pl.when(step == 0)
    def _():
        wait_all(ids, parts, weights, sem, 0, 9)

    def conv(c, _):
        rows = rows_of(c, CONV_ROWS)
        hidden = conv_rows(slab, (), weights, c * CONV_ROWS, CONV_ROWS, False) + vec[7:8]
        r1[0, rows, :] = x[0, rows, :].astype(F32) + hidden
        return 0

    chunks(HW // CONV_ROWS, conv)


MM_ROWS = 512


def attention(ids, weight, live, *refs):
    parts = refs[:1]
    (
    r1, cot, vec, out, dr1, grads, sums, weights,
    nhat, n3, n3t, q, k, v, da, dat, qt, kt, vt, att, dyb, dq, dk, dv, dn3, acc, sem, flat, flat_sem,
    ) = refs[1:]
    step = pl.program_id(0)

    def out_copy(n):
        return pltpu.make_async_copy(flat.at[n], grads.at[:, 9 + n], flat_sem.at[n])

    @pl.when(step == 0)
    def _():
        start_all(ids, parts, weights, sem, 0, 4)
        sums[...] = jnp.zeros((8, C), F32)

    mean, inv = norm_stats(lambda rows: r1[0, rows, :])
    gain = vec[8:9]
    bias = vec[9:10]
    image_weight = weight[step]

    def normalize(c, total):
        rows = rows_of(c, ROWS)
        normed = (r1[0, rows, :] - mean) * inv
        nhat[rows, :] = normed
        n3[rows, :] = (normed * gain + bias).astype(BF16)
        low = (cot[0, rows, :].astype(F32) * image_weight).astype(BF16)
        dyb[rows, :] = low
        return total + jnp.sum(low.astype(F32), axis=0, keepdims=True)

    zero = jnp.zeros((1, C), F32)
    sum_dy = chunks(HW // ROWS, normalize, zero)

    @pl.when(step == 0)
    def _():
        wait_all(ids, parts, weights, sem, 0, 4)

    def project(c, _):
        rows = rows_of(c, MM_ROWS)
        normed = n3[rows, :]
        q[rows, :] = (mm(normed, weights[0]) + vec[10:11]).astype(BF16) * 0.125
        k[rows, :] = mm(normed, weights[1]).astype(BF16)
        v[rows, :] = (mm(normed, weights[2]) + vec[11:12]).astype(BF16)
        da[rows, :] = mm_t(dyb[rows, :], weights[3]).astype(BF16)
        return 0

    chunks(HW // MM_ROWS, project)
    n3t[...] = n3[...].T
    qt[...] = q[...].T
    kt[...] = k[...].T
    vt[...] = v[...].T
    dat[...] = da[...].T

    def head_pair(pair, _):
        cols = pl.ds(pl.multiple_of(pair * 128, 128), 128)
        first = lax.broadcasted_iota(jnp.int32, (HW, 128), 1) < HEAD

        def one_head(value, side):
            blank = jnp.zeros_like(value)
            return jnp.where(first, value, blank) if side == 0 else jnp.where(first, blank, value)

        keys, values = k[:, cols], v[:, cols]
        expos, scaled, dots = [], [], []
        for side in range(2):
            head_rows = pl.ds(pl.multiple_of(pair * 128 + side * HEAD, HEAD), HEAD)
            scores = mm(one_head(keys, side), qt[cols, :])
            expo = jnp.exp(scores - jnp.max(scores, axis=0, keepdims=True))
            inverse = 1.0 / jnp.sum(expo, axis=0, keepdims=True)
            expos.append(expo.astype(BF16))
            attended = mm(vt[head_rows, :], expos[side]) * inverse
            att[head_rows, :] = attended.astype(BF16)
            scaled.append((dat[head_rows, :].astype(F32) * inverse).astype(BF16))
            dots.append(jnp.sum(attended * scaled[side].astype(F32), axis=0, keepdims=True))
        both = jnp.concatenate(scaled, axis=0)
        turned = both.T
        dks, dvs = [], []
        for side in range(2):
            head_rows = pl.ds(pl.multiple_of(pair * 128 + side * HEAD, HEAD), HEAD)
            dprobs = mm(one_head(values, side), both)
            dscores = (expos[side].astype(F32) * (dprobs - dots[side])).astype(BF16)
            dvs.append(mm(expos[side], turned))
            dks.append(mm(dscores, q[:, cols]))
            dat[head_rows, :] = (mm(kt[head_rows, :], dscores) * 0.125).astype(BF16)
        dk[:, cols] = jnp.where(first, dks[0], dks[1]).astype(BF16)
        dv[:, cols] = jnp.where(first, dvs[0], dvs[1]).astype(BF16)
        return 0

    chunks(HEADS // 2, head_pair)
    dq[...] = dat[...].T
    q[...] = att[...].T

    is_live = live[step] > 0

    def result(c, _):
        rows = rows_of(c, MM_ROWS)
        y = r1[0, rows, :] + mm(q[rows, :], weights[3]) + vec[12:13]
        out[0, rows, :] = jnp.where(is_live, y, 0.0).astype(BF16)
        dn3[rows, :] = (
            mm_t(dq[rows, :], weights[0])
            + mm_t(dk[rows, :], weights[1])
            + mm_t(dv[rows, :], weights[2])
        )
        return 0

    chunks(HW // MM_ROWS, result)

    terms = (
        lambda: mm(n3t[...], dq[...]),
        lambda: mm(n3t[...], dk[...]),
        lambda: mm(n3t[...], dv[...]),
        lambda: mm(att[...], dyb[...]),
    )
    for n, term in enumerate(terms):
        @pl.when(step == 0)
        def _(n=n, term=term):
            acc[n] = term()

        @pl.when(step != 0)
        def _(n=n, term=term):
            store_flat(flat, n, (acc[n] + term()).astype(BF16))
            out_copy(n).start()

    def column_sums(c, totals):
        rows = rows_of(c, ROWS)
        grad = dn3[rows, :]
        new = (
            grad * nhat[rows, :],
            grad,
            dq[rows, :].astype(F32),
            dv[rows, :].astype(F32),
        )
        return tuple(t + jnp.sum(n, axis=0, keepdims=True) for t, n in zip(totals, new))

    sum_cross, sum_grad, sum_q, sum_v = chunks(HW // ROWS, column_sums, (zero,) * 4)
    sums[...] += jnp.concatenate(
        [sum_cross, sum_grad, sum_q, sum_v, sum_dy, jnp.zeros((3, C), F32)], axis=0
    )
    mean_grad = group_mean(gain * sum_grad)
    mean_cross = group_mean(gain * sum_cross)

    def back(c, _):
        rows = rows_of(c, ROWS)
        inner = gain * dn3[rows, :] - mean_grad - nhat[rows, :] * mean_cross
        dr1[0, rows, :] = cot[0, rows, :].astype(F32) * image_weight + inv * inner
        return 0

    chunks(HW // ROWS, back)

    @pl.when(step != 0)
    def _():
        for n in range(4):
            out_copy(n).wait()


def split_three(value):
    high = value.astype(BF16)
    rest = value - high.astype(F32)
    middle = rest.astype(BF16)
    return high, middle, (rest - middle.astype(F32)).astype(BF16)


def bwd_two_data(ids, *refs):
    parts = refs[:8]
    dr1, nhat, stats, vec, emb, dh1, dvec, demb, sums = refs[8:17]
    weights, maps, slab, dz, sem, map_sem = refs[17:]
    step = pl.program_id(0)

    @pl.when(step == 0)
    def _():
        start_all(ids, parts, weights, sem, 0, 9)
        start_all(ids, parts, maps, map_sem, 9, 4)
        clear_pads(slab)
        sums[...] = jnp.zeros((8, C), F32)

    zero = jnp.zeros((1, C), F32)

    def fill(c, total):
        chunk = dr1[0, rows_of(c, ROWS), :]
        store_slab(slab, (), c, chunk)
        return total + jnp.sum(chunk.astype(BF16).astype(F32), axis=0, keepdims=True)

    sum_h2 = chunks(HW // ROWS, fill, zero)

    @pl.when(step == 0)
    def _():
        wait_all(ids, parts, weights, sem, 0, 9)
        wait_all(ids, parts, maps, map_sem, 9, 4)

    scale = 1.0 + stats[0, 0:1]
    shift = stats[0, 1:2]
    inv = stats[0, 2:3]
    gain = vec[5:6]
    bias = vec[6:7]

    def conv(c, _):
        dz[rows_of(c, CONV_ROWS), :] = conv_rows(
            slab, (), weights, c * CONV_ROWS, CONV_ROWS, True
        )
        return 0

    chunks(HW // CONV_ROWS, conv)

    def slope(c, totals):
        rows = rows_of(c, ROWS)
        normed = nhat[0, rows, :]
        pre = (normed * gain + bias) * scale + shift
        grad = dz[rows, :] * silu_slope(pre)
        dz[rows, :] = grad
        return (
            totals[0] + jnp.sum(grad, axis=0, keepdims=True),
            totals[1] + jnp.sum(grad * normed, axis=0, keepdims=True),
        )

    sum_dz, sum_cross = chunks(HW // ROWS, slope, (zero, zero))
    factor = scale * gain
    mean_grad = group_mean(factor * sum_dz)
    mean_cross = group_mean(factor * sum_cross)

    def back(c, total):
        rows = rows_of(c, ROWS)
        low = (inv * (factor * dz[rows, :] - mean_grad - nhat[0, rows, :] * mean_cross)).astype(BF16)
        dh1[0, rows, :] = low
        return total + jnp.sum(low.astype(F32), axis=0, keepdims=True)

    sum_h1 = chunks(HW // ROWS, back, zero)
    dscale = gain * sum_cross + bias * sum_dz
    sums[...] += jnp.concatenate(
        [sum_h1, dscale, sum_dz, scale * sum_cross, scale * sum_dz, sum_h2, jnp.zeros((2, C), F32)],
        axis=0,
    )
    pieces_scale = split_three(dscale)
    pieces_shift = split_three(sum_dz)
    blank = jnp.zeros((5, C), F32)

    def stack(pieces):
        return jnp.concatenate([p.astype(F32) for p in pieces] + [blank], axis=0).astype(BF16)

    d_scale = stack(pieces_scale)
    d_shift = stack(pieces_shift)

    def reach(upper):
        parts = mm_t(d_scale, maps[upper]) + mm_t(d_shift, maps[2 + upper])
        return jnp.sum(parts, axis=0, keepdims=True)

    row = jnp.concatenate([reach(0), reach(1)], axis=1)
    demb[0] = jnp.broadcast_to(row * silu_slope(emb[0, 0:1].astype(F32)), (8, EMB))
    dvec[0] = jnp.concatenate([dscale, sum_dz, jnp.zeros((6, C), F32)], axis=0)


def fill_taps(grad, act, slab, at):
    step = pl.program_id(0)

    @pl.when(step == 0)
    def _():
        clear_pads(slab)

    def fill(c, _):
        store_slab(slab, (step,), c, grad[0, rows_of(c, ROWS), :].astype(F32))
        return 0

    chunks(HW // ROWS, fill)
    at[step] = act[0].T


def tap_grad(slab, at, tap):
    di = 2 - tap // 3
    dj = tap // 3 * 3 + 2 - tap
    rows = pl.ds(pl.multiple_of(di * SIDE, SIDE), HW)
    total = mm(at[0], slab[0, dj, rows, :])
    for image in range(1, slab.shape[0]):
        total = total + mm(at[image], slab[image, dj, rows, :])
    return total.astype(BF16)


def one_taps(ids, grad, act, keep, send, slab, at):
    fill_taps(grad, act, slab, at)

    @pl.when(pl.program_id(0) == pl.num_programs(0) - 1)
    def _():
        def one(tap, _):
            store_pieces(ids, keep, send, tap, tap_grad(slab, at, tap))
            return 0

        for tap in range(9):
            one(tap, 0)


def two_taps(grad, act, others, out, slab, at, flat, sem):
    fill_taps(grad, act, slab, at)

    def out_copy(tap):
        return pltpu.make_async_copy(flat.at[tap % 2], out.at[:, tap], sem.at[tap % 2])

    @pl.when(pl.program_id(0) == pl.num_programs(0) - 1)
    def _():
        for tap in range(9):
            if tap > 1:
                out_copy(tap - 2).wait()
            store_flat(flat, tap % 2, tap_grad(slab, at, tap))
            out_copy(tap).start()
        out_copy(7).wait()
        out_copy(8).wait()


def bwd_one_data(ids, *refs):
    parts, (dh1, x, dr1, vec, dx, sums, weights, slab, dp, sem) = refs[:8], refs[8:]
    step = pl.program_id(0)

    @pl.when(step == 0)
    def _():
        start_all(ids, parts, weights, sem, 0, 9)
        clear_pads(slab)
        sums[...] = jnp.zeros((8, C), F32)

    def fill(c, _):
        store_slab(slab, (), c, dh1[0, rows_of(c, ROWS), :].astype(F32))
        return 0

    chunks(HW // ROWS, fill)

    def read(rows):
        return x[0, rows, :].astype(F32)

    mean, inv = norm_stats(read)
    gain = vec[0:1]
    bias = vec[1:2]

    @pl.when(step == 0)
    def _():
        wait_all(ids, parts, weights, sem, 0, 9)

    def conv(c, _):
        dp[rows_of(c, CONV_ROWS), :] = conv_rows(
            slab, (), weights, c * CONV_ROWS, CONV_ROWS, True
        )
        return 0

    chunks(HW // CONV_ROWS, conv)
    zero = jnp.zeros((1, C), F32)

    def slope(c, totals):
        rows = rows_of(c, ROWS)
        normed = (read(rows) - mean) * inv
        grad = dp[rows, :] * silu_slope(normed * gain + bias)
        dp[rows, :] = grad
        return (
            totals[0] + jnp.sum(grad * normed, axis=0, keepdims=True),
            totals[1] + jnp.sum(grad, axis=0, keepdims=True),
        )

    sum_cross, sum_grad = chunks(HW // ROWS, slope, (zero, zero))
    sums[...] += jnp.concatenate([sum_cross, sum_grad, jnp.zeros((6, C), F32)], axis=0)
    mean_grad = group_mean(gain * sum_grad)
    mean_cross = group_mean(gain * sum_cross)

    def back(c, _):
        rows = rows_of(c, ROWS)
        normed = (read(rows) - mean) * inv
        dx[0, rows, :] = dr1[0, rows, :] + inv * (
            gain * dp[rows, :] - mean_grad - normed * mean_cross
        )
        return 0

    chunks(HW // ROWS, back)


def per_image(*shape):
    return pl.BlockSpec((1,) + shape, lambda i: (i,) + (0,) * len(shape))


def whole(*shape):
    return pl.BlockSpec(shape, lambda i: (0,) * len(shape))


def struct(shape, kind):
    return jax.ShapeDtypeStruct(shape, kind)


def call(body, images, in_specs, out_specs, out_shape, scratch, args, name, flops=20 * 10**9, aliases=None):
    return pl.pallas_call(
        body,
        grid=(images,),
        in_specs=in_specs,
        out_specs=out_specs,
        out_shape=out_shape,
        scratch_shapes=scratch,
        input_output_aliases=aliases or {},
        name=name,
        compiler_params=pltpu.CompilerParams(
            vmem_limit_bytes=VMEM_LIMIT, dimension_semantics=("arbitrary",)
        ),
        cost_estimate=pl.CostEstimate(flops=flops, bytes_accessed=30 * 2**20, transcendentals=0),
    )(*args)


IMAGE = per_image(HW, C)
VEC = whole(16, C)
PARTS = [ANY] * 8
SEMS = pltpu.SemaphoreType.DMA((COPIES,))


def layer(images, emb, act, cotangent, weight, live, plan, gathered):
    chunk_one, planes_two, chunk_attn = gathered
    ids = plan.ids
    count = images.shape[0]
    big = lambda kind: struct((count, HW, C), kind)
    taps = pltpu.VMEM((9, C, C), BF16)
    maps = pltpu.VMEM((4, C, C), BF16)
    slab = pltpu.VMEM((3, SLAB, C), BF16)
    slabs = pltpu.VMEM((count, 3, SLAB, C), BF16)
    turned = pltpu.VMEM((count, C, HW), BF16)
    low = pltpu.VMEM((HW, C), BF16)
    lowt = pltpu.VMEM((C, HW), BF16)
    full = pltpu.VMEM((HW, C), F32)
    h1, a1, vectors = call(
        fwd_one, count, [SMEM] + PARTS + [IMAGE], [IMAGE, IMAGE, VEC],
        [big(F32), big(BF16), struct((16, C), F32)],
        [taps, slab, pltpu.VMEM((4, 2, 4, PIECE, C), BF16), SEMS, pltpu.SemaphoreType.DMA((4,))],
        (ids, *chunk_one, images), "first_conv",
    )
    planes_two, h1 = lax.optimization_barrier((planes_two, h1))
    chunk_two = plan.gather_core(planes_two)
    act_rows = jnp.broadcast_to(act[:, None, :], (count, 16, EMB))
    a2, r1, nhat, stats = call(
        fwd_two, count, [SMEM] + PARTS + [IMAGE, IMAGE, per_image(16, EMB), VEC],
        [IMAGE, IMAGE, IMAGE, per_image(8, C)],
        [big(BF16), big(F32), big(F32), struct((count, 8, C), F32)],
        [taps, maps, slab, SEMS, SEMS],
        (ids, *chunk_two, h1, images, act_rows, vectors), "second_conv",
    )
    early = struct((16, 13, 2, PIECE, C), BF16)
    out, dr1, grads_attn, sums_attn = call(
        attention, count, [SMEM, SMEM, SMEM, ANY] + [IMAGE, IMAGE, VEC],
        [IMAGE, IMAGE, ANY, whole(8, C)],
        [big(BF16), big(F32), early, struct((8, C), F32)],
        [maps, full, low, lowt, low, low, low, low, lowt, lowt, lowt, lowt, lowt,
         low, low, low, low, full, pltpu.VMEM((4, C, C), F32), SEMS,
         pltpu.VMEM((4, 16, 2, PIECE, C), BF16), pltpu.SemaphoreType.DMA((4,))],
        (ids, weight, live, chunk_attn, r1, cotangent, vectors), "attention", 80 * 10**9,
    )
    (early,) = call(
        two_taps, count, [IMAGE, IMAGE, ANY], [ANY], [early],
        [slabs, turned, pltpu.VMEM((2, 16, 2, PIECE, C), BF16), pltpu.SemaphoreType.DMA((2,))],
        (dr1, a2, grads_attn), "second_conv_taps", aliases={2: 0},
    )
    grads_early = plan.reduce_early(early)
    dr1, _ = lax.optimization_barrier((dr1, early))
    emb_rows = jnp.broadcast_to(emb[:, None, :], (count, 8, EMB))
    dh1, dvec, demb, sums_two = call(
        bwd_two_data, count,
        [SMEM] + PARTS + [IMAGE, IMAGE, per_image(8, C), VEC, per_image(8, EMB)],
        [IMAGE, per_image(8, C), per_image(8, EMB), whole(8, C)],
        [big(BF16), struct((count, 8, C), F32), struct((count, 8, EMB), F32), struct((8, C), F32)],
        [taps, maps, slab, full, SEMS, SEMS],
        (ids, *chunk_two, dr1, nhat, stats, vectors, emb_rows), "second_conv_back",
    )
    late = call(
        one_taps, count, [SMEM, IMAGE, IMAGE], [whole(4, 4, 9, PIECE, C)] * 2,
        [struct((4, 4, 9, PIECE, C), BF16)] * 2,
        [slabs, turned], (ids, dh1, a1), "first_conv_taps",
    )
    planes = plan.reduce_core(*late)
    dh1, _ = lax.optimization_barrier((dh1, planes))
    dx, sums_one = call(
        bwd_one_data, count, [SMEM] + PARTS + [IMAGE, IMAGE, IMAGE, VEC], [IMAGE, whole(8, C)],
        [big(F32), struct((8, C), F32)],
        [taps, slab, full, SEMS],
        (ids, *chunk_one, dh1, images, dr1, vectors), "first_conv_back",
    )
    grads_late = plan.reduce_late(planes, dx)
    grads = plan.finish_early(grads_late, grads_early)
    map_terms = dvec[:, :2].astype(BF16)
    grad_vectors = jnp.concatenate([sums_one[:2], sums_two[:6], sums_attn[:5]], axis=0)
    return out, dx, demb[:, 0], grads, map_terms, grad_vectors


def split_two(value):
    high = value.astype(BF16)
    return high, (value - high.astype(F32)).astype(BF16)


def mm_two(dot, a, b):
    return dot(a[0], b[0]) + (dot(a[0], b[1]) + dot(a[1], b[0]))


def rotated_adam(block, rate, got, terms, left, right, first, second, master, *refs):
    new_first, new_second, new_master, low, grad = refs
    slot = pl.program_id(0)
    held = block[slot]
    for n in range(PIECES):
        place = flat_place(n) * PIECE
        grad[place : place + PIECE] = got[n, rows_of(slot, PIECE), :]

    @pl.when((held >= 18) & (held < 22))
    def _():
        acts = terms[(held - 18) % 2]
        sides = terms[2 + (held - 18) // 2]
        grad[...] = mm(acts.astype(F32).T.astype(BF16), sides).astype(BF16)

    lefts = split_two(left[0])
    rights = split_two(right[0])
    g = grad[...]
    turned = split_two(mm(g, rights[0]) + mm(g, rights[1]))
    rotated = mm_two(mm, (lefts[0].T, lefts[1].T), turned)
    moment = MOMENT_DECAY * first[0] + (1.0 - MOMENT_DECAY) * rotated
    square = MOMENT_DECAY * second[0] + (1.0 - MOMENT_DECAY) * rotated * rotated
    new_first[0] = moment
    new_second[0] = square
    correction = 1.0 - MOMENT_DECAY**STEP
    direction = moment * (1.0 / correction) / (jnp.sqrt(square * (1.0 / correction)) + ADAM_EPS)
    update = mm(lefts[0], mm_t(direction.astype(BF16), rights[0]).astype(BF16))
    fresh = master[0] - rate[slot] * (update + WEIGHT_DECAY * master[0])
    new_master[0] = fresh
    low[0] = fresh.astype(BF16)


def optimize(slot_block, rate, got, terms, state):
    count = state[0].shape[0]
    matrix = per_image(C, C)
    full = struct((count, C, C), F32)
    return call(
        rotated_adam, count,
        [SMEM, SMEM, whole(*got.shape), whole(*terms.shape)] + [matrix] * 5,
        [matrix] * 4, [full, full, full, struct((count, C, C), BF16)],
        [pltpu.VMEM((C, C), BF16)], (slot_block, rate, got, terms, *state), "rotated_adam",
    )


AXES = ("rep", "shard")


def swap(value, mask):
    return lax.ppermute(value, AXES, [(i, i ^ mask) for i in range(PIECES)])


def plane_mask(step):
    return (step // 2) * 16 + (step % 2) * 2


def gather_line(piece):
    return jnp.stack([piece] + [swap(piece, 4 * k) for k in (1, 2, 3)])


def gather_first(line):
    split = (line.shape[1] + 1) // 2
    halves = line[:, :split], line[:, split:]
    return [jnp.stack([half, swap(half, mask)]) for half, mask in zip(halves, (16, 2))]


def gather_second(firsts):
    seconds = [swap(first, mask) for first, mask in zip(firsts, (2, 16))]
    return [firsts[0], seconds[0], firsts[1], seconds[1]]


def gather_plane(line):
    line = line[None]
    return [line] + [swap(line, mask) for mask in (2, 16, 18)]


def gather_core(plane):
    return plane + [swap(part, 1) for part in plane]


def add_up(*terms):
    total = terms[0].astype(F32)
    for term in terms[1:]:
        total = total + term.astype(F32)
    return total.astype(BF16)


def block_slots(owner, mats_all):
    block_ids = jnp.arange(mats_all, dtype=jnp.int32)
    return jnp.sum(
        jnp.where(owner[None, :] == block_ids[:, None], block_ids[None, :], 0), axis=1
    )


def pick_slots(grads, slots):
    index = jnp.where(slots < 18, slots, jnp.clip(slots - 4, 0, 21))
    held = (slots < 18) | ((slots >= 22) & (slots < BLOCKS))
    picked = jnp.take(grads, index, axis=0)
    return jnp.where(held.reshape((-1,) + (1,) * (grads.ndim - 1)), picked, jnp.zeros((), BF16))


class Split:
    def __init__(self):
        self.rep = lax.axis_index("rep")
        shard = lax.axis_index("shard")
        self.ids = jnp.stack([shard % 2, self.rep * 2 + shard // 2 % 2, shard // 4])

    def gather(self, master, vec_master, owner, act):
        mat_dev = master.shape[0]
        rows = master.astype(BF16).reshape(mat_dev, 2, 2, 2, 4, PIECE, C)
        rows = lax.dynamic_index_in_dim(rows, self.rep, 2, keepdims=False)
        rows = rows.transpose(3, 2, 1, 0, 4, 5).reshape(16, mat_dev, PIECE, C)
        slots = lax.all_to_all(rows, "shard", 0, 0).reshape(16 * mat_dev, PIECE, C)
        blocks = jnp.take(slots, owner[:BLOCKS], axis=0)
        width = vec_master.shape[1]
        vec = jnp.pad(vec_master.astype(BF16), ((0, 16 - VECS), (0, C - width)))
        place = lax.axis_index("shard") * width
        vec = jnp.where(self.rep == 0, jnp.roll(vec, place, axis=1), jnp.zeros((), BF16))
        rows = act.reshape(-1, C)
        rows = jnp.pad(rows, ((0, PIECE - rows.shape[0]), (0, 0)))
        attn = jnp.concatenate([blocks[22:26], rows[None]], axis=0)
        line_one = gather_line(jnp.concatenate([blocks[:9], vec[None]], axis=0))
        second, line_one = lax.optimization_barrier((blocks[9:22], line_one))
        first_one = gather_first(line_one)
        line_two = gather_line(second)
        planes_one = gather_second(first_one)
        line_two, attn, planes_one = lax.optimization_barrier((line_two, attn, planes_one))
        one = gather_core(planes_one)
        attn = lax.all_gather(attn, AXES)
        acts = attn[:, 4, : act.size // C].reshape(-1, 2, C).transpose(1, 0, 2)
        return one, gather_plane(line_two), attn, acts

    def gather_core(self, planes):
        return gather_core(planes)

    def reduce_early(self, grads):
        return lax.psum_scatter(grads, "shard", scatter_dimension=0, tiled=True)[0]

    def finish_early(self, late, *early):
        own = jnp.concatenate(early, axis=0)
        mine = lax.dynamic_index_in_dim(own, self.rep, 1, keepdims=False)
        other = lax.dynamic_index_in_dim(own, 1 - self.rep, 1, keepdims=False)
        return jnp.concatenate([late, add_up(mine, swap(other, 16))], axis=0)

    def reduce_core(self, keep, send):
        other = swap(send, 1)
        return [add_up(keep[k], other[k]) for k in range(4)]

    def reduce_late(self, planes, after):
        line = [swap(planes[k], plane_mask(k)) for k in (1, 2, 3)]
        lines = [add_up(planes[0][j], *[part[j] for part in line]) for j in range(4)]
        lines, _ = lax.optimization_barrier((lines, after))
        return add_up(lines[0], *[swap(lines[k], 4 * k) for k in (1, 2, 3)])

    def own(self, grads, slots, mat_dev, map_terms, grad_vectors):
        picked = pick_slots(grads, slots).reshape(16, mat_dev * PIECE, C)
        terms = jnp.broadcast_to(map_terms.reshape(1, -1, C), (16, map_terms.size // C, C))
        width = C // 16
        vec = grad_vectors.astype(BF16).reshape(VECS, 16, width).transpose(1, 0, 2)
        vec = jnp.pad(vec.reshape(16, 1, VECS * width), ((0, 0), (0, 0), (0, C - VECS * width)))
        sent = jnp.concatenate([picked, terms, vec], axis=1)
        got = lax.all_to_all(jnp.concatenate([sent, sent]), AXES, 0, 0)
        split = mat_dev * PIECE
        terms = got[:, split:-1].reshape(-1, 2, C).transpose(1, 0, 2)
        vec = jnp.sum(got[:, -1, : VECS * width].astype(F32), axis=0)
        return got, terms, vec.reshape(VECS, width)


class Plain:
    def __init__(self):
        self.ids = jnp.zeros((3,), jnp.int32)

    def gather(self, master, vec_master, owner, act):
        slots = lax.all_gather(master.astype(BF16), "shard", axis=0, tiled=True)
        vec = lax.all_gather(vec_master.astype(BF16), "shard", axis=1, tiled=True)
        blocks = jnp.take(slots, owner[:BLOCKS], axis=0)

        def parts(some):
            split = (some.shape[0] + 1) // 2
            pieces = some.reshape(-1, 2, 4, 4, PIECE, C).transpose(1, 2, 3, 0, 4, 5)
            halves = (slice(0, split), slice(split, None))
            return [
                jnp.stack([pieces[core, plane][:, halves[n // 2]] for plane in planes])
                for core in range(2)
                for n, (planes, _) in enumerate(HALVED)
            ]

        rows = jnp.zeros((C, C), BF16).at[:VECS].set(vec)
        one = parts(jnp.concatenate([blocks[:9], rows[None]], axis=0))
        flat = blocks[22:26].reshape(4, 2, 2, 2, 4, PIECE, C).transpose(2, 4, 3, 1, 0, 5, 6)
        acts = lax.all_gather(act, AXES, axis=0, tiled=True).reshape(-1, 2, C).transpose(1, 0, 2)
        return one, parts(blocks[9:22]), flat.reshape(PIECES, 4, PIECE, C), acts

    def gather_core(self, planes):
        return planes

    def reduce_early(self, grads):
        split = grads.reshape(4, 2, 2, -1, 2, PIECE, C).transpose(3, 2, 4, 1, 0, 5, 6)
        return split.reshape(-1, C, C)

    def finish_early(self, late, *early):
        return jnp.concatenate([late, *early], axis=0)

    def reduce_core(self, keep, send):
        return [jnp.stack([keep, send]).transpose(3, 0, 1, 2, 4, 5).reshape(-1, C, C)]

    def reduce_late(self, planes, after):
        return planes[0]

    def own(self, grads, slots, mat_dev, map_terms, grad_vectors):
        picked = pick_slots(grads, slots)
        mine = lax.psum_scatter(picked, "shard", scatter_dimension=0, tiled=True)
        rows = lax.psum(mine, "rep").reshape(mat_dev, 2, 2, 2, 4, PIECE, C)
        got = rows.transpose(2, 4, 3, 1, 0, 5, 6).reshape(PIECES, mat_dev * PIECE, C)
        terms = lax.all_gather(map_terms, AXES, axis=0, tiled=True)
        terms = terms.transpose(1, 0, 2)
        vec = lax.psum_scatter(grad_vectors, "shard", scatter_dimension=1, tiled=True)
        return got, terms, lax.psum(vec, "rep")


def shards(
    images,
    embeds,
    cotangent,
    counts,
    bucket_weight,
    owner,
    master,
    first_moment,
    second_moment,
    left_basis,
    right_basis,
    vec_master,
    vec_first,
    vec_second,
):
    mat_dev = master.shape[0]
    mats_all = mat_dev * lax.axis_size("shard")
    sizes = (lax.axis_size("rep"), lax.axis_size("shard"))
    plan = Split() if sizes == (2, 16) else Plain()
    emb = embeds.astype(F32)
    act = jax.nn.silu(emb).astype(BF16)
    *gathered, acts = plan.gather(master, vec_master, owner, act)
    slot_ids = jnp.arange(images.shape[0], dtype=jnp.int32)
    live = (slot_ids < counts[0, 0] + counts[0, 1]).astype(jnp.int32)
    weight = jnp.where(slot_ids < counts[0, 0], bucket_weight[0], bucket_weight[1])
    weight = jnp.where(live > 0, weight, 0.0)
    outputs, grad_images, grad_embeds, grads, map_terms, grad_vectors = layer(
        images, emb, act, cotangent, weight, live, plan, gathered
    )
    all_slots = block_slots(owner, mats_all)
    shard = lax.axis_index("shard")
    slot_block = lax.dynamic_slice_in_dim(all_slots, shard * mat_dev, mat_dev, 0)
    got, terms, own_vec = plan.own(grads, all_slots, mat_dev, map_terms, grad_vectors)
    step_rate = jnp.where(slot_block < BLOCKS, 2.0 * block_spread(slot_block), 0.0)
    new_first, new_second, new_master, master_low = optimize(
        slot_block,
        step_rate,
        got,
        jnp.concatenate([acts, terms], axis=0),
        (left_basis, right_basis, first_moment, second_moment, master),
    )
    correction = 1.0 - MOMENT_DECAY**STEP
    vec_first_new = MOMENT_DECAY * vec_first + (1.0 - MOMENT_DECAY) * own_vec
    vec_second_new = MOMENT_DECAY * vec_second + (1.0 - MOMENT_DECAY) * own_vec * own_vec
    vec_master_new = vec_master - VECTOR_RATE * (vec_first_new / correction) / (
        jnp.sqrt(vec_second_new / correction) + ADAM_EPS
    )
    return (
        outputs,
        grad_images,
        grad_embeds,
        new_first,
        new_second,
        new_master,
        master_low,
        vec_first_new,
        vec_second_new,
        vec_master_new,
        vec_master_new.astype(jnp.bfloat16),
    )


def solution(mesh):
    return jax.shard_map(
        shards,
        mesh=mesh,
        in_specs=(
            P(("rep", "shard"), None, None),
            P(("rep", "shard"), None),
            P(("rep", "shard"), None, None),
            P(("rep", "shard"), None),
            P(),
            P(),
            P("shard", None, None),
            P("shard", None, None),
            P("shard", None, None),
            P("shard", None, None),
            P("shard", None, None),
            P(None, "shard"),
            P(None, "shard"),
            P(None, "shard"),
        ),
        out_specs=(
            P(("rep", "shard"), None, None),
            P(("rep", "shard"), None, None),
            P(("rep", "shard"), None),
            P("shard", None, None),
            P("shard", None, None),
            P("shard", None, None),
            P("shard", None, None),
            P(None, "shard"),
            P(None, "shard"),
            P(None, "shard"),
            P(None, "shard"),
        ),
        check_vma=False,
    )
```

```python
import functools
import math

import jax
import jax.numpy as jnp
from jax import lax
from jax.experimental import pallas as pl
from jax.experimental.pallas import tpu as pltpu
from jax.sharding import PartitionSpec as P

C = 512
EMB = 1024
HEADS = 8
HEAD = 64
GROUPS = 32
SIDE = 32
HW = 1024
BLOCKS = 26
VECS = 13
STEP = 2
PAD = SIDE
SLAB = HW + 2 * PAD
ROWS = 128
QROWS = 256

EPS_NORM = 1e-05
ADAM_EPS = 1e-08
MOMENT_DECAY = 0.5
WEIGHT_DECAY = 0.01
VECTOR_RATE = 0.2
PRECISE = lax.Precision.HIGHEST
F32 = jnp.float32
BF16 = jnp.bfloat16
ANY = pl.BlockSpec(memory_space=pl.ANY)
SMEM = pl.BlockSpec(memory_space=pltpu.SMEM)
VMEM = pl.BlockSpec(memory_space=pltpu.VMEM)
VMEM_LIMIT = 56 * 2**20


def block_spread(block_index):
    return jnp.where(
        block_index < 18,
        (9.0 * C) ** (-0.5),
        jnp.where(
            block_index < 22,
            EMB ** (-0.5),
            jnp.where(
                block_index < 24,
                1.25 * C ** (-0.5),
                jnp.where(
                    block_index < 25,
                    C ** (-0.5),
                    jnp.where(block_index < 26, 0.295 * (HW / C) ** 0.5, C ** (-0.5)),
                ),
            ),
        ),
    )


def mm(a, b):
    return jnp.dot(a, b, preferred_element_type=F32)


def mm_t(a, b):
    return lax.dot_general(a, b, (((1,), (1,)), ((), ())), preferred_element_type=F32)


def sigmoid(u):
    return 1.0 / (1.0 + jnp.exp(-u))


def silu_slope(u):
    s = sigmoid(u)
    return s * (1.0 + u * (1.0 - s))


def chunks(count, body, init=0):
    return lax.fori_loop(0, count, body, init)


def rows_of(index, size):
    return pl.ds(pl.multiple_of(index * size, size), size)


def group_mean(column_sum):
    total = jnp.broadcast_to(column_sum, (8, C))
    lane = lax.broadcasted_iota(jnp.int32, (8, C), 1)
    for step in (1, 2, 4, 8):
        other = jnp.where(
            (lane & step) != 0, pltpu.roll(total, step, 1), pltpu.roll(total, C - step, 1)
        )
        total = total + other
    return total[0:1] * (1.0 / (HW * (C // GROUPS)))


def norm_stats(read):
    zero = jnp.zeros((1, C), F32)
    total = chunks(
        HW // ROWS,
        lambda c, t: t + jnp.sum(read(rows_of(c, ROWS)), axis=0, keepdims=True),
        zero,
    )
    mean = group_mean(total)

    def squares(c, t):
        centered = read(rows_of(c, ROWS)) - mean
        return t + jnp.sum(centered * centered, axis=0, keepdims=True)

    var = group_mean(chunks(HW // ROWS, squares, zero))
    return mean, lax.rsqrt(var + EPS_NORM)


def clear_pads(slab):
    zeros = jnp.zeros((PAD, C), BF16)
    for lead in slab_leads(slab):
        slab[lead + (pl.ds(0, PAD), slice(None))] = zeros
        slab[lead + (pl.ds(PAD + HW, PAD), slice(None))] = zeros


def slab_leads(slab):
    if len(slab.shape) == 3:
        return [(j,) for j in range(3)]
    return [(i, j) for i in range(slab.shape[0]) for j in range(3)]


def store_slab(slab, lead, c, chunk):
    column = lax.broadcasted_iota(jnp.int32, (ROWS, C), 0) & (SIDE - 1)
    before = jnp.where(column == 0, 0.0, pltpu.roll(chunk, 1, 0))
    after = jnp.where(column == SIDE - 1, 0.0, pltpu.roll(chunk, ROWS - 1, 0))
    rows = pl.ds(pl.multiple_of(c * ROWS + PAD, PAD), ROWS)
    slab[lead + (0, rows, slice(None))] = before.astype(BF16)
    slab[lead + (1, rows, slice(None))] = chunk.astype(BF16)
    slab[lead + (2, rows, slice(None))] = after.astype(BF16)


def conv_rows(slab, lead, weights, base, size, back):
    total = None
    for tap in range(9):
        di, dj = tap // 3, tap % 3
        if back:
            di, dj = 2 - di, 2 - dj
        rows = pl.ds(pl.multiple_of(base + di * SIDE, SIDE), size)
        piece = slab[lead + (dj, rows, slice(None))]
        term = (mm_t if back else mm)(piece, weights[tap])
        total = term if total is None else total + term
    return total


CONV_ROWS = 1024


PIECES = 32
PIECE = C // PIECES


def piece_rows(ids, core, plane, line):
    index = ((ids[0] ^ core) * 4 + (ids[1] ^ plane)) * 4 + (ids[2] ^ line)
    return pl.ds(pl.multiple_of(index * PIECE, PIECE), PIECE)


DIRECT = (((0,), 0), ((1,), 0), ((2,), 0), ((3,), 0))
HALVED = (((0, 2), 0), ((1, 3), 0), ((0, 1), 1), ((2, 3), 1))
COPIES = 64


def flat_place(n):
    return (n % 2 * 4 + n // 16 * 2 + n // 2 % 2) * 4 + n // 4 % 4


def block_copies(ids, parts, dest, sem, first, count):
    if len(parts) == 1:
        return [
            pltpu.make_async_copy(
                parts[0].at[n, pl.ds(first, count)],
                dest.at[:, pl.ds(flat_place(n) * PIECE, PIECE), :],
                sem.at[n],
            )
            for n in range(PIECES)
        ]
    copies = []
    layout = HALVED if parts[0].shape[0] == 2 else DIRECT
    for n, part in enumerate(parts):
        planes, half = layout[n % 4]
        start = half * parts[0].shape[2]
        low, high = max(first, start), min(first + count, start + part.shape[2])
        if low >= high:
            continue
        for side, plane in enumerate(planes):
            for line in range(4):
                rows = piece_rows(ids, n // 4, plane, line)
                copies.append(
                    pltpu.make_async_copy(
                        part.at[side, line, pl.ds(low - start, high - low)],
                        dest.at[pl.ds(low - first, high - low), rows, :],
                        sem.at[len(copies)],
                    )
                )
    return copies


def start_all(*args):
    for copy in block_copies(*args):
        copy.start()


def wait_all(*args):
    for copy in block_copies(*args):
        copy.wait()


def store_flat(out, slot, grad):
    for n in range(PIECES):
        place = flat_place(n) * PIECE
        out[slot, n % 16, n // 16] = grad[place : place + PIECE]


def store_pieces(ids, keep, send, block, grad):
    half = C // 2
    mine = ids[0] == 0
    kept = jnp.where(mine, grad[:half], grad[half:])
    sent = jnp.where(mine, grad[half:], grad[:half])
    for plane in range(4):
        for line in range(4):
            rows = slice((plane * 4 + line) * PIECE, (plane * 4 + line + 1) * PIECE)
            keep[plane ^ ids[1], line ^ ids[2], block] = kept[rows]
            send[plane ^ ids[1], line ^ ids[2], block] = sent[rows]


def fwd_one(ids, *refs):
    parts = refs[:8]
    x, nhat, a1, stats, vec, weights, slab, hidden, held, sem, vec_sem = refs[8:]
    step = pl.program_id(0)

    def vec_copies():
        last = [part for n, part in enumerate(parts) if n % 4 > 1]
        return [
            pltpu.make_async_copy(part.at[:, :, part.shape[2] - 1], held.at[n], vec_sem.at[n])
            for n, part in enumerate(last)
        ]

    @pl.when(step == 0)
    def _():
        for copy in vec_copies():
            copy.start()
        start_all(ids, parts, weights, sem, 0, 9)
        clear_pads(slab)

    def read(rows):
        return x[0, rows, :].astype(F32)

    mean, inv = norm_stats(read)

    @pl.when(step == 0)
    def _():
        for copy in vec_copies():
            copy.wait()
        total = jnp.zeros((16, C), F32)
        for n in range(PIECES):
            total = total + held[n // 8, n // 4 % 2, n % 4].astype(F32)
        vec[...] = total

    gain = inv * vec[0:1]
    bias = vec[1:2]

    def activate(c, _):
        rows = rows_of(c, ROWS)
        pre = (read(rows) - mean) * gain + bias
        act = pre * sigmoid(pre)
        a1[0, rows, :] = act.astype(BF16)
        store_slab(slab, (), c, act)
        return 0

    chunks(HW // ROWS, activate)

    @pl.when(step == 0)
    def _():
        wait_all(ids, parts, weights, sem, 0, 9)

    def conv(c, _):
        hidden[rows_of(c, CONV_ROWS), :] = (
            conv_rows(slab, (), weights, c * CONV_ROWS, CONV_ROWS, False) + vec[2:3]
        )
        return 0

    chunks(HW // CONV_ROWS, conv)
    mean_two, inv_two = norm_stats(lambda rows: hidden[rows, :])
    stats[0] = jnp.concatenate([mean, inv, inv_two, jnp.zeros((5, C), F32)], axis=0)

    def normalize(c, _):
        rows = rows_of(c, ROWS)
        nhat[0, rows, :] = (hidden[rows, :] - mean_two) * inv_two
        return 0

    chunks(HW // ROWS, normalize)


def fwd_two(ids, *refs):
    parts = refs[:8]
    nhat, x, act, vec, a2, r1, stats, weights, maps, slab, sem, map_sem = refs[8:]
    step = pl.program_id(0)

    @pl.when(step == 0)
    def _():
        start_all(ids, parts, maps, map_sem, 9, 4)
        start_all(ids, parts, weights, sem, 0, 9)
        clear_pads(slab)

    @pl.when(step == 0)
    def _():
        wait_all(ids, parts, maps, map_sem, 9, 4)

    row = act[0]
    scale = (mm(row[:, :C], maps[0]) + mm(row[:, C:], maps[1]))[0:1] + vec[3:4]
    shift = (mm(row[:, :C], maps[2]) + mm(row[:, C:], maps[3]))[0:1] + vec[4:5]
    stats[0] = jnp.concatenate([scale, shift, jnp.zeros((6, C), F32)], axis=0)
    gain = vec[5:6]
    bias = vec[6:7]

    def activate(c, _):
        rows = rows_of(c, ROWS)
        pre = (nhat[0, rows, :] * gain + bias) * (1.0 + scale) + shift
        act_two = pre * sigmoid(pre)
        a2[0, rows, :] = act_two.astype(BF16)
        store_slab(slab, (), c, act_two)
        return 0

    chunks(HW // ROWS, activate)

    @pl.when(step == 0)
    def _():
        wait_all(ids, parts, weights, sem, 0, 9)

    def conv(c, _):
        rows = rows_of(c, CONV_ROWS)
        hidden = conv_rows(slab, (), weights, c * CONV_ROWS, CONV_ROWS, False) + vec[7:8]
        r1[0, rows, :] = x[0, rows, :].astype(F32) + hidden
        return 0

    chunks(HW // CONV_ROWS, conv)


MM_ROWS = 512


def attention(ids, counts, bucket_weight, *refs):
    parts = refs[:1]
    (
    r1, cot, vec, out, dr1, grads, sums, weights,
    nhat, n3, n3t, q, k, v, da, dat, qt, kt, vt, att, dyb, dq, dk, dv, dn3, acc, sem, flat, flat_sem,
    ) = refs[1:]
    step = pl.program_id(0)

    def out_copy(n):
        return pltpu.make_async_copy(flat.at[n], grads.at[:, 9 + n], flat_sem.at[n])

    @pl.when(step == 0)
    def _():
        start_all(ids, parts, weights, sem, 0, 4)
        sums[...] = jnp.zeros((8, C), F32)

    mean, inv = norm_stats(lambda rows: r1[0, rows, :])
    gain = vec[8:9]
    bias = vec[9:10]
    is_live = step < counts[0, 0] + counts[0, 1]
    image_weight = jnp.where(step < counts[0, 0], bucket_weight[0], bucket_weight[1])
    image_weight = jnp.where(is_live, image_weight, 0.0)

    def normalize(c, total):
        rows = rows_of(c, ROWS)
        normed = (r1[0, rows, :] - mean) * inv
        nhat[rows, :] = normed
        n3[rows, :] = (normed * gain + bias).astype(BF16)
        low = (cot[0, rows, :].astype(F32) * image_weight).astype(BF16)
        dyb[rows, :] = low
        return total + jnp.sum(low.astype(F32), axis=0, keepdims=True)

    zero = jnp.zeros((1, C), F32)
    sum_dy = chunks(HW // ROWS, normalize, zero)

    @pl.when(step == 0)
    def _():
        wait_all(ids, parts, weights, sem, 0, 4)

    def project(c, _):
        rows = rows_of(c, MM_ROWS)
        normed = n3[rows, :]
        q[rows, :] = (mm(normed, weights[0]) + vec[10:11]).astype(BF16) * 0.125
        k[rows, :] = mm(normed, weights[1]).astype(BF16)
        v[rows, :] = (mm(normed, weights[2]) + vec[11:12]).astype(BF16)
        da[rows, :] = mm_t(dyb[rows, :], weights[3]).astype(BF16)
        return 0

    chunks(HW // MM_ROWS, project)
    n3t[...] = n3[...].T
    qt[...] = q[...].T
    kt[...] = k[...].T
    vt[...] = v[...].T
    dat[...] = da[...].T

    def head_pair(pair, _):
        cols = pl.ds(pl.multiple_of(pair * 128, 128), 128)
        first = lax.broadcasted_iota(jnp.int32, (HW, 128), 1) < HEAD

        def one_head(value, side):
            blank = jnp.zeros_like(value)
            return jnp.where(first, value, blank) if side == 0 else jnp.where(first, blank, value)

        keys, values = k[:, cols], v[:, cols]
        expos, scaled, dots = [], [], []
        for side in range(2):
            head_rows = pl.ds(pl.multiple_of(pair * 128 + side * HEAD, HEAD), HEAD)
            scores = mm(one_head(keys, side), qt[cols, :])
            expo = jnp.exp(scores - jnp.max(scores, axis=0, keepdims=True))
            inverse = 1.0 / jnp.sum(expo, axis=0, keepdims=True)
            expos.append(expo.astype(BF16))
            attended = mm(vt[head_rows, :], expos[side]) * inverse
            att[head_rows, :] = attended.astype(BF16)
            scaled.append((dat[head_rows, :].astype(F32) * inverse).astype(BF16))
            dots.append(jnp.sum(attended * scaled[side].astype(F32), axis=0, keepdims=True))
        both = jnp.concatenate(scaled, axis=0)
        turned = both.T
        dks, dvs = [], []
        for side in range(2):
            head_rows = pl.ds(pl.multiple_of(pair * 128 + side * HEAD, HEAD), HEAD)
            dprobs = mm(one_head(values, side), both)
            dscores = (expos[side].astype(F32) * (dprobs - dots[side])).astype(BF16)
            dvs.append(mm(expos[side], turned))
            dks.append(mm(dscores, q[:, cols]))
            dat[head_rows, :] = (mm(kt[head_rows, :], dscores) * 0.125).astype(BF16)
        dk[:, cols] = jnp.where(first, dks[0], dks[1]).astype(BF16)
        dv[:, cols] = jnp.where(first, dvs[0], dvs[1]).astype(BF16)
        return 0

    chunks(HEADS // 2, head_pair)
    dq[...] = dat[...].T
    q[...] = att[...].T


    def result(c, _):
        rows = rows_of(c, MM_ROWS)
        y = r1[0, rows, :] + mm(q[rows, :], weights[3]) + vec[12:13]
        out[0, rows, :] = jnp.where(is_live, y, 0.0).astype(BF16)
        dn3[rows, :] = (
            mm_t(dq[rows, :], weights[0])
            + mm_t(dk[rows, :], weights[1])
            + mm_t(dv[rows, :], weights[2])
        )
        return 0

    chunks(HW // MM_ROWS, result)

    terms = (
        lambda: mm(n3t[...], dq[...]),
        lambda: mm(n3t[...], dk[...]),
        lambda: mm(n3t[...], dv[...]),
        lambda: mm(att[...], dyb[...]),
    )
    for n, term in enumerate(terms):
        @pl.when(step == 0)
        def _(n=n, term=term):
            acc[n] = term()

        @pl.when(step != 0)
        def _(n=n, term=term):
            store_flat(flat, n, (acc[n] + term()).astype(BF16))
            out_copy(n).start()

    def column_sums(c, totals):
        rows = rows_of(c, ROWS)
        grad = dn3[rows, :]
        new = (
            grad * nhat[rows, :],
            grad,
            dq[rows, :].astype(F32),
            dv[rows, :].astype(F32),
        )
        return tuple(t + jnp.sum(n, axis=0, keepdims=True) for t, n in zip(totals, new))

    sum_cross, sum_grad, sum_q, sum_v = chunks(HW // ROWS, column_sums, (zero,) * 4)
    sums[...] += jnp.concatenate(
        [sum_cross, sum_grad, sum_q, sum_v, sum_dy, jnp.zeros((3, C), F32)], axis=0
    )
    mean_grad = group_mean(gain * sum_grad)
    mean_cross = group_mean(gain * sum_cross)

    def back(c, _):
        rows = rows_of(c, ROWS)
        inner = gain * dn3[rows, :] - mean_grad - nhat[rows, :] * mean_cross
        dr1[0, rows, :] = cot[0, rows, :].astype(F32) * image_weight + inv * inner
        return 0

    chunks(HW // ROWS, back)

    @pl.when(step != 0)
    def _():
        for n in range(4):
            out_copy(n).wait()


def split_three(value):
    high = value.astype(BF16)
    rest = value - high.astype(F32)
    middle = rest.astype(BF16)
    return high, middle, (rest - middle.astype(F32)).astype(BF16)


def bwd_two_data(ids, *refs):
    parts = refs[:8]
    dr1, nhat, stats, norms, vec, emb, dh1, dvec, demb, sums = refs[8:18]
    weights, maps, slab, dz, sem, map_sem = refs[18:]
    step = pl.program_id(0)

    @pl.when(step == 0)
    def _():
        start_all(ids, parts, weights, sem, 0, 9)
        start_all(ids, parts, maps, map_sem, 9, 4)
        clear_pads(slab)
        sums[...] = jnp.zeros((8, C), F32)

    zero = jnp.zeros((1, C), F32)

    def fill(c, total):
        chunk = dr1[0, rows_of(c, ROWS), :]
        store_slab(slab, (), c, chunk)
        return total + jnp.sum(chunk.astype(BF16).astype(F32), axis=0, keepdims=True)

    sum_h2 = chunks(HW // ROWS, fill, zero)

    @pl.when(step == 0)
    def _():
        wait_all(ids, parts, weights, sem, 0, 9)
        wait_all(ids, parts, maps, map_sem, 9, 4)

    scale = 1.0 + stats[0, 0:1]
    shift = stats[0, 1:2]
    inv = norms[0, 2:3]
    gain = vec[5:6]
    bias = vec[6:7]

    def conv(c, _):
        dz[rows_of(c, CONV_ROWS), :] = conv_rows(
            slab, (), weights, c * CONV_ROWS, CONV_ROWS, True
        )
        return 0

    chunks(HW // CONV_ROWS, conv)

    def slope(c, totals):
        rows = rows_of(c, ROWS)
        normed = nhat[0, rows, :]
        pre = (normed * gain + bias) * scale + shift
        grad = dz[rows, :] * silu_slope(pre)
        dz[rows, :] = grad
        return (
            totals[0] + jnp.sum(grad, axis=0, keepdims=True),
            totals[1] + jnp.sum(grad * normed, axis=0, keepdims=True),
        )

    sum_dz, sum_cross = chunks(HW // ROWS, slope, (zero, zero))
    factor = scale * gain
    mean_grad = group_mean(factor * sum_dz)
    mean_cross = group_mean(factor * sum_cross)

    def back(c, total):
        rows = rows_of(c, ROWS)
        low = (inv * (factor * dz[rows, :] - mean_grad - nhat[0, rows, :] * mean_cross)).astype(BF16)
        dh1[0, rows, :] = low
        return total + jnp.sum(low.astype(F32), axis=0, keepdims=True)

    sum_h1 = chunks(HW // ROWS, back, zero)
    dscale = gain * sum_cross + bias * sum_dz
    sums[...] += jnp.concatenate(
        [sum_h1, dscale, sum_dz, scale * sum_cross, scale * sum_dz, sum_h2, jnp.zeros((2, C), F32)],
        axis=0,
    )
    pieces_scale = split_three(dscale)
    pieces_shift = split_three(sum_dz)
    blank = jnp.zeros((5, C), F32)

    def stack(pieces):
        return jnp.concatenate([p.astype(F32) for p in pieces] + [blank], axis=0).astype(BF16)

    d_scale = stack(pieces_scale)
    d_shift = stack(pieces_shift)

    def reach(upper):
        parts = mm_t(d_scale, maps[upper]) + mm_t(d_shift, maps[2 + upper])
        return jnp.sum(parts, axis=0, keepdims=True)

    row = jnp.concatenate([reach(0), reach(1)], axis=1)
    demb[0] = jnp.broadcast_to(row * silu_slope(emb[0, 0:1].astype(F32)), (8, EMB))
    dvec[0] = jnp.concatenate([dscale, sum_dz, jnp.zeros((6, C), F32)], axis=0)


def fill_taps(grad, act, slab, at):
    step = pl.program_id(0)

    @pl.when(step == 0)
    def _():
        clear_pads(slab)

    def fill(c, _):
        store_slab(slab, (step,), c, grad[0, rows_of(c, ROWS), :].astype(F32))
        return 0

    chunks(HW // ROWS, fill)
    at[step] = act[0].T


def tap_grad(slab, at, tap):
    di = 2 - tap // 3
    dj = tap // 3 * 3 + 2 - tap
    rows = pl.ds(pl.multiple_of(di * SIDE, SIDE), HW)
    total = mm(at[0], slab[0, dj, rows, :])
    for image in range(1, slab.shape[0]):
        total = total + mm(at[image], slab[image, dj, rows, :])
    return total.astype(BF16)


def one_taps(ids, grad, act, keep, send, slab, at):
    fill_taps(grad, act, slab, at)

    @pl.when(pl.program_id(0) == pl.num_programs(0) - 1)
    def _():
        def one(tap, _):
            store_pieces(ids, keep, send, tap, tap_grad(slab, at, tap))
            return 0

        for tap in range(9):
            one(tap, 0)


def two_taps(grad, act, others, out, slab, at, flat, sem):
    fill_taps(grad, act, slab, at)

    def out_copy(tap):
        return pltpu.make_async_copy(flat.at[tap % 2], out.at[:, tap], sem.at[tap % 2])

    @pl.when(pl.program_id(0) == pl.num_programs(0) - 1)
    def _():
        for tap in range(9):
            if tap > 1:
                out_copy(tap - 2).wait()
            store_flat(flat, tap % 2, tap_grad(slab, at, tap))
            out_copy(tap).start()
        out_copy(7).wait()
        out_copy(8).wait()


def bwd_one_data(ids, *refs):
    parts, (dh1, x, dr1, norms, vec, dx, sums, weights, slab, dp, sem) = refs[:8], refs[8:]
    step = pl.program_id(0)

    @pl.when(step == 0)
    def _():
        start_all(ids, parts, weights, sem, 0, 9)
        clear_pads(slab)
        sums[...] = jnp.zeros((8, C), F32)

    def fill(c, _):
        store_slab(slab, (), c, dh1[0, rows_of(c, ROWS), :].astype(F32))
        return 0

    chunks(HW // ROWS, fill)

    def read(rows):
        return x[0, rows, :].astype(F32)

    mean, inv = norms[0, 0:1], norms[0, 1:2]
    gain = vec[0:1]
    bias = vec[1:2]

    @pl.when(step == 0)
    def _():
        wait_all(ids, parts, weights, sem, 0, 9)

    def conv(c, _):
        dp[rows_of(c, CONV_ROWS), :] = conv_rows(
            slab, (), weights, c * CONV_ROWS, CONV_ROWS, True
        )
        return 0

    chunks(HW // CONV_ROWS, conv)
    zero = jnp.zeros((1, C), F32)

    def slope(c, totals):
        rows = rows_of(c, ROWS)
        normed = (read(rows) - mean) * inv
        grad = dp[rows, :] * silu_slope(normed * gain + bias)
        dp[rows, :] = grad
        return (
            totals[0] + jnp.sum(grad * normed, axis=0, keepdims=True),
            totals[1] + jnp.sum(grad, axis=0, keepdims=True),
        )

    sum_cross, sum_grad = chunks(HW // ROWS, slope, (zero, zero))
    sums[...] += jnp.concatenate([sum_cross, sum_grad, jnp.zeros((6, C), F32)], axis=0)
    mean_grad = group_mean(gain * sum_grad)
    mean_cross = group_mean(gain * sum_cross)

    def back(c, _):
        rows = rows_of(c, ROWS)
        normed = (read(rows) - mean) * inv
        dx[0, rows, :] = dr1[0, rows, :] + inv * (
            gain * dp[rows, :] - mean_grad - normed * mean_cross
        )
        return 0

    chunks(HW // ROWS, back)


def per_image(*shape):
    return pl.BlockSpec((1,) + shape, lambda i: (i,) + (0,) * len(shape))


def whole(*shape):
    return pl.BlockSpec(shape, lambda i: (0,) * len(shape))


def struct(shape, kind):
    return jax.ShapeDtypeStruct(shape, kind)


def call(body, images, in_specs, out_specs, out_shape, scratch, args, name, flops=20 * 10**9, aliases=None):
    return pl.pallas_call(
        body,
        grid=(images,),
        in_specs=in_specs,
        out_specs=out_specs,
        out_shape=out_shape,
        scratch_shapes=scratch,
        input_output_aliases=aliases or {},
        name=name,
        compiler_params=pltpu.CompilerParams(
            vmem_limit_bytes=VMEM_LIMIT, dimension_semantics=("arbitrary",)
        ),
        cost_estimate=pl.CostEstimate(flops=flops, bytes_accessed=30 * 2**20, transcendentals=0),
    )(*args)


IMAGE = per_image(HW, C)
VEC = whole(16, C)
PARTS = [ANY] * 8
SEMS = pltpu.SemaphoreType.DMA((COPIES,))


def layer(images, emb_rows, act_rows, cotangent, counts, bucket_weight, plan, gathered):
    images_one, chunk_one, planes_two, chunk_attn = gathered
    ids = plan.ids
    count = images.shape[0]
    big = lambda kind: struct((count, HW, C), kind)
    taps = pltpu.VMEM((9, C, C), BF16)
    maps = pltpu.VMEM((4, C, C), BF16)
    slab = pltpu.VMEM((3, SLAB, C), BF16)
    slabs = pltpu.VMEM((count, 3, SLAB, C), BF16)
    turned = pltpu.VMEM((count, C, HW), BF16)
    low = pltpu.VMEM((HW, C), BF16)
    lowt = pltpu.VMEM((C, HW), BF16)
    full = pltpu.VMEM((HW, C), F32)
    nhat, a1, norms, vectors = call(
        fwd_one, count, [SMEM] + PARTS + [IMAGE], [IMAGE, IMAGE, per_image(8, C), VEC],
        [big(F32), big(BF16), struct((count, 8, C), F32), struct((16, C), F32)],
        [taps, slab, full, pltpu.VMEM((4, 2, 4, PIECE, C), BF16), SEMS, pltpu.SemaphoreType.DMA((4,))],
        (ids, *chunk_one, images_one), "first_conv",
    )
    planes_two, nhat = lax.optimization_barrier((planes_two, nhat))
    chunk_two = plan.gather_core(planes_two)
    a2, r1, stats = call(
        fwd_two, count, [SMEM] + PARTS + [IMAGE, IMAGE, per_image(16, EMB), VEC],
        [IMAGE, IMAGE, per_image(8, C)],
        [big(BF16), big(F32), struct((count, 8, C), F32)],
        [taps, maps, slab, SEMS, SEMS],
        (plan.ids_two, *chunk_two, nhat, images, act_rows, vectors), "second_conv",
    )
    early = struct((16, 13, 2, PIECE, C), BF16)
    out, dr1, grads_attn, sums_attn = call(
        attention, count, [SMEM, SMEM, SMEM, ANY] + [IMAGE, IMAGE, VEC],
        [IMAGE, IMAGE, ANY, whole(8, C)],
        [big(BF16), big(F32), early, struct((8, C), F32)],
        [maps, full, low, lowt, low, low, low, low, lowt, lowt, lowt, lowt, lowt,
         low, low, low, low, full, pltpu.VMEM((4, C, C), F32), SEMS,
         pltpu.VMEM((4, 16, 2, PIECE, C), BF16), pltpu.SemaphoreType.DMA((4,))],
        (ids, counts, bucket_weight, chunk_attn, r1, cotangent, vectors), "attention", 80 * 10**9,
    )
    (early,) = call(
        two_taps, count, [IMAGE, IMAGE, ANY], [ANY], [early],
        [slabs, turned, pltpu.VMEM((2, 16, 2, PIECE, C), BF16), pltpu.SemaphoreType.DMA((2,))],
        (dr1, a2, grads_attn), "second_conv_taps", aliases={2: 0},
    )
    grads_early = plan.reduce_early(early)
    dr1, _ = lax.optimization_barrier((dr1, early))
    dh1, dvec, demb, sums_two = call(
        bwd_two_data, count,
        [SMEM] + PARTS + [IMAGE, IMAGE, per_image(8, C), per_image(8, C), VEC, per_image(8, EMB)],
        [IMAGE, per_image(8, C), per_image(8, EMB), whole(8, C)],
        [big(BF16), struct((count, 8, C), F32), struct((count, 8, EMB), F32), struct((8, C), F32)],
        [taps, maps, slab, full, SEMS, SEMS],
        (plan.ids_two, *chunk_two, dr1, nhat, stats, norms, vectors, emb_rows), "second_conv_back",
    )
    late = call(
        one_taps, count, [SMEM, IMAGE, IMAGE], [whole(4, 4, 9, PIECE, C)] * 2,
        [struct((4, 4, 9, PIECE, C), BF16)] * 2,
        [slabs, turned], (ids, dh1, a1), "first_conv_taps",
    )
    planes = plan.reduce_core(*late)
    dh1, _ = lax.optimization_barrier((dh1, planes))
    dx, sums_one = call(
        bwd_one_data, count, [SMEM] + PARTS + [IMAGE, IMAGE, IMAGE, per_image(8, C), VEC],
        [IMAGE, whole(8, C)],
        [big(F32), struct((8, C), F32)],
        [taps, slab, full, SEMS],
        (ids, *chunk_one, dh1, images, dr1, norms, vectors), "first_conv_back",
    )
    grads_late = plan.reduce_late(planes, dx)
    grads = plan.finish_early(grads_late, grads_early)
    map_terms = dvec[:, :2].astype(BF16)
    grad_vectors = jnp.concatenate([sums_one[:2], sums_two[:6], sums_attn[:5]], axis=0)
    return out, dx, demb[:, 0], grads, map_terms, grad_vectors


def split_two(value):
    high = value.astype(BF16)
    return high, (value - high.astype(F32)).astype(BF16)


def mm_two(dot, a, b):
    return dot(a[0], b[0]) + (dot(a[0], b[1]) + dot(a[1], b[0]))


def rotated_adam(block, rate, got, terms, left, right, first, second, master, *refs):
    new_first, new_second, new_master, low, grad = refs
    slot = pl.program_id(0)
    held = block[slot]
    for n in range(PIECES):
        place = flat_place(n) * PIECE
        grad[place : place + PIECE] = got[n, rows_of(slot, PIECE), :]

    @pl.when((held >= 18) & (held < 22))
    def _():
        acts = terms[(held - 18) % 2]
        sides = terms[2 + (held - 18) // 2]
        grad[...] = mm(acts.astype(F32).T.astype(BF16), sides).astype(BF16)

    lefts = split_two(left[0])
    rights = split_two(right[0])
    g = grad[...]
    turned = split_two(mm(g, rights[0]) + mm(g, rights[1]))
    rotated = mm_two(mm, (lefts[0].T, lefts[1].T), turned)
    moment = MOMENT_DECAY * first[0] + (1.0 - MOMENT_DECAY) * rotated
    square = MOMENT_DECAY * second[0] + (1.0 - MOMENT_DECAY) * rotated * rotated
    new_first[0] = moment
    new_second[0] = square
    correction = 1.0 - MOMENT_DECAY**STEP
    direction = moment * (1.0 / correction) / (jnp.sqrt(square * (1.0 / correction)) + ADAM_EPS)
    update = mm(lefts[0], mm_t(direction.astype(BF16), rights[0]).astype(BF16))
    fresh = master[0] - rate[slot] * (update + WEIGHT_DECAY * master[0])
    new_master[0] = fresh
    low[0] = fresh.astype(BF16)


def optimize(slot_block, rate, got, terms, state):
    count = state[0].shape[0]
    matrix = per_image(C, C)
    full = struct((count, C, C), F32)
    return call(
        rotated_adam, count,
        [SMEM, SMEM, whole(*got.shape), whole(*terms.shape)] + [matrix] * 5,
        [matrix] * 4, [full, full, full, struct((count, C, C), BF16)],
        [pltpu.VMEM((C, C), BF16)], (slot_block, rate, got, terms, *state), "rotated_adam",
    )


AXES = ("rep", "shard")


def swap(value, mask):
    return lax.ppermute(value, AXES, [(i, i ^ mask) for i in range(PIECES)])


def plane_mask(step):
    return (step // 2) * 16 + (step % 2) * 2


def gather_line(piece):
    return jnp.stack([piece] + [swap(piece, 4 * k) for k in (1, 2, 3)])


def gather_first(line):
    split = (line.shape[1] + 1) // 2
    halves = line[:, :split], line[:, split:]
    return [jnp.stack([half, swap(half, mask)]) for half, mask in zip(halves, (16, 2))]


def gather_second(firsts):
    seconds = [swap(first, mask) for first, mask in zip(firsts, (2, 16))]
    return [firsts[0], seconds[0], firsts[1], seconds[1]]


def gather_plane(line):
    line = line[None]
    return [line] + [swap(line, mask) for mask in (2, 16, 18)]


def gather_core(planes, core):
    return planes + [core[0], swap(planes[1], 1), core[1], swap(planes[3], 1)]


def add_up(*terms):
    total = terms[0].astype(F32)
    for term in terms[1:]:
        total = total + term.astype(F32)
    return total.astype(BF16)


def block_slots(owner, mats_all):
    block_ids = jnp.arange(mats_all, dtype=jnp.int32)
    return jnp.sum(
        jnp.where(owner[None, :] == block_ids[:, None], block_ids[None, :], 0), axis=1
    )


def pick_slots(grads, slots):
    index = jnp.where(slots < 18, slots, jnp.clip(slots - 4, 0, 21))
    held = (slots < 18) | ((slots >= 22) & (slots < BLOCKS))
    picked = jnp.take(grads, index, axis=0)
    return jnp.where(held.reshape((-1,) + (1,) * (grads.ndim - 1)), picked, jnp.zeros((), BF16))


class Split:
    def __init__(self):
        self.rep = lax.axis_index("rep")
        shard = lax.axis_index("shard")
        self.ids = jnp.stack([shard % 2, self.rep * 2 + shard // 2 % 2, shard // 4])
        self.ids_two = self.ids * jnp.array([1, 1, 0])

    def gather(self, images, master, vec_master, owner, early):
        mat_dev = master.shape[0]
        rows = master.astype(BF16).reshape(mat_dev, 2, 2, 2, 4, PIECE, C)
        rows = lax.dynamic_index_in_dim(rows, self.rep, 2, keepdims=False)
        rows = rows.transpose(3, 2, 1, 0, 4, 5).reshape(16, mat_dev, PIECE, C)
        slots = lax.all_to_all(rows, "shard", 0, 0).reshape(16 * mat_dev, PIECE, C)
        blocks = jnp.take(slots, owner[:BLOCKS], axis=0)
        early, blocks = lax.optimization_barrier((early, blocks))
        act = early[0]
        width = vec_master.shape[1]
        vec = jnp.pad(vec_master.astype(BF16), ((0, 16 - VECS), (0, C - width)))
        place = lax.axis_index("shard") * width
        vec = jnp.where(self.rep == 0, jnp.roll(vec, place, axis=1), jnp.zeros((), BF16))
        rows = act.reshape(-1, C)
        rows = jnp.pad(rows, ((0, PIECE - rows.shape[0]), (0, 0)))
        attn = jnp.concatenate([blocks[22:26], rows[None]], axis=0)
        line_one = gather_line(jnp.concatenate([blocks[:9], vec[None]], axis=0))
        second, line_one = lax.optimization_barrier((blocks[9:22], line_one))
        first_one = gather_first(line_one)
        groups = [[line * 4 + place for line in range(4)] for place in range(4)]
        line_two = lax.all_to_all(
            jnp.broadcast_to(second[None], (4,) + second.shape), "shard", 0, 0, axis_index_groups=groups
        )
        core_one = [swap(part, 1) for part in first_one]
        planes_one = gather_second(first_one)
        line_two, attn, planes_one, core_one = lax.optimization_barrier(
            (line_two, attn, planes_one, core_one)
        )
        first_two = gather_first(line_two)
        one = gather_core(planes_one, core_one)
        images, first_two = lax.optimization_barrier((images, first_two))
        core_two = [swap(part, 1) for part in first_two]
        attn = lax.all_gather(attn, AXES)
        acts = attn[:, 4, : act.size // C].reshape(-1, 2, C).transpose(1, 0, 2)
        return (*early, images, one, (gather_second(first_two), core_two), attn), acts

    def gather_core(self, planes):
        return gather_core(*planes)

    def reduce_early(self, grads):
        return lax.psum_scatter(grads, "shard", scatter_dimension=0, tiled=True)[0]

    def finish_early(self, late, *early):
        own = jnp.concatenate(early, axis=0)
        mine = lax.dynamic_index_in_dim(own, self.rep, 1, keepdims=False)
        other = lax.dynamic_index_in_dim(own, 1 - self.rep, 1, keepdims=False)
        return jnp.concatenate([late, add_up(mine, swap(other, 16))], axis=0)

    def reduce_core(self, keep, send):
        other = swap(send, 1)
        return [add_up(keep[k], other[k]) for k in range(4)]

    def reduce_late(self, planes, after):
        line = [swap(planes[k], plane_mask(k)) for k in (1, 2, 3)]
        lines = [add_up(planes[0][j], *[part[j] for part in line]) for j in range(4)]
        lines, _ = lax.optimization_barrier((lines, after))
        return add_up(lines[0], *[swap(lines[k], 4 * k) for k in (1, 2, 3)])

    def own(self, grads, slots, mat_dev, map_terms, grad_vectors):
        picked = pick_slots(grads, slots).reshape(16, mat_dev * PIECE, C)
        terms = jnp.broadcast_to(map_terms.reshape(1, -1, C), (16, map_terms.size // C, C))
        width = C // 16
        vec = grad_vectors.astype(BF16).reshape(VECS, 16, width).transpose(1, 0, 2)
        vec = jnp.pad(vec.reshape(16, 1, VECS * width), ((0, 0), (0, 0), (0, C - VECS * width)))
        sent = jnp.concatenate([picked, terms, vec], axis=1)
        got = lax.all_to_all(jnp.concatenate([sent, sent]), AXES, 0, 0)
        split = mat_dev * PIECE
        terms = got[:, split:-1].reshape(-1, 2, C).transpose(1, 0, 2)
        vec = jnp.sum(got[:, -1, : VECS * width].astype(F32), axis=0)
        return got, terms, vec.reshape(VECS, width)


class Plain:
    def __init__(self):
        self.ids = self.ids_two = jnp.zeros((3,), jnp.int32)

    def gather(self, images, master, vec_master, owner, early):
        act = early[0]
        slots = lax.all_gather(master.astype(BF16), "shard", axis=0, tiled=True)
        vec = lax.all_gather(vec_master.astype(BF16), "shard", axis=1, tiled=True)
        blocks = jnp.take(slots, owner[:BLOCKS], axis=0)

        def parts(some):
            split = (some.shape[0] + 1) // 2
            pieces = some.reshape(-1, 2, 4, 4, PIECE, C).transpose(1, 2, 3, 0, 4, 5)
            halves = (slice(0, split), slice(split, None))
            return [
                jnp.stack([pieces[core, plane][:, halves[n // 2]] for plane in planes])
                for core in range(2)
                for n, (planes, _) in enumerate(HALVED)
            ]

        rows = jnp.zeros((C, C), BF16).at[:VECS].set(vec)
        one = parts(jnp.concatenate([blocks[:9], rows[None]], axis=0))
        flat = blocks[22:26].reshape(4, 2, 2, 2, 4, PIECE, C).transpose(2, 4, 3, 1, 0, 5, 6)
        acts = lax.all_gather(act, AXES, axis=0, tiled=True).reshape(-1, 2, C).transpose(1, 0, 2)
        two, attn = parts(blocks[9:22]), flat.reshape(PIECES, 4, PIECE, C)
        return (*early, images, one, two, attn), acts

    def gather_core(self, planes):
        return planes

    def reduce_early(self, grads):
        split = grads.reshape(4, 2, 2, -1, 2, PIECE, C).transpose(3, 2, 4, 1, 0, 5, 6)
        return split.reshape(-1, C, C)

    def finish_early(self, late, *early):
        return jnp.concatenate([late, *early], axis=0)

    def reduce_core(self, keep, send):
        return [jnp.stack([keep, send]).transpose(3, 0, 1, 2, 4, 5).reshape(-1, C, C)]

    def reduce_late(self, planes, after):
        return planes[0]

    def own(self, grads, slots, mat_dev, map_terms, grad_vectors):
        picked = pick_slots(grads, slots)
        mine = lax.psum_scatter(picked, "shard", scatter_dimension=0, tiled=True)
        rows = lax.psum(mine, "rep").reshape(mat_dev, 2, 2, 2, 4, PIECE, C)
        got = rows.transpose(2, 4, 3, 1, 0, 5, 6).reshape(PIECES, mat_dev * PIECE, C)
        terms = lax.all_gather(map_terms, AXES, axis=0, tiled=True)
        terms = terms.transpose(1, 0, 2)
        vec = lax.psum_scatter(grad_vectors, "shard", scatter_dimension=1, tiled=True)
        return got, terms, lax.psum(vec, "rep")


def shards(
    images,
    embeds,
    cotangent,
    counts,
    bucket_weight,
    owner,
    master,
    first_moment,
    second_moment,
    left_basis,
    right_basis,
    vec_master,
    vec_first,
    vec_second,
):
    mat_dev = master.shape[0]
    mats_all = mat_dev * lax.axis_size("shard")
    sizes = (lax.axis_size("rep"), lax.axis_size("shard"))
    plan = Split() if sizes == (2, 16) else Plain()
    emb = embeds.astype(F32)
    act = jax.nn.silu(emb).astype(BF16)
    act_rows = jnp.broadcast_to(act[:, None, :], act.shape[:1] + (16, EMB))
    emb_rows = jnp.broadcast_to(emb[:, None, :], emb.shape[:1] + (8, EMB))
    (act, act_rows, emb_rows, *gathered), acts = plan.gather(
        images, master, vec_master, owner, (act, act_rows, emb_rows)
    )
    outputs, grad_images, grad_embeds, grads, map_terms, grad_vectors = layer(
        images, emb_rows, act_rows, cotangent, counts, bucket_weight, plan, gathered
    )
    all_slots = block_slots(owner, mats_all)
    shard = lax.axis_index("shard")
    slot_block = lax.dynamic_slice_in_dim(all_slots, shard * mat_dev, mat_dev, 0)
    got, terms, own_vec = plan.own(grads, all_slots, mat_dev, map_terms, grad_vectors)
    step_rate = jnp.where(slot_block < BLOCKS, 2.0 * block_spread(slot_block), 0.0)
    new_first, new_second, new_master, master_low = optimize(
        slot_block,
        step_rate,
        got,
        jnp.concatenate([acts, terms], axis=0),
        (left_basis, right_basis, first_moment, second_moment, master),
    )
    correction = 1.0 - MOMENT_DECAY**STEP
    vec_first_new = MOMENT_DECAY * vec_first + (1.0 - MOMENT_DECAY) * own_vec
    vec_second_new = MOMENT_DECAY * vec_second + (1.0 - MOMENT_DECAY) * own_vec * own_vec
    vec_master_new = vec_master - VECTOR_RATE * (vec_first_new / correction) / (
        jnp.sqrt(vec_second_new / correction) + ADAM_EPS
    )
    return (
        outputs,
        grad_images,
        grad_embeds,
        new_first,
        new_second,
        new_master,
        master_low,
        vec_first_new,
        vec_second_new,
        vec_master_new,
        vec_master_new.astype(jnp.bfloat16),
    )


def solution(mesh):
    return jax.shard_map(
        shards,
        mesh=mesh,
        in_specs=(
            P(("rep", "shard"), None, None),
            P(("rep", "shard"), None),
            P(("rep", "shard"), None, None),
            P(("rep", "shard"), None),
            P(),
            P(),
            P("shard", None, None),
            P("shard", None, None),
            P("shard", None, None),
            P("shard", None, None),
            P("shard", None, None),
            P(None, "shard"),
            P(None, "shard"),
            P(None, "shard"),
        ),
        out_specs=(
            P(("rep", "shard"), None, None),
            P(("rep", "shard"), None, None),
            P(("rep", "shard"), None),
            P("shard", None, None),
            P("shard", None, None),
            P("shard", None, None),
            P("shard", None, None),
            P(None, "shard"),
            P(None, "shard"),
            P(None, "shard"),
            P(None, "shard"),
        ),
        check_vma=False,
    )
```
